32 devices in a mesh: groups: 2 (over x), seq: 16 (over z, y, core).
Axes of the slice: x: 2, y: 2, z: 4, core: 2. Of those that a mesh axis runs over, the one named last changes fastest.
Arguments:
- query_rows: bfloat16 [4096, 2048], P(('groups', 'seq')), parts along dimension 0, may hold values from -150 to 150
- key_rows: bfloat16 [4096, 256], P(('groups', 'seq')), parts along dimension 0, may hold values from -4.1 to 4.1
- value_rows: bfloat16 [4096, 256], P(('groups', 'seq')), parts along dimension 0, may hold values from -6 to 6
- sink_positions: int32 [32], P('groups'), parts along dimension 0, may hold values from 0 to 2047
- residual: bfloat16 [4096, 2880], P(('groups', 'seq')), parts along dimension 0, may hold values from -6 to 6
- out_proj: bfloat16 [2048, 2880], replicated, may hold values from -0.125 to 0.125
- norm_gain: float32 [2880], replicated, may hold values from 0.5 to 1.5
- expert_ids: int32 [4096, 4], P(('groups', 'seq')), parts along dimension 0, may hold values from 0 to 7, all different within a row; in each aligned block of 128 rows (0 to 127, 128 to 255, ...) at most 128 rows name the same one
- route_weights: float32 [4096, 4], P(('groups', 'seq')), parts along dimension 0, may hold values from 0.05 to 1
- gate_up: bfloat16 [16, 2880, 1440], P('seq'), may hold values from -0.109375 to 0.109375
- down_proj: bfloat16 [16, 720, 2880], P('seq'), may hold values from -0.15625 to 0.15625
Outputs:
- layer_out: bfloat16 [4096, 2880], P(('groups', 'seq')), parts along dimension 0
The draws below stay inside these ranges and needn't reach their ends.
There are 2 independent parts, one for each index of `groups`. The reference program is written for one: setup_inputs(seed, part) draws one part's arguments, and reference() takes and returns one part's arrays. A program takes and returns all parts, laid end to end along the dimension named above; an argument that names none is the same for every part. Nothing has to cross between parts.
Inputs may be any that keep to these rules, and one draw needn't show every extreme that they name: `expert_ids`: each row names 4 different experts; in the rows of one index of seq no expert is named by more than 128 rows, a bound that some block reaches. `sink_positions`: positions may repeat.
All inputs are finite; a program needn't handle non-finite values.
Results may differ from the reference program's by a relative error of at most 0.013.
Values may be sent and summed in bfloat16 or wider, within the bound.
No kernel may reach another device: no remote copies, remote signals or barrier semaphores. Data moves between devices by JAX's collectives and lax.ppermute only.
A program may use at most 192 MiB of HBM per device.

```python
import math
import jax
import jax.numpy as jnp
import numpy as np
from jax import lax

D = 2880
Q_HEADS = 32
KV_HEADS = 4
HEAD_DIM = 64
FF = 1440
WINDOW = 128
NSINK = 16
TOPK = 4
TOK_DEV = 128
TOKENS = 2048
EXPERTS = 8
CAP = 128
N_SEQ = 16


def shared_keys(key):
    normal_rows = jax.random.normal(key, (TOKENS, KV_HEADS * HEAD_DIM), jnp.float32)
    return jnp.clip(normal_rows, -4.0, 4.0)


def draw_key_rows(key, part):
    base_rows = shared_keys(key)
    return base_rows.astype(jnp.bfloat16)


def draw_query_rows(key, part):
    key = jax.random.fold_in(key, 23)
    query_draw = jnp.clip(jax.random.normal(key, (TOKENS, Q_HEADS * HEAD_DIM), jnp.float32), -4.0, 4.0)
    return query_draw.astype(jnp.bfloat16)


def with_ends(drawn, rng, least, high):
    place = [jax.random.randint(jax.random.fold_in(rng, axis), (), 0, length) for axis, length in enumerate(drawn.shape)]
    longest = drawn.shape.index(max(drawn.shape))
    neighbour = place[:longest] + [(place[longest] + 1) % drawn.shape[longest]] + place[longest + 1:]
    return drawn.at[tuple(place)].set(least).at[tuple(neighbour)].set(high)


def block_levels(key, shape, pieces, least, high):
    gain, own = 1.0, jax.random.fold_in(key, 6)
    for dim, blocks in pieces:
        steps = jnp.exp(jax.random.uniform(jax.random.fold_in(own, dim), (blocks,), jnp.float32, least / len(pieces), high / len(pieces)))
        gain = gain * jnp.repeat(steps, shape[dim] // blocks).reshape([-1 if axis == dim else 1 for axis in range(len(shape))])
    return gain


def deal_out(rng, own, number, rows, count, top, bound, slope):
    sequence = jax.random.permutation(rng, count)
    heavy_load, common = load_shares(count, rows * top, bound, slope, True), load_shares(count, rows * top, bound, slope, False)
    places = jnp.arange(count)

    def named(lengths, turn):
        used = int((lengths > 0).sum())
        fixed = max(1, used // 4)
        shifted = fixed + (places - fixed + turn * (used - fixed)) % max(1, count - fixed)
        return jnp.zeros((count,), jnp.int32).at[sequence[jnp.where(places < fixed, places, shifted)]].set(jnp.asarray(lengths, jnp.int32))

    lengths = jnp.where(number % 4 == 0, named(heavy_load, number // 4), named(common, number - number // 4 - 1))
    mixed = jax.random.permutation(jax.random.fold_in(own, 3), count)
    giver, receiver = mixed[0:count // 2 * 2:2], mixed[1:count // 2 * 2:2]
    room = jnp.minimum(lengths[giver] - 1, bound - lengths[receiver]) // 2
    room = jnp.where((giver == sequence[0]) | (receiver == sequence[0]) | (lengths[receiver] == 0), 0, jnp.maximum(room, 0))
    shifted = jax.random.randint(jax.random.fold_in(own, 4), (count // 2,), 0, 1 << 20) % (room + 1)
    lengths = lengths.at[giver].add(-shifted).at[receiver].add(shifted)
    items = jnp.searchsorted(jnp.cumsum(lengths), jnp.arange(rows * top), side="right").astype(jnp.int32)
    listing = items.reshape(top, rows).T
    listing = listing[jax.random.permutation(jax.random.fold_in(own, 1), rows)]
    turn = jax.random.randint(jax.random.fold_in(own, 2), (rows, 1), 0, top)
    return jnp.take_along_axis(listing, (jnp.arange(top)[None, :] + turn) % top, axis=1)


def load_shares(number_of, total, reach, slope, full):
    weights = [(1 << 20) // math.isqrt(standing ** slope) + 1 for standing in range(1, number_of + 1)]
    largest = reach if full else min(reach, max(-(-total // number_of), total * weights[0] // sum(weights)))
    least = 1 if total - largest >= number_of - 1 else 0
    counts, spare = [largest] + [least] * (number_of - 1), total - largest - least * (number_of - 1)
    while spare > 0:
        free = [i for i in range(1, number_of) if counts[i] < largest] or [i for i in range(1, number_of) if counts[i] < reach]
        pool, left = sum([weights[i] for i in free]), spare
        for i in free:
            extra = min(reach - counts[i], max(1, left * weights[i] // pool), spare)
            counts[i] = counts[i] + extra
            spare = spare - extra
    return np.array(counts)


def bell_draw(own_key, extent, spread, limit, split=(), kind=jnp.bfloat16):
    entries = jax.random.normal(own_key, extent, jnp.float32) * spread
    if len(split) > 0:
        entries = block_levels(own_key, extent, split, -0.22, 0.18) * entries
    return jnp.clip(entries, min=-limit, max=limit).astype(kind)


def setup_inputs(seed: int = 0, part: int = 0) -> dict:
    key_list = jax.random.split(jax.random.key(seed), 12)
    part_keys = jax.random.split(jax.random.fold_in(key_list[11], part), 12)
    query_rows = draw_query_rows(jax.random.fold_in(jax.random.fold_in(key_list[11], part), 71), part)
    key_rows = draw_key_rows(jax.random.fold_in(jax.random.fold_in(key_list[11], part), 71), part)
    value_rows = bell_draw(part_keys[2], (TOKENS, KV_HEADS * HEAD_DIM), 1.0, 6.0, ((0, 16),))
    sink_positions = with_ends(jax.random.randint(part_keys[3], (NSINK,), 0, TOKENS), jax.random.fold_in(part_keys[3], 1), 0, TOKENS - 1).astype(jnp.int32)
    residual = bell_draw(part_keys[4], (TOKENS, D), 1.0, 6.0, ((0, 16),))
    out_proj = bell_draw(key_list[5], (Q_HEADS * HEAD_DIM, D), (Q_HEADS * HEAD_DIM) ** -0.5, 0.125)
    norm_gain = jnp.clip(1.0 + 0.1 * jax.random.normal(key_list[6], (D,), jnp.float32), 0.5, 1.5)
    expert_ids_keys = jax.random.split(jax.random.fold_in(part_keys[7], 1), TOKENS // TOK_DEV)
    expert_ids_turns = jax.random.permutation(jax.random.fold_in(part_keys[7], 3), TOKENS // TOK_DEV)
    expert_ids = jax.vmap(lambda own, number: deal_out(jax.random.fold_in(part_keys[7], 2), own, number, TOK_DEV, EXPERTS, TOPK, CAP, 1))(expert_ids_keys, expert_ids_turns).reshape((TOKENS, TOPK))
    route_weights = jnp.clip(jnp.exp(math.log(1.0) - 2.9957323 * jax.random.uniform(part_keys[8], (TOKENS, TOPK), jnp.float32) ** block_levels(part_keys[8], (TOKENS, TOPK), ((0, 16),), -0.2, 0.2)), 0.05, 1.0)
    gate_up = bell_draw(key_list[9], (2 * EXPERTS, D, FF), D ** -0.5, 0.109375, ((0, 16),))
    down_proj = bell_draw(key_list[10], (2 * EXPERTS, FF // 2, D), FF ** -0.5, 0.15625, ((0, 16),))
    return {"query_rows": query_rows, "key_rows": key_rows, "value_rows": value_rows, "sink_positions": sink_positions, "residual": residual, "out_proj": out_proj, "norm_gain": norm_gain, "expert_ids": expert_ids, "route_weights": route_weights, "gate_up": gate_up, "down_proj": down_proj}


def attend(query_block, key_block, value_block, allowed):
    rows_q = query_block.shape[0]
    rows_k = key_block.shape[0]
    query_wide = query_block.astype(jnp.float32).reshape(rows_q, KV_HEADS, Q_HEADS // KV_HEADS, HEAD_DIM)
    key_wide = key_block.astype(jnp.float32).reshape(rows_k, KV_HEADS, HEAD_DIM)
    value_wide = value_block.astype(jnp.float32).reshape(rows_k, KV_HEADS, HEAD_DIM)
    scores = jnp.einsum('tkgd,skd->kgts', query_wide, key_wide) * HEAD_DIM ** (-0.5)
    scores = jnp.where(allowed[None, None], scores, -jnp.inf)
    largest = lax.optimization_barrier(jnp.max(scores, axis=-1, keepdims=True))
    exponent_terms = jnp.exp(scores - largest)
    attention_probs = (exponent_terms / lax.optimization_barrier(jnp.sum(exponent_terms, axis=-1, keepdims=True))).astype(jnp.bfloat16)
    attended = jnp.einsum('kgts,skd->tkgd', attention_probs.astype(jnp.float32), value_wide)
    return attended.reshape(rows_q, Q_HEADS * HEAD_DIM).astype(jnp.bfloat16)

def window_allowed(query_pos, key_pos):
    return (key_pos[None, :] >= 0) & (key_pos[None, :] <= query_pos[:, None]) & (key_pos[None, :] > query_pos[:, None] - WINDOW)

def sink_allowed(sink_positions, query_pos):
    order = jnp.arange(sink_positions.shape[0], dtype=jnp.int32)
    repeated = jnp.any((sink_positions[:, None] == sink_positions[None, :]) & (order[:, None] > order[None, :]), axis=1)
    return (~repeated)[None, :] & (sink_positions[None, :] <= query_pos[:, None] - WINDOW)

def rms_norm(hidden_state, norm_gain):
    widened = hidden_state.astype(jnp.float32)
    meansq = lax.optimization_barrier(jnp.mean(widened * widened, axis=-1, keepdims=True))
    return (widened * lax.rsqrt(meansq + 1e-05) * norm_gain).astype(jnp.bfloat16)

def reference(query_rows, key_rows, value_rows, sink_positions, residual, out_proj, norm_gain, expert_ids, route_weights, gate_up, down_proj):
    block_rows = min(512, TOKENS)
    kv_width = KV_HEADS * HEAD_DIM
    keys_padded = jnp.concatenate([jnp.zeros((WINDOW, kv_width), jnp.bfloat16), key_rows], 0)
    values_padded = jnp.concatenate([jnp.zeros((WINDOW, kv_width), jnp.bfloat16), value_rows], 0)
    sink_keys = key_rows[sink_positions]
    sink_values = value_rows[sink_positions]

    def one_block(block):
        start_pos = (block * block_rows).astype(jnp.int32)
        query_block = lax.dynamic_slice_in_dim(query_rows, start_pos, block_rows, 0)
        key_block = jnp.concatenate([lax.dynamic_slice_in_dim(keys_padded, start_pos, block_rows + WINDOW, 0), sink_keys], 0)
        value_block = jnp.concatenate([lax.dynamic_slice_in_dim(values_padded, start_pos, block_rows + WINDOW, 0), sink_values], 0)
        query_pos = start_pos + jnp.arange(block_rows, dtype=jnp.int32)
        key_pos = start_pos - WINDOW + jnp.arange(block_rows + WINDOW, dtype=jnp.int32)
        allowed = jnp.concatenate([window_allowed(query_pos, key_pos), sink_allowed(sink_positions, query_pos)], 1)
        return attend(query_block, key_block, value_block, allowed)
    attended = lax.map(one_block, jnp.arange(TOKENS // block_rows, dtype=jnp.int32)).reshape(TOKENS, Q_HEADS * HEAD_DIM)
    hidden_state = (residual.astype(jnp.float32) + jnp.dot(attended, out_proj, preferred_element_type=jnp.float32)).astype(jnp.bfloat16)
    normed = rms_norm(hidden_state, norm_gain)
    half_width = FF // 2
    flat_ids = expert_ids.reshape(-1)
    flat_weights = route_weights.reshape(-1)
    slots_all = N_SEQ * CAP

    def one_expert(expert, totals):
        chosen = flat_ids == expert
        picked = jnp.nonzero(chosen, size=slots_all, fill_value=0)[0].astype(jnp.int32)
        filled = jnp.arange(slots_all, dtype=jnp.int32) < jnp.sum(chosen.astype(jnp.int32))
        token_index = picked // TOPK
        inputs = normed[token_index]
        first_half = gate_up[2 * expert]
        second_half = gate_up[2 * expert + 1]
        gate_cols = jnp.concatenate([first_half[:, :half_width], second_half[:, :half_width]], 1)
        up_cols = jnp.concatenate([first_half[:, half_width:], second_half[:, half_width:]], 1)
        gate_val = jnp.dot(inputs, gate_cols, preferred_element_type=jnp.float32)
        up_val = jnp.dot(inputs, up_cols, preferred_element_type=jnp.float32)
        hidden_units = (jax.nn.silu(gate_val) * up_val).astype(jnp.bfloat16)
        down_rows = jnp.concatenate([down_proj[2 * expert], down_proj[2 * expert + 1]], 0)
        expert_out = jnp.dot(hidden_units, down_rows, preferred_element_type=jnp.float32).astype(jnp.bfloat16)
        scaled = jnp.where(filled, flat_weights[picked], jnp.zeros((), jnp.float32))[:, None] * expert_out.astype(jnp.float32)
        return totals.at[token_index].add(scaled)
    totals = lax.fori_loop(0, EXPERTS, one_expert, jnp.zeros((TOKENS, D), jnp.float32))
    return (hidden_state.astype(jnp.float32) + totals).astype(jnp.bfloat16)
```

```python
import functools

import jax
import jax.numpy as jnp
from jax import lax
from jax.experimental import pallas as pl
from jax.experimental.pallas import tpu as pltpu
from jax.sharding import PartitionSpec as P

Q_HEADS = 32
KV_HEADS = 4
HEAD_DIM = 64
WINDOW = 128
TOPK = 4


def passed_along(block, axis, distance):
    devices = range(lax.axis_size(axis))
    route = [(i - distance, i) for i in devices if i - distance in devices]
    return lax.ppermute(block, axis, route)


def attend(query_block, key_block, value_block, allowed):
    rows_q = query_block.shape[0]
    rows_k = key_block.shape[0]
    query_wide = query_block.reshape(rows_q, KV_HEADS, Q_HEADS // KV_HEADS, HEAD_DIM)
    key_wide = key_block.reshape(rows_k, KV_HEADS, HEAD_DIM)
    value_wide = value_block.reshape(rows_k, KV_HEADS, HEAD_DIM)
    scores = jnp.einsum(
        "tkgd,skd->kgts", query_wide, key_wide, preferred_element_type=jnp.float32
    ) * HEAD_DIM ** (-0.5)
    scores = jnp.where(allowed[None, None], scores, -jnp.inf)
    largest = jnp.max(scores, axis=-1, keepdims=True)
    exponent_terms = jnp.exp(scores - largest)
    attention_probs = (exponent_terms / jnp.sum(exponent_terms, axis=-1, keepdims=True)).astype(
        jnp.bfloat16
    )
    attended = jnp.einsum(
        "kgts,skd->tkgd", attention_probs, value_wide, preferred_element_type=jnp.float32
    )
    return attended.reshape(rows_q, Q_HEADS * HEAD_DIM).astype(jnp.bfloat16)


def window_allowed(query_pos, key_pos):
    return (
        (key_pos[None, :] >= 0)
        & (key_pos[None, :] <= query_pos[:, None])
        & (key_pos[None, :] > query_pos[:, None] - WINDOW)
    )


def sink_allowed(sink_positions, query_pos):
    order = jnp.arange(sink_positions.shape[0], dtype=jnp.int32)
    repeated = jnp.any(
        (sink_positions[:, None] == sink_positions[None, :]) & (order[:, None] > order[None, :]),
        axis=1,
    )
    return (~repeated)[None, :] & (sink_positions[None, :] <= query_pos[:, None] - WINDOW)


def rms_norm(hidden_state, norm_gain):
    widened = hidden_state.astype(jnp.float32)
    meansq = jnp.mean(widened * widened, axis=-1, keepdims=True)
    return (widened * lax.rsqrt(meansq + 1e-05) * norm_gain).astype(jnp.bfloat16)


PLANE = 4


def step_pairs(shards, distance, toward):
    planes = shards // PLANE
    return [
        (PLANE * p + r, PLANE * (p + s * distance) + r)
        for s in toward
        for p in range(planes)
        if 0 <= p + s * distance < planes
        for r in range(PLANE)
    ]


def line_steps(shards):
    planes = shards // PLANE
    steps = []
    for distance in range(1, planes):
        if 2 * distance >= planes:
            steps.append(step_pairs(shards, distance, (1, -1)))
        else:
            steps.append(step_pairs(shards, distance, (1,)))
            steps.append(step_pairs(shards, distance, (-1,)))
    return steps


def column_pairs(receivers):
    return [(i, i ^ 2) for i in sorted(receivers)]


def expert_kernel(
    width, experts, chunks, me_ref, x_ref, y_ref, gu0, gu1, dn0, dn1, ox_ref, oy_ref, rows, gu_v, dn_v, sems
):
    depth = width // chunks
    copies = []
    for half, gate_up in enumerate((gu0, gu1)):
        for k in range(chunks):
            part = pl.ds(k * depth, depth)
            copies.append(
                pltpu.make_async_copy(
                    gate_up.at[part], gu_v.at[half, part], sems.at[half * (chunks + 1) + k]
                )
            )
        down = dn0 if half == 0 else dn1
        copies.append(
            pltpu.make_async_copy(down, dn_v.at[half], sems.at[half * (chunks + 1) + chunks])
        )
    for copy in copies:
        copy.start()
    count = x_ref.shape[0]
    rows[:count, :] = x_ref[:, :]
    rows[count:, :] = y_ref[:, :]
    hidden = gu_v.shape[2] // 2
    total = None
    for half in range(2):
        projected = None
        for k in range(chunks):
            copies[half * (chunks + 1) + k].wait()
            term = jnp.dot(
                rows[:, k * depth : (k + 1) * depth],
                gu_v[half, k * depth : (k + 1) * depth, :],
                preferred_element_type=jnp.float32,
            )
            projected = term if projected is None else projected + term
        gate = projected[:, :hidden]
        up = projected[:, hidden:]
        units = (gate / (1.0 + jnp.exp(-gate)) * up).astype(jnp.bfloat16)
        copies[half * (chunks + 1) + chunks].wait()
        term = jnp.dot(units, dn_v[half], preferred_element_type=jnp.float32)
        total = term if total is None else total + term
    base = width // 128 * 128
    extra = rows[:, base:].astype(jnp.float32)
    place = lax.broadcasted_iota(jnp.int32, extra.shape, 1) - (width - base)
    mine = (place == me_ref[0]) | (place == experts + me_ref[0])
    weight = jnp.sum(jnp.where(mine, extra, 0.0), axis=1, keepdims=True)
    total = total * weight
    ox_ref[:, :] = total[:count]
    oy_ref[:, :] = total[count:].astype(jnp.bfloat16)


def expert_rows(me, x, y, gu0, gu1, dn0, dn1, width, experts):
    chunks = 3
    count = x.shape[0]
    vmem = pl.BlockSpec(memory_space=pltpu.VMEM)
    hbm = pl.BlockSpec(memory_space=pl.ANY)
    return pl.pallas_call(
        functools.partial(expert_kernel, width, experts, chunks),
        out_shape=(
            jax.ShapeDtypeStruct((count, width), jnp.float32),
            jax.ShapeDtypeStruct((count, width), jnp.bfloat16),
        ),
        in_specs=[pl.BlockSpec(memory_space=pltpu.SMEM), vmem, vmem, hbm, hbm, hbm, hbm],
        out_specs=(vmem, vmem),
        scratch_shapes=[
            pltpu.VMEM((2 * count, x.shape[1]), jnp.bfloat16),
            pltpu.VMEM((2,) + gu0.shape, jnp.bfloat16),
            pltpu.VMEM((2,) + dn0.shape, jnp.bfloat16),
            pltpu.SemaphoreType.DMA((2 * chunks + 2,)),
        ],
        compiler_params=pltpu.CompilerParams(vmem_limit_bytes=56 * 1024 * 1024),
        cost_estimate=pl.CostEstimate(
            flops=2 * 2 * count * 3 * width * gu0.shape[1],
            bytes_accessed=2 * 2 * (gu0.size + dn0.size),
            transcendentals=2 * count * gu0.shape[1],
        ),
    )(me, x, y, gu0, gu1, dn0, dn1)


def summed(block, axis):
    shards = lax.axis_size(axis)
    step = 1
    while step < shards:
        block = block + lax.ppermute(block, axis, [(i, i ^ step) for i in range(shards)])
        step *= 2
    return block


def on_device(
    query_rows,
    key_rows,
    value_rows,
    sink_positions,
    residual,
    out_proj,
    norm_gain,
    expert_ids,
    route_weights,
    gate_up,
    down_proj,
):
    rows_dev = query_rows.shape[0]
    width = residual.shape[1]
    shards = lax.axis_size("seq")
    my_index = lax.axis_index("seq")
    first_pos = my_index * rows_dev
    to_core = [(i, i ^ 1) for i in range(shards)]
    gu_own, dn_own = gate_up[0], down_proj[0]
    gu_other = lax.ppermute(gu_own, "seq", to_core)
    dn_other = lax.ppermute(dn_own, "seq", to_core)
    halo_keys, halo_values = passed_along((key_rows, value_rows), "seq", 1)
    own_pos = first_pos + jnp.arange(rows_dev, dtype=jnp.int32)
    pick_rows = (sink_positions[:, None] == own_pos[None, :]).astype(jnp.bfloat16)
    local_rows = jnp.concatenate([key_rows, value_rows], 1)
    sink_rows = jnp.dot(pick_rows, local_rows, preferred_element_type=jnp.float32)
    sink_rows = summed(sink_rows.astype(jnp.bfloat16), "seq")
    sink_keys = sink_rows[:, : key_rows.shape[1]]
    sink_values = sink_rows[:, key_rows.shape[1] :]
    keys_joined = jnp.concatenate([halo_keys, key_rows], 0)
    values_joined = jnp.concatenate([halo_values, value_rows], 0)
    block_rows = min(512, rows_dev)
    query_pos = first_pos + 0 + jnp.arange(block_rows, dtype=jnp.int32)
    key_pos = first_pos + 0 - WINDOW + jnp.arange(block_rows + WINDOW, dtype=jnp.int32)
    key_block = jnp.concatenate([keys_joined, sink_keys], 0)
    value_block = jnp.concatenate([values_joined, sink_values], 0)
    allowed = jnp.concatenate(
        [window_allowed(query_pos, key_pos), sink_allowed(sink_positions, query_pos)], 1
    )
    pieces = attend(query_rows, key_block, value_block, allowed)
    hidden_state = (
        residual.astype(jnp.float32) + jnp.dot(pieces, out_proj, preferred_element_type=jnp.float32)
    ).astype(jnp.bfloat16)
    normed = rms_norm(hidden_state, norm_gain)
    experts = shards // 2
    chosen = expert_ids[:, :, None] == jnp.arange(experts, dtype=jnp.int32)
    weight = jnp.sum(jnp.where(chosen, route_weights[:, :, None], 0.0), axis=1)
    high = weight.astype(jnp.bfloat16)
    low = (weight - high.astype(jnp.float32)).astype(jnp.bfloat16)
    spare = -width % 128
    spare += 0 if spare >= 2 * experts else 128
    blank = jnp.zeros((rows_dev, spare - 2 * experts), jnp.bfloat16)
    own_rows = jnp.concatenate([normed, high, low, blank], 1)
    me = (my_index // 2).reshape(1)
    steps = [None] + line_steps(shards)
    everyone = set(range(shards))
    column_rows = [own_rows if s is None else lax.ppermute(own_rows, "seq", s) for s in steps]
    receivers = [everyone if s is None else {d for _, d in s} for s in steps]
    cross_rows = [
        lax.ppermute(block, "seq", column_pairs(r)) for block, r in zip(column_rows, receivers)
    ]
    combined = hidden_state.astype(jnp.float32)
    for s, x, y, r in zip(steps, column_rows, cross_rows, receivers):
        mine, theirs = expert_rows(me, x, y, gu_own, gu_other, dn_own, dn_other, width, experts)
        returned = lax.ppermute(theirs, "seq", column_pairs(r))
        both = mine + returned.astype(jnp.float32)
        if s is None:
            combined = combined + both
        else:
            back = lax.ppermute(both.astype(jnp.bfloat16), "seq", [(d, o) for o, d in s])
            combined = combined + back.astype(jnp.float32)
    return combined.astype(jnp.bfloat16)


def solution(mesh):
    in_specs = (
        P(("groups", "seq"), None),
        P(("groups", "seq"), None),
        P(("groups", "seq"), None),
        P("groups"),
        P(("groups", "seq"), None),
        P(),
        P(),
        P(("groups", "seq"), None),
        P(("groups", "seq"), None),
        P("seq", None, None),
        P("seq", None, None),
    )
    out_specs = P(("groups", "seq"), None)
    return jax.shard_map(
        on_device, mesh=mesh, in_specs=in_specs, out_specs=out_specs, check_vma=False
    )
```

```python
import functools

import jax
import jax.numpy as jnp
from jax import lax
from jax.experimental import pallas as pl
from jax.experimental.pallas import tpu as pltpu
from jax.sharding import PartitionSpec as P

Q_HEADS = 32
KV_HEADS = 4
HEAD_DIM = 64
WINDOW = 128
TOPK = 4
PLANE = 4
NEVER = -1e30
VMEM_BYTES = 56 * 1024 * 1024


def window_allowed(query_pos, key_pos):
    return (
        (key_pos[:, None] >= 0)
        & (key_pos[:, None] <= query_pos[None, :])
        & (key_pos[:, None] > query_pos[None, :] - WINDOW)
    )


def sink_allowed(sink_positions, query_pos):
    order = jnp.arange(sink_positions.shape[0], dtype=jnp.int32)
    repeated = jnp.any(
        (sink_positions[:, None] == sink_positions[None, :]) & (order[:, None] > order[None, :]),
        axis=1,
    )
    return (~repeated)[:, None] & (sink_positions[:, None] <= query_pos[None, :] - WINDOW)


def summed(block, axis):
    shards = lax.axis_size(axis)
    step = 1
    while step < shards:
        reach = min(4, shards // step)
        parts = [
            lax.ppermute(block, axis, [(i, i ^ (step * m)) for i in range(shards)])
            for m in range(1, reach)
        ]
        for part in parts:
            block = block + part
        step *= reach
    return block


def even_rows(rows, most):
    return max(r for r in range(16, most + 1, 16) if rows % r == 0)


def fetched(pieces, sems, ahead):
    copies = [pltpu.make_async_copy(src, dst, sems.at[i]) for i, (src, dst) in enumerate(pieces)]
    for copy in copies[:ahead]:
        copy.start()

    def wait(i):
        copies[i].wait()
        if i + ahead < len(copies):
            copies[i + ahead].start()

    return wait


def attention_kernel(
    experts,
    query_t,
    keys,
    values,
    sinks,
    bias,
    residual_t,
    gain,
    ids_t,
    route_t,
    out_proj_t,
    hidden_ref,
    rows_ref,
    proj_v,
    att_v,
    sems,
):
    width, heads_width = proj_v.shape
    tokens = query_t.shape[1]
    part = even_rows(width, 480)
    parts = width // part
    wait = fetched(
        [
            (out_proj_t.at[pl.ds(r * part, part)], proj_v.at[pl.ds(r * part, part)])
            for r in range(parts)
        ],
        sems,
        parts,
    )
    group = Q_HEADS // KV_HEADS
    near = keys.shape[0]
    wide_bias = jnp.concatenate([bias[:, :]] * group, 1)
    scale = HEAD_DIM ** (-0.5)
    for g in range(KV_HEADS):
        lanes = slice(g * HEAD_DIM, (g + 1) * HEAD_DIM)
        value_lanes = slice((KV_HEADS + g) * HEAD_DIM, (KV_HEADS + g + 1) * HEAD_DIM)
        first = g * group * HEAD_DIM
        query = jnp.concatenate(
            [
                query_t[first + h * HEAD_DIM : first + (h + 1) * HEAD_DIM, :]
                for h in range(group)
            ],
            1,
        )
        near_scores = (
            jnp.dot(keys[:, lanes], query, preferred_element_type=jnp.float32) * scale
            + wide_bias[:near]
        )
        sink_scores = (
            jnp.dot(sinks[:, lanes], query, preferred_element_type=jnp.float32) * scale
            + wide_bias[near:]
        )
        largest = jnp.maximum(
            jnp.max(near_scores, axis=0, keepdims=True),
            jnp.max(sink_scores, axis=0, keepdims=True),
        )
        near_terms = jnp.exp(near_scores - largest)
        sink_terms = jnp.exp(sink_scores - largest)
        total = jnp.sum(near_terms, axis=0, keepdims=True) + jnp.sum(
            sink_terms, axis=0, keepdims=True
        )
        down = (((0,), (0,)), ((), ()))
        gathered = lax.dot_general(
            values[:, lanes],
            near_terms.astype(jnp.bfloat16),
            down,
            preferred_element_type=jnp.float32,
        ) + lax.dot_general(
            sinks[:, value_lanes],
            sink_terms.astype(jnp.bfloat16),
            down,
            preferred_element_type=jnp.float32,
        )
        gathered = (gathered / total).astype(jnp.bfloat16)
        for h in range(group):
            att_v[first + h * HEAD_DIM : first + (h + 1) * HEAD_DIM, :] = gathered[
                :, h * tokens : (h + 1) * tokens
            ]
    squares = jnp.zeros((1, tokens), jnp.float32)
    for r in range(parts):
        wait(r)
        rows = slice(r * part, (r + 1) * part)
        state = (
            jnp.dot(proj_v[rows, :], att_v[:, :], preferred_element_type=jnp.float32)
            + residual_t[rows, :].astype(jnp.float32)
        ).astype(jnp.bfloat16)
        hidden_ref[rows, :] = state
        state = state.astype(jnp.float32)
        squares = squares + jnp.sum(state * state, axis=0, keepdims=True)
    inverse = lax.rsqrt(squares / width + 1e-05)
    for r in range(parts):
        rows = slice(r * part, (r + 1) * part)
        rows_ref[rows, :] = (
            hidden_ref[rows, :].astype(jnp.float32) * inverse * gain[rows, :]
        ).astype(jnp.bfloat16)
    expert = lax.broadcasted_iota(jnp.int32, (experts, tokens), 0)
    weight = jnp.zeros((experts, tokens), jnp.float32)
    for k in range(TOPK):
        weight = weight + jnp.where(ids_t[k : k + 1, :] == expert, route_t[k : k + 1, :], 0.0)
    high = weight.astype(jnp.bfloat16).astype(jnp.float32)
    rows_ref[width:, :] = jnp.concatenate([high, weight - high], 0).astype(jnp.bfloat16)


def attended_rows(
    query_t, keys, values, sinks, bias, residual_t, gain, ids_t, route_t, out_proj_t, experts
):
    width, heads_width = out_proj_t.shape
    tokens = query_t.shape[1]
    vmem = pl.BlockSpec(memory_space=pltpu.VMEM)
    return pl.pallas_call(
        functools.partial(attention_kernel, experts),
        out_shape=(
            jax.ShapeDtypeStruct((width, tokens), jnp.bfloat16),
            jax.ShapeDtypeStruct((width + 2 * experts, tokens), jnp.bfloat16),
        ),
        in_specs=[vmem] * 9 + [pl.BlockSpec(memory_space=pl.ANY)],
        out_specs=(vmem, vmem),
        scratch_shapes=[
            pltpu.VMEM((width, heads_width), jnp.bfloat16),
            pltpu.VMEM((heads_width, tokens), jnp.bfloat16),
            pltpu.SemaphoreType.DMA((width // even_rows(width, 480),)),
        ],
        compiler_params=pltpu.CompilerParams(vmem_limit_bytes=VMEM_BYTES),
        cost_estimate=pl.CostEstimate(
            flops=2 * tokens * width * heads_width,
            bytes_accessed=2 * width * heads_width,
            transcendentals=tokens * Q_HEADS * bias.shape[0],
        ),
    )(query_t, keys, values, sinks, bias, residual_t, gain, ids_t, route_t, out_proj_t)


def expert_kernel(
    experts, me_ref, x_ref, y_ref, gu0, gu1, dn0, dn1, *refs
):
    *out_refs, rows, units, gu_v, dn_v, sems = refs
    hidden = gu_v.shape[1] // 2
    width = gu_v.shape[2]
    tokens = x_ref.shape[1]
    part = even_rows(hidden, 240)
    parts = hidden // part
    depth = even_rows(width, 480)
    depths = width // depth
    pieces = []
    for half, gate_up in enumerate((gu0, gu1)):
        for k in range(parts):
            for first in (k * part, hidden + k * part):
                at = pl.ds(first, part)
                pieces.append((gate_up.at[at], gu_v.at[half, at]))
    for k in range(depths):
        at = pl.ds(k * depth, depth)
        pieces.append((dn0.at[at], dn_v.at[0, at]))
        pieces.append((dn1.at[at], dn_v.at[1, at]))
    wait = fetched(pieces, sems, 8)
    rows[:, :tokens] = x_ref[:, :]
    rows[:, tokens:] = y_ref[:, :]
    extra = rows[width:, :].astype(jnp.float32)
    place = lax.broadcasted_iota(jnp.int32, extra.shape, 0)
    mine = (place == me_ref[0]) | (place == experts + me_ref[0])
    weight = jnp.sum(jnp.where(mine, extra, 0.0), axis=0, keepdims=True)
    i = 0
    for half in range(2):
        for k in range(parts):
            wait(i)
            gate = jnp.dot(
                gu_v[half, k * part : (k + 1) * part, :],
                rows[:width, :],
                preferred_element_type=jnp.float32,
            )
            wait(i + 1)
            up = jnp.dot(
                gu_v[half, hidden + k * part : hidden + (k + 1) * part, :],
                rows[:width, :],
                preferred_element_type=jnp.float32,
            )
            i += 2
            units[half, k * part : (k + 1) * part, :] = (
                gate / (1.0 + jnp.exp(-gate)) * up
            ).astype(jnp.bfloat16)
    for k in range(depths):
        wait(i)
        wait(i + 1)
        i += 2
        at = slice(k * depth, (k + 1) * depth)
        total = (
            jnp.dot(dn_v[0, at, :], units[0], preferred_element_type=jnp.float32)
            + jnp.dot(dn_v[1, at, :], units[1], preferred_element_type=jnp.float32)
        ) * weight
        if len(out_refs) == 1:
            out_refs[0][at, :] = total.astype(out_refs[0].dtype)
        else:
            out_refs[0][at, :] = total[:, :tokens].astype(out_refs[0].dtype)
            out_refs[1][at, :] = total[:, tokens:].astype(out_refs[1].dtype)


def expert_rows(me, x, y, weights, experts, kinds):
    gu0, gu1, dn0, dn1 = weights
    tokens = x.shape[1]
    hidden, width = gu0.shape[0] // 2, gu0.shape[1]
    parts, depths = hidden // even_rows(hidden, 240), width // even_rows(width, 480)
    vmem = pl.BlockSpec(memory_space=pltpu.VMEM)
    hbm = pl.BlockSpec(memory_space=pl.ANY)
    share = 2 * tokens // len(kinds)
    return pl.pallas_call(
        functools.partial(expert_kernel, experts),
        out_shape=[jax.ShapeDtypeStruct((width, share), kind) for kind in kinds],
        in_specs=[pl.BlockSpec(memory_space=pltpu.SMEM), vmem, vmem, hbm, hbm, hbm, hbm],
        out_specs=[vmem] * len(kinds),
        scratch_shapes=[
            pltpu.VMEM((x.shape[0], 2 * tokens), jnp.bfloat16),
            pltpu.VMEM((2, hidden, 2 * tokens), jnp.bfloat16),
            pltpu.VMEM((2,) + gu0.shape, jnp.bfloat16),
            pltpu.VMEM((2,) + dn0.shape, jnp.bfloat16),
            pltpu.SemaphoreType.DMA((4 * parts + 2 * depths,)),
        ],
        compiler_params=pltpu.CompilerParams(vmem_limit_bytes=VMEM_BYTES),
        cost_estimate=pl.CostEstimate(
            flops=2 * 2 * tokens * 2 * 3 * width * hidden,
            bytes_accessed=2 * 2 * (gu0.size + dn0.size),
            transcendentals=4 * tokens * hidden,
        ),
    )(me, x, y, gu0, gu1, dn0, dn1)


def line_pairs(shards, distance, way, sources):
    planes = shards // PLANE
    return [
        (PLANE * p + r, PLANE * (p + way * distance) + r)
        for p in sources
        if 0 <= p + way * distance < planes
        for r in range(PLANE)
    ]


def column_pairs(planes):
    return [(PLANE * p + r, (PLANE * p + r) ^ 2) for p in planes for r in range(PLANE)]


def passed_rows(own, plane, planes):
    shards = planes * PLANE
    found = []
    below = above = own
    merged = None
    for distance in range(1, planes):
        from_below = range(distance, planes)
        from_above = range(planes - distance)
        if merged is None:
            below = lax.ppermute(
                below, "seq", line_pairs(shards, 1, 1, range(distance - 1, planes))
            )
            above = lax.ppermute(
                above, "seq", line_pairs(shards, 1, -1, range(planes - distance + 1))
            )
        else:
            merged = lax.ppermute(
                merged,
                "seq",
                line_pairs(shards, 1, 1, range(distance - 1, planes))
                + line_pairs(shards, 1, -1, range(planes - distance + 1)),
            )
        if 2 * distance < planes:
            found.append((distance, [(p, 1) for p in from_below], below))
            found.append((distance, [(p, -1) for p in from_above], above))
        else:
            if merged is None:
                merged = jnp.where(plane >= distance, below, above)
            holders = [(p, 1) for p in from_below] + [(p, -1) for p in from_above]
            found.append((distance, holders, merged))
    return found


def on_device(
    query_rows,
    key_rows,
    value_rows,
    sink_positions,
    residual,
    out_proj,
    norm_gain,
    expert_ids,
    route_weights,
    gate_up,
    down_proj,
):
    rows_dev = query_rows.shape[0]
    width = residual.shape[1]
    shards = lax.axis_size("seq")
    planes = shards // PLANE
    experts = shards // 2
    my_index = lax.axis_index("seq")
    plane = my_index // PLANE
    first_pos = my_index * rows_dev
    own_pos = first_pos + jnp.arange(rows_dev, dtype=jnp.int32)

    local_rows = jnp.concatenate([key_rows, value_rows], 1)
    halo_rows = lax.ppermute(local_rows, "seq", [(i, i + 1) for i in range(shards - 1)])
    pick_rows = (sink_positions[:, None] == own_pos[None, :]).astype(jnp.bfloat16)
    sink_rows = jnp.dot(pick_rows, local_rows, preferred_element_type=jnp.float32)
    sink_rows = summed(sink_rows.astype(jnp.bfloat16), "seq")

    to_core = [(i, i ^ 1) for i in range(shards)]
    gu_own = jnp.swapaxes(gate_up[0], 0, 1)
    dn_own = jnp.swapaxes(down_proj[0], 0, 1)
    gu_other = lax.ppermute(gu_own, "seq", to_core)
    dn_other = lax.ppermute(dn_own, "seq", to_core)
    weights = (gu_own, gu_other, dn_own, dn_other)

    joined = jnp.concatenate([halo_rows, local_rows], 0)
    keys_joined = joined[:, : key_rows.shape[1]]
    values_joined = joined[:, key_rows.shape[1] :]
    key_pos = first_pos - WINDOW + jnp.arange(rows_dev + WINDOW, dtype=jnp.int32)
    allowed = jnp.concatenate(
        [window_allowed(own_pos, key_pos), sink_allowed(sink_positions, own_pos)], 0
    )
    bias = jnp.where(allowed, 0.0, NEVER).astype(jnp.float32)
    hidden_state, own = attended_rows(
        query_rows.T,
        keys_joined,
        values_joined,
        sink_rows,
        bias,
        residual.T,
        norm_gain[:, None],
        expert_ids.T,
        route_weights.T,
        out_proj.T,
        experts,
    )

    me = (my_index // 2).reshape(1)
    every = range(planes)
    own_cross = lax.ppermute(own, "seq", column_pairs(every))
    found = passed_rows(own, plane, planes)
    crossed = [
        lax.ppermute(block, "seq", column_pairs(sorted(p for p, _ in holders)))
        for _, holders, block in found
    ]
    (mine,) = expert_rows(me, own, own_cross, weights, experts, (jnp.float32,))
    column_sum = hidden_state.astype(jnp.float32) + mine[:, :rows_dev]
    cross_sum = mine[:, rows_dev:]
    for (distance, holders, x), y in zip(found, crossed):
        home = [
            (PLANE * p + r, PLANE * (p - way * distance) + r)
            for p, way in holders
            for r in range(PLANE)
        ]
        if distance == 1:
            (part,) = expert_rows(me, x, y, weights, experts, (jnp.bfloat16,))
            back = lax.ppermute(part, "seq", home).astype(jnp.float32)
            column_sum = column_sum + back[:, :rows_dev]
            cross_sum = cross_sum + back[:, rows_dev:]
        else:
            mine, theirs = expert_rows(me, x, y, weights, experts, (jnp.float32, jnp.bfloat16))
            theirs = lax.ppermute(
                theirs, "seq", column_pairs(sorted(p for p, _ in holders))
            )
            both = (mine + theirs.astype(jnp.float32)).astype(jnp.bfloat16)
            column_sum = column_sum + lax.ppermute(both, "seq", home).astype(jnp.float32)
    crossing = lax.ppermute(cross_sum.astype(jnp.bfloat16), "seq", column_pairs(every))
    return (column_sum + crossing.astype(jnp.float32)).astype(jnp.bfloat16).T


def solution(mesh):
    in_specs = (
        P(("groups", "seq"), None),
        P(("groups", "seq"), None),
        P(("groups", "seq"), None),
        P("groups"),
        P(("groups", "seq"), None),
        P(),
        P(),
        P(("groups", "seq"), None),
        P(("groups", "seq"), None),
        P("seq", None, None),
        P("seq", None, None),
    )
    out_specs = P(("groups", "seq"), None)
    return jax.shard_map(
        on_device, mesh=mesh, in_specs=in_specs, out_specs=out_specs, check_vma=False
    )
```

```python
import functools

import jax
import jax.numpy as jnp
from jax import lax
from jax.experimental import pallas as pl
from jax.experimental.pallas import tpu as pltpu
from jax.sharding import PartitionSpec as P

Q_HEADS = 32
KV_HEADS = 4
HEAD_DIM = 64
WINDOW = 128
TOPK = 4
PLANE = 4
NEVER = -1e30
VMEM_BYTES = 56 * 1024 * 1024
HIDDEN_PART = 720
OUT_PART = 1024
AHEAD = 8


def window_allowed(query_pos, key_pos):
    return (
        (key_pos[:, None] >= 0)
        & (key_pos[:, None] <= query_pos[None, :])
        & (key_pos[:, None] > query_pos[None, :] - WINDOW)
    )


def sink_allowed(sink_positions, query_pos):
    order = jnp.arange(sink_positions.shape[0], dtype=jnp.int32)
    repeated = jnp.any(
        (sink_positions[:, None] == sink_positions[None, :]) & (order[:, None] > order[None, :]),
        axis=1,
    )
    return (~repeated)[:, None] & (sink_positions[:, None] <= query_pos[None, :] - WINDOW)


def after(block, *earlier):
    return lax.optimization_barrier((block, earlier))[0]


def summed(block, axis, halo):
    shards = lax.axis_size(axis)
    step = 1
    while step < shards:
        reach = min(4, shards // step)
        parts = [
            lax.ppermute(block, axis, [(i, i ^ (step * m)) for i in range(shards)])
            for m in range(1, reach)
        ]
        for part in parts:
            block = block + part
        if step == 1:
            block = after(block, halo)
        step *= reach
    return block


def even_rows(rows, most):
    return max(r for r in range(16, most + 1, 16) if rows % r == 0)


def fetched(pieces, sems, ahead):
    copies = [pltpu.make_async_copy(src, dst, sems.at[i]) for i, (src, dst) in enumerate(pieces)]
    for copy in copies[:ahead]:
        copy.start()

    def wait(i):
        copies[i].wait()
        if i + ahead < len(copies):
            copies[i + ahead].start()

    return wait


def attention_kernel(
    experts,
    query_t,
    keys,
    values,
    sinks,
    bias,
    residual_t,
    gain,
    ids_t,
    route_t,
    out_proj_t,
    hidden_ref,
    rows_ref,
    proj_v,
    att_v,
    sems,
):
    width, heads_width = proj_v.shape
    tokens = query_t.shape[1]
    part = even_rows(width, 480)
    parts = width // part
    wait = fetched(
        [
            (out_proj_t.at[pl.ds(r * part, part)], proj_v.at[pl.ds(r * part, part)])
            for r in range(parts)
        ],
        sems,
        parts,
    )
    group = Q_HEADS // KV_HEADS
    near = keys.shape[0]
    wide_bias = jnp.concatenate([bias[:, :]] * group, 1)
    scale = HEAD_DIM ** (-0.5)
    for g in range(KV_HEADS):
        lanes = slice(g * HEAD_DIM, (g + 1) * HEAD_DIM)
        value_lanes = slice((KV_HEADS + g) * HEAD_DIM, (KV_HEADS + g + 1) * HEAD_DIM)
        first = g * group * HEAD_DIM
        query = jnp.concatenate(
            [
                query_t[first + h * HEAD_DIM : first + (h + 1) * HEAD_DIM, :]
                for h in range(group)
            ],
            1,
        )
        near_scores = (
            jnp.dot(keys[:, lanes], query, preferred_element_type=jnp.float32) * scale
            + wide_bias[:near]
        )
        sink_scores = (
            jnp.dot(sinks[:, lanes], query, preferred_element_type=jnp.float32) * scale
            + wide_bias[near:]
        )
        largest = jnp.maximum(
            jnp.max(near_scores, axis=0, keepdims=True),
            jnp.max(sink_scores, axis=0, keepdims=True),
        )
        near_terms = jnp.exp(near_scores - largest)
        sink_terms = jnp.exp(sink_scores - largest)
        total = jnp.sum(near_terms, axis=0, keepdims=True) + jnp.sum(
            sink_terms, axis=0, keepdims=True
        )
        down = (((0,), (0,)), ((), ()))
        gathered = lax.dot_general(
            values[:, lanes],
            near_terms.astype(jnp.bfloat16),
            down,
            preferred_element_type=jnp.float32,
        ) + lax.dot_general(
            sinks[:, value_lanes],
            sink_terms.astype(jnp.bfloat16),
            down,
            preferred_element_type=jnp.float32,
        )
        gathered = (gathered / total).astype(jnp.bfloat16)
        for h in range(group):
            att_v[first + h * HEAD_DIM : first + (h + 1) * HEAD_DIM, :] = gathered[
                :, h * tokens : (h + 1) * tokens
            ]
    squares = jnp.zeros((1, tokens), jnp.float32)
    for r in range(parts):
        wait(r)
        rows = slice(r * part, (r + 1) * part)
        state = (
            jnp.dot(proj_v[rows, :], att_v[:, :], preferred_element_type=jnp.float32)
            + residual_t[rows, :].astype(jnp.float32)
        ).astype(jnp.bfloat16)
        hidden_ref[rows, :] = state
        state = state.astype(jnp.float32)
        squares = squares + jnp.sum(state * state, axis=0, keepdims=True)
    inverse = lax.rsqrt(squares / width + 1e-05)
    for r in range(parts):
        rows = slice(r * part, (r + 1) * part)
        rows_ref[rows, :] = (
            hidden_ref[rows, :].astype(jnp.float32) * inverse * gain[rows, :]
        ).astype(jnp.bfloat16)
    expert = lax.broadcasted_iota(jnp.int32, (experts, tokens), 0)
    weight = jnp.zeros((experts, tokens), jnp.float32)
    for k in range(TOPK):
        weight = weight + jnp.where(ids_t[k : k + 1, :] == expert, route_t[k : k + 1, :], 0.0)
    high = weight.astype(jnp.bfloat16).astype(jnp.float32)
    rows_ref[width:, :] = jnp.concatenate([high, weight - high], 0).astype(jnp.bfloat16)


def attended_rows(
    query_t, keys, values, sinks, bias, residual_t, gain, ids_t, route_t, out_proj_t, experts
):
    width, heads_width = out_proj_t.shape
    tokens = query_t.shape[1]
    vmem = pl.BlockSpec(memory_space=pltpu.VMEM)
    return pl.pallas_call(
        functools.partial(attention_kernel, experts),
        out_shape=(
            jax.ShapeDtypeStruct((width, tokens), jnp.bfloat16),
            jax.ShapeDtypeStruct((width + 2 * experts, tokens), jnp.bfloat16),
        ),
        in_specs=[vmem] * 9 + [pl.BlockSpec(memory_space=pl.ANY)],
        out_specs=(vmem, vmem),
        scratch_shapes=[
            pltpu.VMEM((width, heads_width), jnp.bfloat16),
            pltpu.VMEM((heads_width, tokens), jnp.bfloat16),
            pltpu.SemaphoreType.DMA((width // even_rows(width, 480),)),
        ],
        compiler_params=pltpu.CompilerParams(vmem_limit_bytes=VMEM_BYTES),
        cost_estimate=pl.CostEstimate(
            flops=2 * tokens * width * heads_width,
            bytes_accessed=2 * width * heads_width,
            transcendentals=tokens * Q_HEADS * bias.shape[0],
        ),
    )(query_t, keys, values, sinks, bias, residual_t, gain, ids_t, route_t, out_proj_t)


def expert_kernel(experts, me_ref, x_ref, y_ref, gu0, gu1, dn0, dn1, *refs):
    *out_refs, rows, units, gu_v, dn_v, sems = refs
    hidden = gu_v.shape[1] // 2
    width = gu_v.shape[2]
    tokens = x_ref.shape[1]
    part = even_rows(hidden, HIDDEN_PART)
    parts = hidden // part
    pieces = []
    for half, (gate_up, down) in enumerate(((gu0, dn0), (gu1, dn1))):
        for k in range(parts):
            for first in (k * part, hidden + k * part):
                at = pl.ds(first, part)
                pieces.append((gate_up.at[at], gu_v.at[half, at]))
        pieces.append((down, dn_v.at[half]))
    wait = fetched(pieces, sems, AHEAD)
    rows[:, :tokens] = x_ref[:, :]
    rows[:, tokens:] = y_ref[:, :]
    extra = rows[width:, :].astype(jnp.float32)
    place = lax.broadcasted_iota(jnp.int32, extra.shape, 0)
    mine = (place == me_ref[0]) | (place == experts + me_ref[0])
    weight = jnp.sum(jnp.where(mine, extra, 0.0), axis=0, keepdims=True)
    i = 0
    for half in range(2):
        for k in range(parts):
            wait(i)
            gate = jnp.dot(
                gu_v[half, k * part : (k + 1) * part, :],
                rows[:width, :],
                preferred_element_type=jnp.float32,
            )
            wait(i + 1)
            up = jnp.dot(
                gu_v[half, hidden + k * part : hidden + (k + 1) * part, :],
                rows[:width, :],
                preferred_element_type=jnp.float32,
            )
            i += 2
            units[half, k * part : (k + 1) * part, :] = (
                gate / (1.0 + jnp.exp(-gate)) * up
            ).astype(jnp.bfloat16)
        wait(i)
        i += 1
    for first in range(0, width, OUT_PART):
        at = slice(first, min(first + OUT_PART, width))
        total = (product(dn_v[0, :, at], units[0]) + product(dn_v[1, :, at], units[1])) * weight
        if len(out_refs) == 1:
            out_refs[0][at, :] = total.astype(out_refs[0].dtype)
        else:
            out_refs[0][at, :] = total[:, :tokens].astype(out_refs[0].dtype)
            out_refs[1][at, :] = total[:, tokens:].astype(out_refs[1].dtype)


def product(down, units):
    return lax.dot_general(
        down, units, (((0,), (0,)), ((), ())), preferred_element_type=jnp.float32
    )


def expert_rows(me, x, y, weights, experts, kinds):
    gu0, gu1, dn0, dn1 = weights
    tokens = x.shape[1]
    hidden, width = gu0.shape[0] // 2, gu0.shape[1]
    parts = hidden // even_rows(hidden, HIDDEN_PART)
    vmem = pl.BlockSpec(memory_space=pltpu.VMEM)
    hbm = pl.BlockSpec(memory_space=pl.ANY)
    share = 2 * tokens // len(kinds)
    return pl.pallas_call(
        functools.partial(expert_kernel, experts),
        out_shape=[jax.ShapeDtypeStruct((width, share), kind) for kind in kinds],
        in_specs=[pl.BlockSpec(memory_space=pltpu.SMEM), vmem, vmem, hbm, hbm, hbm, hbm],
        out_specs=[vmem] * len(kinds),
        scratch_shapes=[
            pltpu.VMEM((x.shape[0], 2 * tokens), jnp.bfloat16),
            pltpu.VMEM((2, hidden, 2 * tokens), jnp.bfloat16),
            pltpu.VMEM((2,) + gu0.shape, jnp.bfloat16),
            pltpu.VMEM((2,) + dn0.shape, jnp.bfloat16),
            pltpu.SemaphoreType.DMA((4 * parts + 2,)),
        ],
        compiler_params=pltpu.CompilerParams(vmem_limit_bytes=VMEM_BYTES),
        cost_estimate=pl.CostEstimate(
            flops=2 * 2 * tokens * 2 * 3 * width * hidden,
            bytes_accessed=2 * 2 * (gu0.size + dn0.size),
            transcendentals=4 * tokens * hidden,
        ),
    )(me, x, y, gu0, gu1, dn0, dn1)


def line_pairs(moves):
    return [(PLANE * p + r, PLANE * q + r) for p, q in moves for r in range(PLANE)]


def column_pairs(planes):
    return [(PLANE * p + r, (PLANE * p + r) ^ 2) for p in range(planes) for r in range(PLANE)]


def sources(planes):
    return [
        sorted(
            (q for q in range(planes) if q != p),
            key=lambda q: (abs(q - p), -(planes - p if q > p else p)),
        )
        for p in range(planes)
    ]


def rounds(moves):
    lists = []
    for p, q in moves:
        for held in lists:
            if all(q != to for _, to in held):
                held.append((p, q))
                break
        else:
            lists.append([(p, q)])
    return lists


def next_blocks(held, distance, planes):
    up = [(p, p + 1) for p in range(distance - 1, planes - 1)]
    down = [(p, p - 1) for p in range(1, planes - distance + 1)]
    if len(held) == 1 and distance > 1:
        return [lax.ppermute(held[0], "seq", line_pairs(up + down))]
    below, above = held if len(held) == 2 else held * 2
    return [
        lax.ppermute(below, "seq", line_pairs(up)),
        lax.ppermute(above, "seq", line_pairs(down)),
    ]


def slot_block(arrivals, plane, origins):
    chosen = {}
    for p, q in enumerate(origins):
        blocks = arrivals[abs(q - p)]
        block = blocks[0] if len(blocks) == 1 or q < p else blocks[1]
        chosen.setdefault(id(block), (block, []))[1].append(p)
    (result, _), *others = chosen.values()
    for block, holders in others:
        here = functools.reduce(jnp.logical_or, [plane == p for p in holders])
        result = jnp.where(here, block, result)
    return result


def on_device(
    query_rows,
    key_rows,
    value_rows,
    sink_positions,
    residual,
    out_proj,
    norm_gain,
    expert_ids,
    route_weights,
    gate_up,
    down_proj,
):
    rows_dev = query_rows.shape[0]
    width = residual.shape[1]
    shards = lax.axis_size("seq")
    planes = shards // PLANE
    experts = shards // 2
    my_index = lax.axis_index("seq")
    plane = my_index // PLANE
    first_pos = my_index * rows_dev
    own_pos = first_pos + jnp.arange(rows_dev, dtype=jnp.int32)

    local_rows = jnp.concatenate([key_rows, value_rows], 1)
    halo_rows = lax.ppermute(local_rows, "seq", [(i, i + 1) for i in range(shards - 1)])
    pick_rows = (sink_positions[:, None] == own_pos[None, :]).astype(jnp.bfloat16)
    sink_rows = jnp.dot(pick_rows, local_rows, preferred_element_type=jnp.float32)
    sink_rows = summed(sink_rows.astype(jnp.bfloat16), "seq", halo_rows)

    to_core = [(i, i ^ 1) for i in range(shards)]
    gu_own = jnp.swapaxes(gate_up[0], 0, 1)
    dn_own = down_proj[0]
    gu_other = lax.ppermute(gu_own, "seq", to_core)
    dn_other = lax.ppermute(dn_own, "seq", to_core)
    weights = (gu_own, gu_other, dn_own, dn_other)

    joined = jnp.concatenate([halo_rows, local_rows], 0)
    keys_joined = joined[:, : key_rows.shape[1]]
    values_joined = joined[:, key_rows.shape[1] :]
    key_pos = first_pos - WINDOW + jnp.arange(rows_dev + WINDOW, dtype=jnp.int32)
    allowed = jnp.concatenate(
        [window_allowed(own_pos, key_pos), sink_allowed(sink_positions, own_pos)], 0
    )
    bias = jnp.where(allowed, 0.0, NEVER).astype(jnp.float32)
    hidden_state, own = attended_rows(
        query_rows.T,
        keys_joined,
        values_joined,
        sink_rows,
        bias,
        residual.T,
        norm_gain[:, None],
        expert_ids.T,
        route_weights.T,
        out_proj.T,
        experts,
    )

    me = (my_index // 2).reshape(1)
    across = column_pairs(planes)
    order = sources(planes)
    expert = functools.partial(expert_rows, me)
    half = jnp.bfloat16

    held = next_blocks([own], 1, planes)
    arrivals = {1: held}
    cross = lax.ppermute(own, "seq", across)
    block, ready = own, (cross, *held)
    sums = []
    for j in range(1, planes):
        nearer = [after(x, *ready) for x in arrivals[j]]
        next_block = after(slot_block(arrivals, plane, [o[j - 1] for o in order]), *ready)
        next_cross = lax.ppermute(next_block, "seq", across)
        if j + 1 < planes:
            held = next_blocks(nearer, j + 1, planes)
            if len(held) == 2 and 2 * (j + 1) >= planes:
                held = [jnp.where(plane >= j + 1, held[0], held[1])]
            arrivals[j + 1] = held
        else:
            held = []
        flows = []
        if j == 1:
            mine, theirs = expert(block, cross, weights, experts, (jnp.float32, jnp.float32))
            column_sum = hidden_state.astype(jnp.float32) + mine
            cross_sum = theirs
            done = mine
        elif j == 2:
            near = expert(block, cross, weights, experts, (half, half))
            done = near[0]
        else:
            if j == 3:
                flows = [(0, near[0])]
            elif j == 4:
                flows = [(1, near[1])]
            sums.append((j - 1, expert(block, cross, weights, experts, (jnp.float32, half))))
            done = sums[-1][1][1]
        backs = []
        for side, part in flows:
            part = after(part, *ready)
            for moves in rounds([(p, o[0]) for p, o in enumerate(order)]):
                backs.append((side, lax.ppermute(part, "seq", line_pairs(moves))))
        for side, back in backs:
            if side == 0:
                column_sum = column_sum + back.astype(jnp.float32)
            else:
                cross_sum = cross_sum + back.astype(jnp.float32)
        block, cross = next_block, next_cross
        ready = (next_cross, done, *held, *[back for _, back in backs])
    last = planes - 1
    parts = expert(block, cross, weights, experts, (jnp.float32, half))
    sums.append((last, parts))
    pending = None
    for n, (j, (mine, theirs)) in enumerate(sums):
        theirs = after(theirs, *ready)
        returned = lax.ppermute(theirs, "seq", across)
        backs = []
        if n == 0 and planes <= 4:
            part = after(near[1], *ready)
            for moves in rounds([(p, o[0]) for p, o in enumerate(order)]):
                back = lax.ppermute(part, "seq", line_pairs(moves))
                cross_sum = cross_sum + back.astype(jnp.float32)
                backs.append(back)
        if pending is not None:
            k, both = pending
            for moves in rounds([(p, o[k - 1]) for p, o in enumerate(order)]):
                back = lax.ppermute(both, "seq", line_pairs(moves))
                column_sum = column_sum + back.astype(jnp.float32)
        pending = (j, (mine + returned.astype(jnp.float32)).astype(half))
        ready = (returned, *backs)
    crossing = lax.ppermute(after(cross_sum.astype(half), *ready), "seq", across)
    k, both = pending
    for moves in rounds([(p, o[k - 1]) for p, o in enumerate(order)]):
        back = lax.ppermute(both, "seq", line_pairs(moves))
        column_sum = column_sum + back.astype(jnp.float32)
    return (column_sum + crossing.astype(jnp.float32)).astype(half).T


def solution(mesh):
    in_specs = (
        P(("groups", "seq"), None),
        P(("groups", "seq"), None),
        P(("groups", "seq"), None),
        P("groups"),
        P(("groups", "seq"), None),
        P(),
        P(),
        P(("groups", "seq"), None),
        P(("groups", "seq"), None),
        P("seq", None, None),
        P("seq", None, None),
    )
    out_specs = P(("groups", "seq"), None)
    return jax.shard_map(
        on_device, mesh=mesh, in_specs=in_specs, out_specs=out_specs, check_vma=False
    )
```

```python
import functools

import jax
import jax.numpy as jnp
from jax import lax
from jax.experimental import pallas as pl
from jax.experimental.pallas import tpu as pltpu
from jax.sharding import PartitionSpec as P

Q_HEADS = 32
KV_HEADS = 4
HEAD_DIM = 64
WINDOW = 128
TOPK = 4
PLANE = 4
NEVER = -1e30
VMEM_BYTES = 56 * 1024 * 1024
HIDDEN_PART = 720
OUT_PART = 1024
AHEAD = 8


def window_allowed(query_pos, key_pos):
    return (
        (key_pos[:, None] >= 0)
        & (key_pos[:, None] <= query_pos[None, :])
        & (key_pos[:, None] > query_pos[None, :] - WINDOW)
    )


def sink_allowed(sink_positions, query_pos):
    order = jnp.arange(sink_positions.shape[0], dtype=jnp.int32)
    repeated = jnp.any(
        (sink_positions[:, None] == sink_positions[None, :]) & (order[:, None] > order[None, :]),
        axis=1,
    )
    return (~repeated)[:, None] & (sink_positions[:, None] <= query_pos[None, :] - WINDOW)


def after(block, *earlier):
    return lax.optimization_barrier((block, earlier))[0]


def summed(block, axis, halo, later):
    shards = lax.axis_size(axis)
    step = 1
    while step < shards:
        reach = min(4, shards // step)
        parts = [
            lax.ppermute(block, axis, [(i, i ^ (step * m)) for i in range(shards)])
            for m in range(1, reach)
        ]
        for part in parts:
            block = block + part
        if step == 1:
            block, halo, later = lax.optimization_barrier((block, halo, later))
        step *= reach
    return block, halo, later


def even_rows(rows, most):
    return max(r for r in range(16, most + 1, 16) if rows % r == 0)


def fetched(pieces, sems, ahead):
    copies = [pltpu.make_async_copy(src, dst, sems.at[i]) for i, (src, dst) in enumerate(pieces)]
    for copy in copies[:ahead]:
        copy.start()

    def wait(i):
        copies[i].wait()
        if i + ahead < len(copies):
            copies[i + ahead].start()

    return wait


def attention_kernel(
    experts,
    query_t,
    keys,
    values,
    sinks,
    bias,
    residual_t,
    gain,
    ids_t,
    route_t,
    out_proj_t,
    hidden_ref,
    rows_ref,
    proj_v,
    att_v,
    sems,
):
    width, heads_width = proj_v.shape
    tokens = query_t.shape[1]
    part = even_rows(width, 480)
    parts = width // part
    wait = fetched(
        [
            (out_proj_t.at[pl.ds(r * part, part)], proj_v.at[pl.ds(r * part, part)])
            for r in range(parts)
        ],
        sems,
        parts,
    )
    group = Q_HEADS // KV_HEADS
    near = keys.shape[0]
    wide_bias = jnp.concatenate([bias[:, :]] * group, 1)
    scale = HEAD_DIM ** (-0.5)
    for g in range(KV_HEADS):
        lanes = slice(g * HEAD_DIM, (g + 1) * HEAD_DIM)
        value_lanes = slice((KV_HEADS + g) * HEAD_DIM, (KV_HEADS + g + 1) * HEAD_DIM)
        first = g * group * HEAD_DIM
        query = jnp.concatenate(
            [
                query_t[first + h * HEAD_DIM : first + (h + 1) * HEAD_DIM, :]
                for h in range(group)
            ],
            1,
        )
        near_scores = (
            jnp.dot(keys[:, lanes], query, preferred_element_type=jnp.float32) * scale
            + wide_bias[:near]
        )
        sink_scores = (
            jnp.dot(sinks[:, lanes], query, preferred_element_type=jnp.float32) * scale
            + wide_bias[near:]
        )
        largest = jnp.maximum(
            jnp.max(near_scores, axis=0, keepdims=True),
            jnp.max(sink_scores, axis=0, keepdims=True),
        )
        near_terms = jnp.exp(near_scores - largest)
        sink_terms = jnp.exp(sink_scores - largest)
        total = jnp.sum(near_terms, axis=0, keepdims=True) + jnp.sum(
            sink_terms, axis=0, keepdims=True
        )
        down = (((0,), (0,)), ((), ()))
        gathered = lax.dot_general(
            values[:, lanes],
            near_terms.astype(jnp.bfloat16),
            down,
            preferred_element_type=jnp.float32,
        ) + lax.dot_general(
            sinks[:, value_lanes],
            sink_terms.astype(jnp.bfloat16),
            down,
            preferred_element_type=jnp.float32,
        )
        gathered = (gathered / total).astype(jnp.bfloat16)
        for h in range(group):
            att_v[first + h * HEAD_DIM : first + (h + 1) * HEAD_DIM, :] = gathered[
                :, h * tokens : (h + 1) * tokens
            ]
    squares = jnp.zeros((1, tokens), jnp.float32)
    for r in range(parts):
        wait(r)
        rows = slice(r * part, (r + 1) * part)
        state = (
            jnp.dot(proj_v[rows, :], att_v[:, :], preferred_element_type=jnp.float32)
            + residual_t[rows, :].astype(jnp.float32)
        ).astype(jnp.bfloat16)
        hidden_ref[rows, :] = state
        state = state.astype(jnp.float32)
        squares = squares + jnp.sum(state * state, axis=0, keepdims=True)
    inverse = lax.rsqrt(squares / width + 1e-05)
    for r in range(parts):
        rows = slice(r * part, (r + 1) * part)
        rows_ref[rows, :] = (
            hidden_ref[rows, :].astype(jnp.float32) * inverse * gain[rows, :]
        ).astype(jnp.bfloat16)
    expert = lax.broadcasted_iota(jnp.int32, (experts, tokens), 0)
    weight = jnp.zeros((experts, tokens), jnp.float32)
    for k in range(TOPK):
        weight = weight + jnp.where(ids_t[k : k + 1, :] == expert, route_t[k : k + 1, :], 0.0)
    high = weight.astype(jnp.bfloat16).astype(jnp.float32)
    rows_ref[width:, :] = jnp.concatenate([high, weight - high], 0).astype(jnp.bfloat16)


def attended_rows(
    query_t, keys, values, sinks, bias, residual_t, gain, ids_t, route_t, out_proj_t, experts
):
    width, heads_width = out_proj_t.shape
    tokens = query_t.shape[1]
    vmem = pl.BlockSpec(memory_space=pltpu.VMEM)
    return pl.pallas_call(
        functools.partial(attention_kernel, experts),
        out_shape=(
            jax.ShapeDtypeStruct((width, tokens), jnp.bfloat16),
            jax.ShapeDtypeStruct((width + 2 * experts, tokens), jnp.bfloat16),
        ),
        in_specs=[vmem] * 9 + [pl.BlockSpec(memory_space=pl.ANY)],
        out_specs=(vmem, vmem),
        scratch_shapes=[
            pltpu.VMEM((width, heads_width), jnp.bfloat16),
            pltpu.VMEM((heads_width, tokens), jnp.bfloat16),
            pltpu.SemaphoreType.DMA((width // even_rows(width, 480),)),
        ],
        compiler_params=pltpu.CompilerParams(vmem_limit_bytes=VMEM_BYTES),
        cost_estimate=pl.CostEstimate(
            flops=2 * tokens * width * heads_width,
            bytes_accessed=2 * width * heads_width,
            transcendentals=tokens * Q_HEADS * bias.shape[0],
        ),
    )(query_t, keys, values, sinks, bias, residual_t, gain, ids_t, route_t, out_proj_t)


def expert_kernel(experts, me_ref, x_ref, y_ref, gu0, gu1, dn0, dn1, *refs):
    *out_refs, rows, units, gu_v, dn_v, sems = refs
    hidden = gu_v.shape[1] // 2
    width = gu_v.shape[2]
    tokens = x_ref.shape[1]
    part = even_rows(hidden, HIDDEN_PART)
    parts = hidden // part
    pieces = []
    for half, (gate_up, down) in enumerate(((gu0, dn0), (gu1, dn1))):
        for k in range(parts):
            for first in (k * part, hidden + k * part):
                at = pl.ds(first, part)
                pieces.append((gate_up.at[at], gu_v.at[half, at]))
        pieces.append((down, dn_v.at[half]))
    wait = fetched(pieces, sems, AHEAD)
    rows[:, :tokens] = x_ref[:, :]
    rows[:, tokens:] = y_ref[:, :]
    extra = rows[width:, :].astype(jnp.float32)
    place = lax.broadcasted_iota(jnp.int32, extra.shape, 0)
    mine = (place == me_ref[0]) | (place == experts + me_ref[0])
    weight = jnp.sum(jnp.where(mine, extra, 0.0), axis=0, keepdims=True)
    i = 0
    for half in range(2):
        for k in range(parts):
            wait(i)
            gate = jnp.dot(
                gu_v[half, k * part : (k + 1) * part, :],
                rows[:width, :],
                preferred_element_type=jnp.float32,
            )
            wait(i + 1)
            up = jnp.dot(
                gu_v[half, hidden + k * part : hidden + (k + 1) * part, :],
                rows[:width, :],
                preferred_element_type=jnp.float32,
            )
            i += 2
            units[half, k * part : (k + 1) * part, :] = (
                gate / (1.0 + jnp.exp(-gate)) * up
            ).astype(jnp.bfloat16)
        wait(i)
        i += 1
    for first in range(0, width, OUT_PART):
        at = slice(first, min(first + OUT_PART, width))
        total = (product(dn_v[0, :, at], units[0]) + product(dn_v[1, :, at], units[1])) * weight
        if len(out_refs) == 1:
            out_refs[0][at, :] = total.astype(out_refs[0].dtype)
        else:
            out_refs[0][at, :] = total[:, :tokens].astype(out_refs[0].dtype)
            out_refs[1][at, :] = total[:, tokens:].astype(out_refs[1].dtype)


def product(down, units):
    return lax.dot_general(
        down, units, (((0,), (0,)), ((), ())), preferred_element_type=jnp.float32
    )


def expert_rows(me, x, y, weights, experts, kinds):
    gu0, gu1, dn0, dn1 = weights
    tokens = x.shape[1]
    hidden, width = gu0.shape[0] // 2, gu0.shape[1]
    parts = hidden // even_rows(hidden, HIDDEN_PART)
    vmem = pl.BlockSpec(memory_space=pltpu.VMEM)
    hbm = pl.BlockSpec(memory_space=pl.ANY)
    share = 2 * tokens // len(kinds)
    return pl.pallas_call(
        functools.partial(expert_kernel, experts),
        out_shape=[jax.ShapeDtypeStruct((width, share), kind) for kind in kinds],
        in_specs=[pl.BlockSpec(memory_space=pltpu.SMEM), vmem, vmem, hbm, hbm, hbm, hbm],
        out_specs=[vmem] * len(kinds),
        scratch_shapes=[
            pltpu.VMEM((x.shape[0], 2 * tokens), jnp.bfloat16),
            pltpu.VMEM((2, hidden, 2 * tokens), jnp.bfloat16),
            pltpu.VMEM((2,) + gu0.shape, jnp.bfloat16),
            pltpu.VMEM((2,) + dn0.shape, jnp.bfloat16),
            pltpu.SemaphoreType.DMA((4 * parts + 2,)),
        ],
        compiler_params=pltpu.CompilerParams(vmem_limit_bytes=VMEM_BYTES),
        cost_estimate=pl.CostEstimate(
            flops=2 * 2 * tokens * 2 * 3 * width * hidden,
            bytes_accessed=2 * 2 * (gu0.size + dn0.size),
            transcendentals=4 * tokens * hidden,
        ),
    )(me, x, y, gu0, gu1, dn0, dn1)


def line_pairs(moves):
    return [(PLANE * p + r, PLANE * q + r) for p, q in moves for r in range(PLANE)]


def column_pairs(planes):
    return [(PLANE * p + r, (PLANE * p + r) ^ 2) for p in range(planes) for r in range(PLANE)]


def sources(planes):
    return [
        sorted(
            (q for q in range(planes) if q != p),
            key=lambda q: (abs(q - p), -(planes - p if q > p else p)),
        )
        for p in range(planes)
    ]


def rounds(moves):
    lists = []
    for p, q in moves:
        for held in lists:
            if all(q != to for _, to in held):
                held.append((p, q))
                break
        else:
            lists.append([(p, q)])
    return lists


def next_blocks(held, distance, planes):
    up = [(p, p + 1) for p in range(distance - 1, planes - 1)]
    down = [(p, p - 1) for p in range(1, planes - distance + 1)]
    if len(held) == 1 and distance > 1:
        return [lax.ppermute(held[0], "seq", line_pairs(up + down))]
    below, above = held if len(held) == 2 else held * 2
    return [
        lax.ppermute(below, "seq", line_pairs(up)),
        lax.ppermute(above, "seq", line_pairs(down)),
    ]


def slot_block(arrivals, plane, origins):
    chosen = {}
    for p, q in enumerate(origins):
        blocks = arrivals[abs(q - p)]
        block = blocks[0] if len(blocks) == 1 or q < p else blocks[1]
        chosen.setdefault(id(block), (block, []))[1].append(p)
    (result, _), *others = chosen.values()
    for block, holders in others:
        here = functools.reduce(jnp.logical_or, [plane == p for p in holders])
        result = jnp.where(here, block, result)
    return result


def on_device(
    query_rows,
    key_rows,
    value_rows,
    sink_positions,
    residual,
    out_proj,
    norm_gain,
    expert_ids,
    route_weights,
    gate_up,
    down_proj,
):
    rows_dev = query_rows.shape[0]
    width = residual.shape[1]
    shards = lax.axis_size("seq")
    planes = shards // PLANE
    experts = shards // 2
    my_index = lax.axis_index("seq")
    plane = my_index // PLANE
    first_pos = my_index * rows_dev
    own_pos = first_pos + jnp.arange(rows_dev, dtype=jnp.int32)

    local_rows = jnp.concatenate([key_rows, value_rows], 1)
    halo_rows = lax.ppermute(local_rows, "seq", [(i, i + 1) for i in range(shards - 1)])
    pick_rows = (sink_positions[:, None] == own_pos[None, :]).astype(jnp.bfloat16)
    sink_rows = jnp.dot(pick_rows, local_rows, preferred_element_type=jnp.float32)
    later = (query_rows, norm_gain, sink_positions)
    sink_rows, halo_rows, later = summed(
        sink_rows.astype(jnp.bfloat16), "seq", halo_rows, later
    )
    query_rows, norm_gain, sink_positions = later

    to_core = [(i, i ^ 1) for i in range(shards)]
    gu_own = jnp.swapaxes(gate_up[0], 0, 1)
    dn_own = down_proj[0]
    gu_other = lax.ppermute(gu_own, "seq", to_core)
    dn_other = lax.ppermute(dn_own, "seq", to_core)
    weights = (gu_own, gu_other, dn_own, dn_other)

    joined = jnp.concatenate([halo_rows, local_rows], 0)
    keys_joined = joined[:, : key_rows.shape[1]]
    values_joined = joined[:, key_rows.shape[1] :]
    key_pos = first_pos - WINDOW + jnp.arange(rows_dev + WINDOW, dtype=jnp.int32)
    allowed = jnp.concatenate(
        [window_allowed(own_pos, key_pos), sink_allowed(sink_positions, own_pos)], 0
    )
    bias = jnp.where(allowed, 0.0, NEVER).astype(jnp.float32)
    hidden_state, own = attended_rows(
        query_rows.T,
        keys_joined,
        values_joined,
        sink_rows,
        bias,
        residual.T,
        norm_gain[:, None],
        expert_ids.T,
        route_weights.T,
        out_proj.T,
        experts,
    )

    me = (my_index // 2).reshape(1)
    across = column_pairs(planes)
    order = sources(planes)
    expert = functools.partial(expert_rows, me)
    half = jnp.bfloat16

    held = next_blocks([own], 1, planes)
    arrivals = {1: held}
    cross = lax.ppermute(own, "seq", across)
    block, ready = own, (cross, *held)
    sums = []
    for j in range(1, planes):
        nearer = [after(x, *ready) for x in arrivals[j]]
        next_block = after(slot_block(arrivals, plane, [o[j - 1] for o in order]), *ready)
        next_cross = lax.ppermute(next_block, "seq", across)
        if j + 1 < planes:
            held = next_blocks(nearer, j + 1, planes)
        else:
            held = []
        flows = []
        if j == 1:
            mine, theirs = expert(block, cross, weights, experts, (jnp.float32, jnp.float32))
            column_sum = hidden_state.astype(jnp.float32) + mine
            cross_sum = theirs
            done = mine
        elif j == 2:
            near = expert(block, cross, weights, experts, (half, half))
            done = near[0]
        else:
            if j == 3:
                flows = [(0, near[0])]
            elif j == 4:
                flows = [(1, near[1])]
            sums.append((j - 1, expert(block, cross, weights, experts, (jnp.float32, half))))
            done = sums[-1][1][1]
        backs = []
        for side, part in flows:
            part = after(part, *ready)
            for moves in rounds([(p, o[0]) for p, o in enumerate(order)]):
                backs.append((side, lax.ppermute(part, "seq", line_pairs(moves))))
        for side, back in backs:
            if side == 0:
                column_sum = column_sum + back.astype(jnp.float32)
            else:
                cross_sum = cross_sum + back.astype(jnp.float32)
        block, cross = next_block, next_cross
        ready = (next_cross, done, *held, *[back for _, back in backs])
        if held:
            held = [after(x, *ready) for x in held]
            if len(held) == 2 and 2 * (j + 1) >= planes:
                held = [jnp.where(plane >= j + 1, held[0], held[1])]
            arrivals[j + 1] = held
    last = planes - 1
    parts = expert(block, cross, weights, experts, (jnp.float32, half))
    sums.append((last, parts))
    pending = None
    for n, (j, (mine, theirs)) in enumerate(sums):
        theirs = after(theirs, *ready)
        returned = lax.ppermute(theirs, "seq", across)
        backs = []
        if n == 0 and planes <= 4:
            part = after(near[1], *ready)
            for moves in rounds([(p, o[0]) for p, o in enumerate(order)]):
                back = lax.ppermute(part, "seq", line_pairs(moves))
                cross_sum = cross_sum + back.astype(jnp.float32)
                backs.append(back)
        if pending is not None:
            k, both = pending
            for moves in rounds([(p, o[k - 1]) for p, o in enumerate(order)]):
                back = lax.ppermute(both, "seq", line_pairs(moves))
                column_sum = column_sum + back.astype(jnp.float32)
        pending = (j, (mine + returned.astype(jnp.float32)).astype(half))
        ready = (returned, *backs)
    crossing = lax.ppermute(after(cross_sum.astype(half), *ready), "seq", across)
    k, both = pending
    for moves in rounds([(p, o[k - 1]) for p, o in enumerate(order)]):
        back = lax.ppermute(both, "seq", line_pairs(moves))
        column_sum = column_sum + back.astype(jnp.float32)
    return (column_sum + crossing.astype(jnp.float32)).astype(half).T


def solution(mesh):
    in_specs = (
        P(("groups", "seq"), None),
        P(("groups", "seq"), None),
        P(("groups", "seq"), None),
        P("groups"),
        P(("groups", "seq"), None),
        P(),
        P(),
        P(("groups", "seq"), None),
        P(("groups", "seq"), None),
        P("seq", None, None),
        P("seq", None, None),
    )
    out_specs = P(("groups", "seq"), None)
    return jax.shard_map(
        on_device, mesh=mesh, in_specs=in_specs, out_specs=out_specs, check_vma=False
    )
```

```python
import functools

import jax
import jax.numpy as jnp
from jax import lax
from jax.experimental import pallas as pl
from jax.experimental.pallas import tpu as pltpu
from jax.sharding import PartitionSpec as P

Q_HEADS = 32
KV_HEADS = 4
HEAD_DIM = 64
WINDOW = 128
TOPK = 4
PLANE = 4
NEVER = -1e30
VMEM_BYTES = 56 * 1024 * 1024
HIDDEN_PART = 240
OUT_PART = 1024


def window_allowed(query_pos, key_pos):
    return (
        (key_pos[:, None] >= 0)
        & (key_pos[:, None] <= query_pos[None, :])
        & (key_pos[:, None] > query_pos[None, :] - WINDOW)
    )


def sink_allowed(sink_positions, query_pos):
    order = jnp.arange(sink_positions.shape[0], dtype=jnp.int32)
    repeated = jnp.any(
        (sink_positions[:, None] == sink_positions[None, :]) & (order[:, None] > order[None, :]),
        axis=1,
    )
    return (~repeated)[:, None] & (sink_positions[:, None] <= query_pos[None, :] - WINDOW)


def after(block, *earlier):
    return lax.optimization_barrier((block, earlier))[0]


def summed(block, axis, halo, later):
    shards = lax.axis_size(axis)
    step = 1
    while step < shards:
        reach = min(4, shards // step)
        parts = [
            lax.ppermute(block, axis, [(i, i ^ (step * m)) for i in range(shards)])
            for m in range(1, reach)
        ]
        for part in parts:
            block = block + part
        if step == 1:
            block, halo, later = lax.optimization_barrier((block, halo, later))
        step *= reach
    return block, halo, later


def even_rows(rows, most):
    return max(r for r in range(16, most + 1, 16) if rows % r == 0)


def attention_kernel(
    experts,
    query_t,
    keys,
    values,
    sinks,
    bias,
    residual_t,
    gain,
    ids_t,
    route_t,
    out_proj_t,
    hidden_ref,
    rows_ref,
    proj_v,
    att_v,
    sems,
):
    parts, part, heads_width = proj_v.shape
    width = parts * part
    tokens = query_t.shape[1]

    def proj_copy(r):
        at = pl.ds(pl.multiple_of(r * part, 16), part)
        return pltpu.make_async_copy(out_proj_t.at[at], proj_v.at[r], sems.at[r])

    for r in range(parts):
        proj_copy(r).start()
    group = Q_HEADS // KV_HEADS
    near = keys.shape[0]
    wide_bias = jnp.concatenate([bias[:, :]] * group, 1)
    scale = HEAD_DIM ** (-0.5)
    for g in range(KV_HEADS):
        lanes = slice(g * HEAD_DIM, (g + 1) * HEAD_DIM)
        value_lanes = slice((KV_HEADS + g) * HEAD_DIM, (KV_HEADS + g + 1) * HEAD_DIM)
        first = g * group * HEAD_DIM
        query = jnp.concatenate(
            [
                query_t[first + h * HEAD_DIM : first + (h + 1) * HEAD_DIM, :]
                for h in range(group)
            ],
            1,
        )
        near_scores = (
            jnp.dot(keys[:, lanes], query, preferred_element_type=jnp.float32) * scale
            + wide_bias[:near]
        )
        sink_scores = (
            jnp.dot(sinks[:, lanes], query, preferred_element_type=jnp.float32) * scale
            + wide_bias[near:]
        )
        largest = jnp.maximum(
            jnp.max(near_scores, axis=0, keepdims=True),
            jnp.max(sink_scores, axis=0, keepdims=True),
        )
        near_terms = jnp.exp(near_scores - largest)
        sink_terms = jnp.exp(sink_scores - largest)
        total = jnp.sum(near_terms, axis=0, keepdims=True) + jnp.sum(
            sink_terms, axis=0, keepdims=True
        )
        down = (((0,), (0,)), ((), ()))
        gathered = lax.dot_general(
            values[:, lanes],
            near_terms.astype(jnp.bfloat16),
            down,
            preferred_element_type=jnp.float32,
        ) + lax.dot_general(
            sinks[:, value_lanes],
            sink_terms.astype(jnp.bfloat16),
            down,
            preferred_element_type=jnp.float32,
        )
        gathered = (gathered / total).astype(jnp.bfloat16)
        for h in range(group):
            att_v[first + h * HEAD_DIM : first + (h + 1) * HEAD_DIM, :] = gathered[
                :, h * tokens : (h + 1) * tokens
            ]

    def project(r, squares):
        proj_copy(r).wait()
        rows = pl.ds(pl.multiple_of(r * part, 16), part)
        state = (
            jnp.dot(proj_v[r], att_v[:, :], preferred_element_type=jnp.float32)
            + residual_t[rows, :].astype(jnp.float32)
        ).astype(jnp.bfloat16)
        hidden_ref[rows, :] = state
        state = state.astype(jnp.float32)
        return squares + jnp.sum(state * state, axis=0, keepdims=True)

    squares = lax.fori_loop(0, parts, project, jnp.zeros((1, tokens), jnp.float32))
    inverse = lax.rsqrt(squares / width + 1e-05)
    for r in range(parts):
        rows = slice(r * part, (r + 1) * part)
        rows_ref[rows, :] = (
            hidden_ref[rows, :].astype(jnp.float32) * inverse * gain[rows, :]
        ).astype(jnp.bfloat16)
    expert = lax.broadcasted_iota(jnp.int32, (experts, tokens), 0)
    weight = jnp.zeros((experts, tokens), jnp.float32)
    for k in range(TOPK):
        weight = weight + jnp.where(ids_t[k : k + 1, :] == expert, route_t[k : k + 1, :], 0.0)
    high = weight.astype(jnp.bfloat16).astype(jnp.float32)
    rows_ref[width:, :] = jnp.concatenate([high, weight - high], 0).astype(jnp.bfloat16)


def attended_rows(
    query_t, keys, values, sinks, bias, residual_t, gain, ids_t, route_t, out_proj_t, experts
):
    width, heads_width = out_proj_t.shape
    tokens = query_t.shape[1]
    part = even_rows(width, 480)
    parts = width // part
    vmem = pl.BlockSpec(memory_space=pltpu.VMEM)
    return pl.pallas_call(
        functools.partial(attention_kernel, experts),
        out_shape=(
            jax.ShapeDtypeStruct((width, tokens), jnp.bfloat16),
            jax.ShapeDtypeStruct((width + 2 * experts, tokens), jnp.bfloat16),
        ),
        in_specs=[vmem] * 9 + [pl.BlockSpec(memory_space=pl.ANY)],
        out_specs=(vmem, vmem),
        scratch_shapes=[
            pltpu.VMEM((parts, part, heads_width), jnp.bfloat16),
            pltpu.VMEM((heads_width, tokens), jnp.bfloat16),
            pltpu.SemaphoreType.DMA((parts,)),
        ],
        compiler_params=pltpu.CompilerParams(vmem_limit_bytes=VMEM_BYTES),
        cost_estimate=pl.CostEstimate(
            flops=2 * tokens * width * heads_width,
            bytes_accessed=2 * width * heads_width,
            transcendentals=tokens * Q_HEADS * bias.shape[0],
        ),
    )(query_t, keys, values, sinks, bias, residual_t, gain, ids_t, route_t, out_proj_t)


def expert_kernel(experts, me_ref, x_ref, y_ref, gu0, gu1, dn0, dn1, *refs):
    *out_refs, rows, units, gu_v, dn_v, gu_sems, dn_sems = refs
    hidden = units.shape[1]
    width = gu_v.shape[4]
    tokens = x_ref.shape[1]
    parts, part = gu_v.shape[2:4]

    def gate_up_copy(half, side, k):
        source = (gu0, gu1)[half].at[pl.ds(pl.multiple_of(side * hidden + k * part, 16), part)]
        return pltpu.make_async_copy(source, gu_v.at[half, side, k], gu_sems.at[half, side, k])

    def down_copy(half, k):
        at = pl.ds(pl.multiple_of(k * part, 16), part)
        source = (dn0, dn1)[half].at[at]
        return pltpu.make_async_copy(source, dn_v.at[half, at], dn_sems.at[half, k])

    for k in range(parts):
        gate_up_copy(0, 0, k).start()
        gate_up_copy(0, 1, k).start()
    rows[:, :tokens] = x_ref[:, :]
    rows[:, tokens:] = y_ref[:, :]

    def step(half, k):
        gate_up_copy(half, 0, k).wait()
        gate_up_copy(half, 1, k).wait()
        if half == 0:
            gate_up_copy(1, 0, k).start()
            gate_up_copy(1, 1, k).start()
            down_copy(0, k).start()
        else:
            down_copy(1, k).start()
        gate, up = (
            jnp.dot(gu_v[half, side, k], rows[:width, :], preferred_element_type=jnp.float32)
            for side in range(2)
        )
        units[half, pl.ds(pl.multiple_of(k * part, 16), part), :] = (
            gate / (1.0 + jnp.exp(-gate)) * up
        ).astype(jnp.bfloat16)

    for half in range(2):
        pl.loop(0, parts)(functools.partial(step, half))
    extra = rows[width:, :].astype(jnp.float32)
    place = lax.broadcasted_iota(jnp.int32, extra.shape, 0)
    mine = (place == me_ref[0]) | (place == experts + me_ref[0])
    weight = jnp.sum(jnp.where(mine, extra, 0.0), axis=0, keepdims=True)
    for half in range(2):
        for k in range(parts):
            down_copy(half, k).wait()
    for first in range(0, width, OUT_PART):
        at = slice(first, min(first + OUT_PART, width))
        total = (product(dn_v[0, :, at], units[0]) + product(dn_v[1, :, at], units[1])) * weight
        out_refs[0][at, :] = total[:, :tokens].astype(out_refs[0].dtype)
        out_refs[1][at, :] = total[:, tokens:].astype(out_refs[1].dtype)


def product(down, units):
    return lax.dot_general(
        down, units, (((0,), (0,)), ((), ())), preferred_element_type=jnp.float32
    )


def expert_rows(me, x, y, weights, experts, kinds):
    gu0, gu1, dn0, dn1 = weights
    tokens = x.shape[1]
    hidden, width = gu0.shape[0] // 2, gu0.shape[1]
    part = even_rows(hidden, HIDDEN_PART)
    parts = hidden // part
    vmem = pl.BlockSpec(memory_space=pltpu.VMEM)
    hbm = pl.BlockSpec(memory_space=pl.ANY)
    return pl.pallas_call(
        functools.partial(expert_kernel, experts),
        out_shape=[jax.ShapeDtypeStruct((width, tokens), kind) for kind in kinds],
        in_specs=[pl.BlockSpec(memory_space=pltpu.SMEM), vmem, vmem, hbm, hbm, hbm, hbm],
        out_specs=[vmem] * len(kinds),
        scratch_shapes=[
            pltpu.VMEM((x.shape[0], 2 * tokens), jnp.bfloat16),
            pltpu.VMEM((2, hidden, 2 * tokens), jnp.bfloat16),
            pltpu.VMEM((2, 2, parts, part, width), jnp.bfloat16),
            pltpu.VMEM((2,) + dn0.shape, jnp.bfloat16),
            pltpu.SemaphoreType.DMA((2, 2, parts)),
            pltpu.SemaphoreType.DMA((2, parts)),
        ],
        compiler_params=pltpu.CompilerParams(vmem_limit_bytes=VMEM_BYTES),
        cost_estimate=pl.CostEstimate(
            flops=2 * 2 * tokens * 2 * 3 * width * hidden,
            bytes_accessed=2 * 2 * (gu0.size + dn0.size),
            transcendentals=4 * tokens * hidden,
        ),
    )(me, x, y, gu0, gu1, dn0, dn1)


def line_pairs(moves):
    return [(PLANE * p + r, PLANE * q + r) for p, q in moves for r in range(PLANE)]


def column_pairs(planes):
    return [(PLANE * p + r, (PLANE * p + r) ^ 2) for p in range(planes) for r in range(PLANE)]


def sources(planes):
    return [
        sorted(
            (q for q in range(planes) if q != p),
            key=lambda q: (abs(q - p), -(planes - p if q > p else p)),
        )
        for p in range(planes)
    ]


def rounds(moves):
    lists = []
    for p, q in moves:
        for held in lists:
            if all(q != to for _, to in held):
                held.append((p, q))
                break
        else:
            lists.append([(p, q)])
    return lists


def next_blocks(held, distance, planes):
    up = [(p, p + 1) for p in range(distance - 1, planes - 1)]
    down = [(p, p - 1) for p in range(1, planes - distance + 1)]
    if len(held) == 1 and distance > 1:
        return [lax.ppermute(held[0], "seq", line_pairs(up + down))]
    below, above = held if len(held) == 2 else held * 2
    return [
        lax.ppermute(below, "seq", line_pairs(up)),
        lax.ppermute(above, "seq", line_pairs(down)),
    ]


def slot_block(arrivals, plane, origins):
    chosen = {}
    for p, q in enumerate(origins):
        blocks = arrivals[abs(q - p)]
        block = blocks[0] if len(blocks) == 1 or q < p else blocks[1]
        chosen.setdefault(id(block), (block, []))[1].append(p)
    (result, _), *others = chosen.values()
    for block, holders in others:
        here = functools.reduce(jnp.logical_or, [plane == p for p in holders])
        result = jnp.where(here, block, result)
    return result


def on_device(
    query_rows,
    key_rows,
    value_rows,
    sink_positions,
    residual,
    out_proj,
    norm_gain,
    expert_ids,
    route_weights,
    gate_up,
    down_proj,
):
    rows_dev = query_rows.shape[0]
    width = residual.shape[1]
    shards = lax.axis_size("seq")
    planes = shards // PLANE
    experts = shards // 2
    my_index = lax.axis_index("seq")
    plane = my_index // PLANE
    first_pos = my_index * rows_dev
    own_pos = first_pos + jnp.arange(rows_dev, dtype=jnp.int32)

    local_rows = jnp.concatenate([key_rows, value_rows], 1)
    halo_rows = lax.ppermute(local_rows, "seq", [(i, i + 1) for i in range(shards - 1)])
    pick_rows = (sink_positions[:, None] == own_pos[None, :]).astype(jnp.bfloat16)
    sink_rows = jnp.dot(pick_rows, local_rows, preferred_element_type=jnp.float32)
    later = (query_rows, norm_gain, sink_positions)
    sink_rows, halo_rows, later = summed(
        sink_rows.astype(jnp.bfloat16), "seq", halo_rows, later
    )
    query_rows, norm_gain, sink_positions = later

    to_core = [(i, i ^ 1) for i in range(shards)]
    gu_own = jnp.swapaxes(gate_up[0], 0, 1)
    dn_own = down_proj[0]
    gu_other = lax.ppermute(gu_own, "seq", to_core)
    dn_other = lax.ppermute(dn_own, "seq", to_core)
    weights = (gu_own, gu_other, dn_own, dn_other)

    joined = jnp.concatenate([halo_rows, local_rows], 0)
    keys_joined = joined[:, : key_rows.shape[1]]
    values_joined = joined[:, key_rows.shape[1] :]
    key_pos = first_pos - WINDOW + jnp.arange(rows_dev + WINDOW, dtype=jnp.int32)
    allowed = jnp.concatenate(
        [window_allowed(own_pos, key_pos), sink_allowed(sink_positions, own_pos)], 0
    )
    bias = jnp.where(allowed, 0.0, NEVER).astype(jnp.float32)
    hidden_state, own = attended_rows(
        query_rows.T,
        keys_joined,
        values_joined,
        sink_rows,
        bias,
        residual.T,
        norm_gain[:, None],
        expert_ids.T,
        route_weights.T,
        out_proj.T,
        experts,
    )

    me = (my_index // 2).reshape(1)
    across = column_pairs(planes)
    order = sources(planes)
    expert = functools.partial(expert_rows, me)
    half = jnp.bfloat16

    held = next_blocks([own], 1, planes)
    arrivals = {1: held}
    cross = lax.ppermute(own, "seq", across)
    block, ready = own, (cross, *held)
    sums = []
    for j in range(1, planes):
        nearer = [after(x, *ready) for x in arrivals[j]]
        next_block = after(slot_block(arrivals, plane, [o[j - 1] for o in order]), *ready)
        next_cross = lax.ppermute(next_block, "seq", across)
        if j + 1 < planes:
            held = next_blocks(nearer, j + 1, planes)
        else:
            held = []
        flows = []
        if j == 1:
            mine, theirs = expert(block, cross, weights, experts, (jnp.float32, jnp.float32))
            column_sum = hidden_state.astype(jnp.float32) + mine
            cross_sum = theirs
            done = mine
        elif j == 2:
            near = expert(block, cross, weights, experts, (half, half))
            done = near[0]
        else:
            if j == 3:
                flows = [(0, near[0])]
            elif j == 4:
                flows = [(1, near[1])]
            sums.append((j - 1, expert(block, cross, weights, experts, (jnp.float32, half))))
            done = sums[-1][1][1]
        backs = []
        for side, part in flows:
            part = after(part, *ready)
            for moves in rounds([(p, o[0]) for p, o in enumerate(order)]):
                backs.append((side, lax.ppermute(part, "seq", line_pairs(moves))))
        for side, back in backs:
            if side == 0:
                column_sum = column_sum + back.astype(jnp.float32)
            else:
                cross_sum = cross_sum + back.astype(jnp.float32)
        block, cross = next_block, next_cross
        ready = (next_cross, done, *held, *[back for _, back in backs])
        if held:
            held = [after(x, *ready) for x in held]
            if len(held) == 2 and 2 * (j + 1) >= planes:
                held = [jnp.where(plane >= j + 1, held[0], held[1])]
            arrivals[j + 1] = held
    last = planes - 1
    parts = expert(block, cross, weights, experts, (jnp.float32, half))
    sums.append((last, parts))
    pending = None
    for n, (j, (mine, theirs)) in enumerate(sums):
        theirs = after(theirs, *ready)
        returned = lax.ppermute(theirs, "seq", across)
        backs = []
        if n == 0 and planes <= 4:
            part = after(near[1], *ready)
            for moves in rounds([(p, o[0]) for p, o in enumerate(order)]):
                back = lax.ppermute(part, "seq", line_pairs(moves))
                cross_sum = cross_sum + back.astype(jnp.float32)
                backs.append(back)
        if pending is not None:
            k, both = pending
            for moves in rounds([(p, o[k - 1]) for p, o in enumerate(order)]):
                back = lax.ppermute(both, "seq", line_pairs(moves))
                column_sum = column_sum + back.astype(jnp.float32)
        pending = (j, (mine + returned.astype(jnp.float32)).astype(half))
        ready = (returned, *backs)
    crossing = lax.ppermute(after(cross_sum.astype(half), *ready), "seq", across)
    k, both = pending
    for moves in rounds([(p, o[k - 1]) for p, o in enumerate(order)]):
        back = lax.ppermute(both, "seq", line_pairs(moves))
        column_sum = column_sum + back.astype(jnp.float32)
    return (column_sum + crossing.astype(jnp.float32)).astype(half).T


def solution(mesh):
    in_specs = (
        P(("groups", "seq"), None),
        P(("groups", "seq"), None),
        P(("groups", "seq"), None),
        P("groups"),
        P(("groups", "seq"), None),
        P(),
        P(),
        P(("groups", "seq"), None),
        P(("groups", "seq"), None),
        P("seq", None, None),
        P("seq", None, None),
    )
    out_specs = P(("groups", "seq"), None)
    return jax.shard_map(
        on_device, mesh=mesh, in_specs=in_specs, out_specs=out_specs, check_vma=False
    )
```

```python
import functools

import jax
import jax.numpy as jnp
from jax import lax
from jax.experimental import pallas as pl
from jax.experimental.pallas import tpu as pltpu
from jax.sharding import PartitionSpec as P

Q_HEADS = 32
KV_HEADS = 4
HEAD_DIM = 64
WINDOW = 128
TOPK = 4
PLANE = 4
NEVER = -1e30
VMEM_BYTES = 56 * 1024 * 1024
HIDDEN_PART = 240
OUT_PART = 1024


def prepare_kernel(index_ref, sinks_ref, keys, values, joined_ref, picked_ref, bias_ref):
    tokens, key_width = keys.shape
    count = sinks_ref.shape[0]
    first_pos = index_ref[0] * tokens
    slot = lax.broadcasted_iota(jnp.int32, (count, tokens), 0)
    lane = lax.broadcasted_iota(jnp.int32, (count, tokens), 1)
    place = jnp.zeros((count, tokens), jnp.int32)
    seen = jnp.zeros((count, tokens), jnp.int32)
    for i in range(count):
        repeated = jnp.int32(0)
        for k in range(i):
            repeated = jnp.where(sinks_ref[i] == sinks_ref[k], jnp.int32(1), repeated)
        place = jnp.where(slot == i, sinks_ref[i], place)
        seen = jnp.where(slot == i, repeated, seen)
    pick = jnp.where(place == first_pos + lane, 1.0, 0.0).astype(jnp.bfloat16)
    for at, rows in ((slice(0, key_width), keys), (slice(key_width, None), values)):
        joined_ref[:, at] = rows[:, :]
        picked_ref[:, at] = jnp.dot(
            pick, rows[:, :], preferred_element_type=jnp.float32
        ).astype(jnp.bfloat16)
    near = bias_ref.shape[0] - count
    key_pos = first_pos - WINDOW + lax.broadcasted_iota(jnp.int32, (near, tokens), 0)
    query_pos = first_pos + lax.broadcasted_iota(jnp.int32, (near, tokens), 1)
    allowed = (key_pos >= 0) & (key_pos <= query_pos) & (key_pos > query_pos - WINDOW)
    bias_ref[:near, :] = jnp.where(allowed, 0.0, NEVER)
    allowed = (seen == 0) & (place <= first_pos + lane - WINDOW)
    bias_ref[near:, :] = jnp.where(allowed, 0.0, NEVER)


def prepared(index, sink_positions, key_rows, value_rows):
    tokens, key_width = key_rows.shape
    count = sink_positions.shape[0]
    smem, vmem = (pl.BlockSpec(memory_space=space) for space in (pltpu.SMEM, pltpu.VMEM))
    return pl.pallas_call(
        prepare_kernel,
        out_shape=(
            jax.ShapeDtypeStruct((tokens, 2 * key_width), jnp.bfloat16),
            jax.ShapeDtypeStruct((count, 2 * key_width), jnp.bfloat16),
            jax.ShapeDtypeStruct((WINDOW + tokens + count, tokens), jnp.float32),
        ),
        in_specs=[smem, smem, vmem, vmem],
        out_specs=(vmem, vmem, vmem),
    )(index, sink_positions, key_rows, value_rows)


def after(block, *earlier):
    return lax.optimization_barrier((block, earlier))[0]


def summed(block, axis, halo, later):
    shards = lax.axis_size(axis)
    step = 1
    while step < shards:
        reach = min(4, shards // step)
        parts = [
            lax.ppermute(block, axis, [(i, i ^ (step * m)) for i in range(shards)])
            for m in range(1, reach)
        ]
        for part in parts:
            block = block + part
        if step == 1:
            block, halo, later = lax.optimization_barrier((block, halo, later))
        step *= reach
    return block, halo, later


def even_rows(rows, most):
    return max(r for r in range(16, most + 1, 16) if rows % r == 0)


def attention_kernel(
    experts,
    query_t,
    halo,
    local,
    sinks,
    bias,
    residual_t,
    gain,
    ids_t,
    route_t,
    out_proj_t,
    hidden_ref,
    rows_ref,
    proj_v,
    att_v,
    sems,
):
    parts, part, heads_width = proj_v.shape
    width = parts * part
    tokens = query_t.shape[1]

    def proj_copy(r):
        at = pl.ds(pl.multiple_of(r * part, 16), part)
        return pltpu.make_async_copy(out_proj_t.at[at], proj_v.at[r], sems.at[r])

    for r in range(parts):
        proj_copy(r).start()
    group = Q_HEADS // KV_HEADS
    near = halo.shape[0] + local.shape[0]
    wide_bias = jnp.concatenate([bias[:, :]] * group, 1)
    scale = HEAD_DIM ** (-0.5)
    for g in range(KV_HEADS):
        lanes = slice(g * HEAD_DIM, (g + 1) * HEAD_DIM)
        value_lanes = slice((KV_HEADS + g) * HEAD_DIM, (KV_HEADS + g + 1) * HEAD_DIM)
        first = g * group * HEAD_DIM
        query = jnp.concatenate(
            [
                query_t[first + h * HEAD_DIM : first + (h + 1) * HEAD_DIM, :]
                for h in range(group)
            ],
            1,
        )
        near_scores = (
            jnp.dot(
                jnp.concatenate([halo[:, lanes], local[:, lanes]], 0),
                query,
                preferred_element_type=jnp.float32,
            )
            * scale
            + wide_bias[:near]
        )
        sink_scores = (
            jnp.dot(sinks[:, lanes], query, preferred_element_type=jnp.float32) * scale
            + wide_bias[near:]
        )
        largest = jnp.maximum(
            jnp.max(near_scores, axis=0, keepdims=True),
            jnp.max(sink_scores, axis=0, keepdims=True),
        )
        near_terms = jnp.exp(near_scores - largest)
        sink_terms = jnp.exp(sink_scores - largest)
        total = jnp.sum(near_terms, axis=0, keepdims=True) + jnp.sum(
            sink_terms, axis=0, keepdims=True
        )
        down = (((0,), (0,)), ((), ()))
        gathered = lax.dot_general(
            jnp.concatenate([halo[:, value_lanes], local[:, value_lanes]], 0),
            near_terms.astype(jnp.bfloat16),
            down,
            preferred_element_type=jnp.float32,
        ) + lax.dot_general(
            sinks[:, value_lanes],
            sink_terms.astype(jnp.bfloat16),
            down,
            preferred_element_type=jnp.float32,
        )
        gathered = (gathered / total).astype(jnp.bfloat16)
        for h in range(group):
            att_v[first + h * HEAD_DIM : first + (h + 1) * HEAD_DIM, :] = gathered[
                :, h * tokens : (h + 1) * tokens
            ]

    def project(r, squares):
        proj_copy(r).wait()
        rows = pl.ds(pl.multiple_of(r * part, 16), part)
        state = (
            jnp.dot(proj_v[r], att_v[:, :], preferred_element_type=jnp.float32)
            + residual_t[rows, :].astype(jnp.float32)
        ).astype(jnp.bfloat16)
        hidden_ref[rows, :] = state
        state = state.astype(jnp.float32)
        return squares + jnp.sum(state * state, axis=0, keepdims=True)

    squares = lax.fori_loop(0, parts, project, jnp.zeros((1, tokens), jnp.float32))
    inverse = lax.rsqrt(squares / width + 1e-05)
    for r in range(parts):
        rows = slice(r * part, (r + 1) * part)
        rows_ref[rows, :] = (
            hidden_ref[rows, :].astype(jnp.float32) * inverse * gain[rows, :]
        ).astype(jnp.bfloat16)
    expert = lax.broadcasted_iota(jnp.int32, (experts, tokens), 0)
    weight = jnp.zeros((experts, tokens), jnp.float32)
    for k in range(TOPK):
        weight = weight + jnp.where(ids_t[k : k + 1, :] == expert, route_t[k : k + 1, :], 0.0)
    high = weight.astype(jnp.bfloat16).astype(jnp.float32)
    rows_ref[width:, :] = jnp.concatenate([high, weight - high], 0).astype(jnp.bfloat16)


def attended_rows(
    query_t, halo, local, sinks, bias, residual_t, gain, ids_t, route_t, out_proj_t, experts
):
    width, heads_width = out_proj_t.shape
    tokens = query_t.shape[1]
    part = even_rows(width, 480)
    parts = width // part
    vmem = pl.BlockSpec(memory_space=pltpu.VMEM)
    return pl.pallas_call(
        functools.partial(attention_kernel, experts),
        out_shape=(
            jax.ShapeDtypeStruct((width, tokens), jnp.bfloat16),
            jax.ShapeDtypeStruct((width + 2 * experts, tokens), jnp.bfloat16),
        ),
        in_specs=[vmem] * 9 + [pl.BlockSpec(memory_space=pl.ANY)],
        out_specs=(vmem, vmem),
        scratch_shapes=[
            pltpu.VMEM((parts, part, heads_width), jnp.bfloat16),
            pltpu.VMEM((heads_width, tokens), jnp.bfloat16),
            pltpu.SemaphoreType.DMA((parts,)),
        ],
        compiler_params=pltpu.CompilerParams(vmem_limit_bytes=VMEM_BYTES),
        cost_estimate=pl.CostEstimate(
            flops=2 * tokens * width * heads_width,
            bytes_accessed=2 * width * heads_width,
            transcendentals=tokens * Q_HEADS * bias.shape[0],
        ),
    )(query_t, halo, local, sinks, bias, residual_t, gain, ids_t, route_t, out_proj_t)


def expert_kernel(experts, me_ref, x_ref, y_ref, gu0, gu1, dn0, dn1, *refs):
    *out_refs, rows, units, gu_v, dn_v, gu_sems, dn_sems = refs
    hidden = units.shape[1]
    width = gu_v.shape[4]
    tokens = x_ref.shape[1]
    parts, part = gu_v.shape[2:4]

    def gate_up_copy(half, side, k):
        source = (gu0, gu1)[half].at[pl.ds(pl.multiple_of(side * hidden + k * part, 16), part)]
        return pltpu.make_async_copy(source, gu_v.at[half, side, k], gu_sems.at[half, side, k])

    def down_copy(half, k):
        at = pl.ds(pl.multiple_of(k * part, 16), part)
        source = (dn0, dn1)[half].at[at]
        return pltpu.make_async_copy(source, dn_v.at[half, at], dn_sems.at[half, k])

    for k in range(parts):
        gate_up_copy(0, 0, k).start()
        gate_up_copy(0, 1, k).start()
    rows[:, :tokens] = x_ref[:, :]
    rows[:, tokens:] = y_ref[:, :]

    def step(half, k):
        gate_up_copy(half, 0, k).wait()
        gate_up_copy(half, 1, k).wait()
        if half == 0:
            gate_up_copy(1, 0, k).start()
            gate_up_copy(1, 1, k).start()
            down_copy(0, k).start()
        else:
            down_copy(1, k).start()
        gate, up = (
            jnp.dot(gu_v[half, side, k], rows[:width, :], preferred_element_type=jnp.float32)
            for side in range(2)
        )
        units[half, pl.ds(pl.multiple_of(k * part, 16), part), :] = (
            gate / (1.0 + jnp.exp(-gate)) * up
        ).astype(jnp.bfloat16)

    for half in range(2):
        pl.loop(0, parts)(functools.partial(step, half))
    extra = rows[width:, :].astype(jnp.float32)
    place = lax.broadcasted_iota(jnp.int32, extra.shape, 0)
    mine = (place == me_ref[0]) | (place == experts + me_ref[0])
    weight = jnp.sum(jnp.where(mine, extra, 0.0), axis=0, keepdims=True)
    for half in range(2):
        for k in range(parts):
            down_copy(half, k).wait()
    for first in range(0, width, OUT_PART):
        at = slice(first, min(first + OUT_PART, width))
        total = (product(dn_v[0, :, at], units[0]) + product(dn_v[1, :, at], units[1])) * weight
        out_refs[0][at, :] = total[:, :tokens].astype(out_refs[0].dtype)
        out_refs[1][at, :] = total[:, tokens:].astype(out_refs[1].dtype)


def product(down, units):
    return lax.dot_general(
        down, units, (((0,), (0,)), ((), ())), preferred_element_type=jnp.float32
    )


def expert_rows(me, x, y, weights, experts, kinds):
    gu0, gu1, dn0, dn1 = weights
    tokens = x.shape[1]
    hidden, width = gu0.shape[0] // 2, gu0.shape[1]
    part = even_rows(hidden, HIDDEN_PART)
    parts = hidden // part
    vmem = pl.BlockSpec(memory_space=pltpu.VMEM)
    hbm = pl.BlockSpec(memory_space=pl.ANY)
    return pl.pallas_call(
        functools.partial(expert_kernel, experts),
        out_shape=[jax.ShapeDtypeStruct((width, tokens), kind) for kind in kinds],
        in_specs=[pl.BlockSpec(memory_space=pltpu.SMEM), vmem, vmem, hbm, hbm, hbm, hbm],
        out_specs=[vmem] * len(kinds),
        scratch_shapes=[
            pltpu.VMEM((x.shape[0], 2 * tokens), jnp.bfloat16),
            pltpu.VMEM((2, hidden, 2 * tokens), jnp.bfloat16),
            pltpu.VMEM((2, 2, parts, part, width), jnp.bfloat16),
            pltpu.VMEM((2,) + dn0.shape, jnp.bfloat16),
            pltpu.SemaphoreType.DMA((2, 2, parts)),
            pltpu.SemaphoreType.DMA((2, parts)),
        ],
        compiler_params=pltpu.CompilerParams(vmem_limit_bytes=VMEM_BYTES),
        cost_estimate=pl.CostEstimate(
            flops=2 * 2 * tokens * 2 * 3 * width * hidden,
            bytes_accessed=2 * 2 * (gu0.size + dn0.size),
            transcendentals=4 * tokens * hidden,
        ),
    )(me, x, y, gu0, gu1, dn0, dn1)


def line_pairs(moves):
    return [(PLANE * p + r, PLANE * q + r) for p, q in moves for r in range(PLANE)]


def column_pairs(planes):
    return [(PLANE * p + r, (PLANE * p + r) ^ 2) for p in range(planes) for r in range(PLANE)]


def sources(planes):
    return [
        sorted(
            (q for q in range(planes) if q != p),
            key=lambda q: (abs(q - p), -(planes - p if q > p else p)),
        )
        for p in range(planes)
    ]


def rounds(moves):
    lists = []
    for p, q in moves:
        for held in lists:
            if all(q != to for _, to in held):
                held.append((p, q))
                break
        else:
            lists.append([(p, q)])
    return lists


def next_blocks(held, distance, planes):
    up = [(p, p + 1) for p in range(distance - 1, planes - 1)]
    down = [(p, p - 1) for p in range(1, planes - distance + 1)]
    if len(held) == 1 and distance > 1:
        return [lax.ppermute(held[0], "seq", line_pairs(up + down))]
    below, above = held if len(held) == 2 else held * 2
    return [
        lax.ppermute(below, "seq", line_pairs(up)),
        lax.ppermute(above, "seq", line_pairs(down)),
    ]


def slot_block(arrivals, plane, origins):
    chosen = {}
    for p, q in enumerate(origins):
        blocks = arrivals[abs(q - p)]
        block = blocks[0] if len(blocks) == 1 or q < p else blocks[1]
        chosen.setdefault(id(block), (block, []))[1].append(p)
    (result, _), *others = chosen.values()
    for block, holders in others:
        here = functools.reduce(jnp.logical_or, [plane == p for p in holders])
        result = jnp.where(here, block, result)
    return result


def on_device(
    query_rows,
    key_rows,
    value_rows,
    sink_positions,
    residual,
    out_proj,
    norm_gain,
    expert_ids,
    route_weights,
    gate_up,
    down_proj,
):
    rows_dev = query_rows.shape[0]
    width = residual.shape[1]
    shards = lax.axis_size("seq")
    planes = shards // PLANE
    experts = shards // 2
    my_index = lax.axis_index("seq")
    plane = my_index // PLANE
    local_rows, sink_rows, bias = prepared(
        my_index.reshape(1), sink_positions, key_rows, value_rows
    )
    halo_rows = lax.ppermute(local_rows, "seq", [(i, i + 1) for i in range(shards - 1)])
    sink_rows, halo_rows, later = summed(sink_rows, "seq", halo_rows, (query_rows, norm_gain))
    query_rows, norm_gain = later

    to_core = [(i, i ^ 1) for i in range(shards)]
    gu_own = jnp.swapaxes(gate_up[0], 0, 1)
    dn_own = down_proj[0]
    gu_other = lax.ppermute(gu_own, "seq", to_core)
    dn_other = lax.ppermute(dn_own, "seq", to_core)
    weights = (gu_own, gu_other, dn_own, dn_other)

    hidden_state, own = attended_rows(
        query_rows.T,
        halo_rows,
        local_rows,
        sink_rows,
        bias,
        residual.T,
        norm_gain[:, None],
        expert_ids.T,
        route_weights.T,
        out_proj.T,
        experts,
    )

    me = (my_index // 2).reshape(1)
    across = column_pairs(planes)
    order = sources(planes)
    expert = functools.partial(expert_rows, me)
    half = jnp.bfloat16

    held = next_blocks([own], 1, planes)
    arrivals = {1: held}
    cross = lax.ppermute(own, "seq", across)
    block, ready = own, (cross, *held)
    sums = []
    for j in range(1, planes):
        nearer = [after(x, *ready) for x in arrivals[j]]
        next_block = after(slot_block(arrivals, plane, [o[j - 1] for o in order]), *ready)
        next_cross = lax.ppermute(next_block, "seq", across)
        if j + 1 < planes:
            held = next_blocks(nearer, j + 1, planes)
        else:
            held = []
        flows = []
        if j == 1:
            mine, theirs = expert(block, cross, weights, experts, (jnp.float32, jnp.float32))
            column_sum = hidden_state.astype(jnp.float32) + mine
            cross_sum = theirs
            done = mine
        elif j == 2:
            near = expert(block, cross, weights, experts, (half, half))
            done = near[0]
        else:
            if j == 3:
                flows = [(0, near[0])]
            elif j == 4:
                flows = [(1, near[1])]
            sums.append((j - 1, expert(block, cross, weights, experts, (jnp.float32, half))))
            done = sums[-1][1][1]
        backs = []
        for side, part in flows:
            part = after(part, *ready)
            for moves in rounds([(p, o[0]) for p, o in enumerate(order)]):
                backs.append((side, lax.ppermute(part, "seq", line_pairs(moves))))
        for side, back in backs:
            if side == 0:
                column_sum = column_sum + back.astype(jnp.float32)
            else:
                cross_sum = cross_sum + back.astype(jnp.float32)
        block, cross = next_block, next_cross
        ready = (next_cross, done, *held, *[back for _, back in backs])
        if held:
            held = [after(x, *ready) for x in held]
            if len(held) == 2 and 2 * (j + 1) >= planes:
                held = [jnp.where(plane >= j + 1, held[0], held[1])]
            arrivals[j + 1] = held
    last = planes - 1
    parts = expert(block, cross, weights, experts, (jnp.float32, half))
    sums.append((last, parts))
    pending = None
    for n, (j, (mine, theirs)) in enumerate(sums):
        theirs = after(theirs, *ready)
        returned = lax.ppermute(theirs, "seq", across)
        backs = []
        if n == 0 and planes <= 4:
            part = after(near[1], *ready)
            for moves in rounds([(p, o[0]) for p, o in enumerate(order)]):
                back = lax.ppermute(part, "seq", line_pairs(moves))
                cross_sum = cross_sum + back.astype(jnp.float32)
                backs.append(back)
        if pending is not None:
            k, both = pending
            for moves in rounds([(p, o[k - 1]) for p, o in enumerate(order)]):
                back = lax.ppermute(both, "seq", line_pairs(moves))
                column_sum = column_sum + back.astype(jnp.float32)
        pending = (j, (mine + returned.astype(jnp.float32)).astype(half))
        ready = (returned, *backs)
    crossing = lax.ppermute(after(cross_sum.astype(half), *ready), "seq", across)
    k, both = pending
    for moves in rounds([(p, o[k - 1]) for p, o in enumerate(order)]):
        back = lax.ppermute(both, "seq", line_pairs(moves))
        column_sum = column_sum + back.astype(jnp.float32)
    return (column_sum + crossing.astype(jnp.float32)).astype(half).T


def solution(mesh):
    in_specs = (
        P(("groups", "seq"), None),
        P(("groups", "seq"), None),
        P(("groups", "seq"), None),
        P("groups"),
        P(("groups", "seq"), None),
        P(),
        P(),
        P(("groups", "seq"), None),
        P(("groups", "seq"), None),
        P("seq", None, None),
        P("seq", None, None),
    )
    out_specs = P(("groups", "seq"), None)
    return jax.shard_map(
        on_device, mesh=mesh, in_specs=in_specs, out_specs=out_specs, check_vma=False
    )
```

```python
import functools

import jax
import jax.numpy as jnp
from jax import lax
from jax.experimental import pallas as pl
from jax.experimental.pallas import tpu as pltpu
from jax.sharding import PartitionSpec as P

Q_HEADS = 32
KV_HEADS = 4
HEAD_DIM = 64
WINDOW = 128
TOPK = 4
PLANE = 4
NEVER = -1e30
VMEM_BYTES = 56 * 1024 * 1024
HIDDEN_PART = 240
OUT_PART = 1024


def prepare_kernel(index_ref, sinks_ref, keys, values, joined_ref, picked_ref, bias_ref):
    tokens, key_width = keys.shape
    count = sinks_ref.shape[0]
    first_pos = index_ref[0] * tokens
    slot = lax.broadcasted_iota(jnp.int32, (count, tokens), 0)
    lane = lax.broadcasted_iota(jnp.int32, (count, tokens), 1)
    place = jnp.zeros((count, tokens), jnp.int32)
    seen = jnp.zeros((count, tokens), jnp.int32)
    for i in range(count):
        repeated = jnp.int32(0)
        for k in range(i):
            repeated = jnp.where(sinks_ref[i] == sinks_ref[k], jnp.int32(1), repeated)
        place = jnp.where(slot == i, sinks_ref[i], place)
        seen = jnp.where(slot == i, repeated, seen)
    pick = jnp.where(place == first_pos + lane, 1.0, 0.0).astype(jnp.bfloat16)
    for at, rows in ((slice(0, key_width), keys), (slice(key_width, None), values)):
        joined_ref[:, at] = rows[:, :]
        picked_ref[:, at] = jnp.dot(
            pick, rows[:, :], preferred_element_type=jnp.float32
        ).astype(jnp.bfloat16)
    near = bias_ref.shape[0] - count
    key_pos = first_pos - WINDOW + lax.broadcasted_iota(jnp.int32, (near, tokens), 0)
    query_pos = first_pos + lax.broadcasted_iota(jnp.int32, (near, tokens), 1)
    allowed = (key_pos >= 0) & (key_pos <= query_pos) & (key_pos > query_pos - WINDOW)
    bias_ref[:near, :] = jnp.where(allowed, 0.0, NEVER)
    allowed = (seen == 0) & (place <= first_pos + lane - WINDOW)
    bias_ref[near:, :] = jnp.where(allowed, 0.0, NEVER)


def prepared(index, sink_positions, key_rows, value_rows):
    tokens, key_width = key_rows.shape
    count = sink_positions.shape[0]
    smem, vmem = (pl.BlockSpec(memory_space=space) for space in (pltpu.SMEM, pltpu.VMEM))
    return pl.pallas_call(
        prepare_kernel,
        out_shape=(
            jax.ShapeDtypeStruct((tokens, 2 * key_width), jnp.bfloat16),
            jax.ShapeDtypeStruct((count, 2 * key_width), jnp.bfloat16),
            jax.ShapeDtypeStruct((WINDOW + tokens + count, tokens), jnp.float32),
        ),
        in_specs=[smem, smem, vmem, vmem],
        out_specs=(vmem, vmem, vmem),
    )(index, sink_positions, key_rows, value_rows)


def after(block, *earlier):
    return lax.optimization_barrier((block, earlier))[0]


def summed(block, axis, halo, later):
    shards = lax.axis_size(axis)
    step = 1
    while step < shards:
        reach = min(4, shards // step)
        parts = [
            lax.ppermute(block, axis, [(i, i ^ (step * m)) for i in range(shards)])
            for m in range(1, reach)
        ]
        for part in parts:
            block = block + part
        if step == 1:
            block, halo, later = lax.optimization_barrier((block, halo, later))
        step *= reach
    return block, halo, later


def even_rows(rows, most):
    return max(r for r in range(16, most + 1, 16) if rows % r == 0)


def attention_kernel(
    experts,
    query_t,
    halo,
    local,
    sinks,
    bias,
    residual_t,
    gain,
    ids_t,
    route_t,
    out_proj_t,
    hidden_ref,
    rows_ref,
    proj_v,
    att_v,
    sems,
):
    parts, part, heads_width = proj_v.shape
    width = parts * part
    tokens = query_t.shape[1]

    def proj_copy(r):
        at = pl.ds(pl.multiple_of(r * part, 16), part)
        return pltpu.make_async_copy(out_proj_t.at[at], proj_v.at[r], sems.at[r])

    for r in range(parts):
        proj_copy(r).start()
    group = Q_HEADS // KV_HEADS
    near = halo.shape[0] + local.shape[0]
    wide_bias = jnp.concatenate([bias[:, :]] * group, 1)
    scale = HEAD_DIM ** (-0.5)
    for g in range(KV_HEADS):
        lanes = slice(g * HEAD_DIM, (g + 1) * HEAD_DIM)
        value_lanes = slice((KV_HEADS + g) * HEAD_DIM, (KV_HEADS + g + 1) * HEAD_DIM)
        first = g * group * HEAD_DIM
        query = jnp.concatenate(
            [
                query_t[first + h * HEAD_DIM : first + (h + 1) * HEAD_DIM, :]
                for h in range(group)
            ],
            1,
        )
        near_scores = (
            jnp.dot(
                jnp.concatenate([halo[:, lanes], local[:, lanes]], 0),
                query,
                preferred_element_type=jnp.float32,
            )
            * scale
            + wide_bias[:near]
        )
        sink_scores = (
            jnp.dot(sinks[:, lanes], query, preferred_element_type=jnp.float32) * scale
            + wide_bias[near:]
        )
        largest = jnp.maximum(
            jnp.max(near_scores, axis=0, keepdims=True),
            jnp.max(sink_scores, axis=0, keepdims=True),
        )
        near_terms = jnp.exp(near_scores - largest)
        sink_terms = jnp.exp(sink_scores - largest)
        total = jnp.sum(near_terms, axis=0, keepdims=True) + jnp.sum(
            sink_terms, axis=0, keepdims=True
        )
        down = (((0,), (0,)), ((), ()))
        gathered = lax.dot_general(
            jnp.concatenate([halo[:, value_lanes], local[:, value_lanes]], 0),
            near_terms.astype(jnp.bfloat16),
            down,
            preferred_element_type=jnp.float32,
        ) + lax.dot_general(
            sinks[:, value_lanes],
            sink_terms.astype(jnp.bfloat16),
            down,
            preferred_element_type=jnp.float32,
        )
        gathered = (gathered / total).astype(jnp.bfloat16)
        for h in range(group):
            att_v[first + h * HEAD_DIM : first + (h + 1) * HEAD_DIM, :] = gathered[
                :, h * tokens : (h + 1) * tokens
            ]

    def project(r, squares):
        proj_copy(r).wait()
        rows = pl.ds(pl.multiple_of(r * part, 16), part)
        state = (
            jnp.dot(proj_v[r], att_v[:, :], preferred_element_type=jnp.float32)
            + residual_t[rows, :].astype(jnp.float32)
        ).astype(jnp.bfloat16)
        hidden_ref[rows, :] = state
        state = state.astype(jnp.float32)
        return squares + jnp.sum(state * state, axis=0, keepdims=True)

    squares = lax.fori_loop(0, parts, project, jnp.zeros((1, tokens), jnp.float32))
    inverse = lax.rsqrt(squares / width + 1e-05)
    for r in range(parts):
        rows = slice(r * part, (r + 1) * part)
        rows_ref[rows, :] = (
            hidden_ref[rows, :].astype(jnp.float32) * inverse * gain[rows, :]
        ).astype(jnp.bfloat16)
    expert = lax.broadcasted_iota(jnp.int32, (experts, tokens), 0)
    weight = jnp.zeros((experts, tokens), jnp.float32)
    for k in range(TOPK):
        weight = weight + jnp.where(ids_t[k : k + 1, :] == expert, route_t[k : k + 1, :], 0.0)
    high = weight.astype(jnp.bfloat16).astype(jnp.float32)
    rows_ref[width:, :] = jnp.concatenate([high, weight - high], 0).astype(jnp.bfloat16)


def attended_rows(
    query_t, halo, local, sinks, bias, residual_t, gain, ids_t, route_t, out_proj_t, experts
):
    width, heads_width = out_proj_t.shape
    tokens = query_t.shape[1]
    part = even_rows(width, 480)
    parts = width // part
    vmem = pl.BlockSpec(memory_space=pltpu.VMEM)
    return pl.pallas_call(
        functools.partial(attention_kernel, experts),
        out_shape=(
            jax.ShapeDtypeStruct((width, tokens), jnp.bfloat16),
            jax.ShapeDtypeStruct((width + 2 * experts, tokens), jnp.bfloat16),
        ),
        in_specs=[vmem] * 9 + [pl.BlockSpec(memory_space=pl.ANY)],
        out_specs=(vmem, vmem),
        scratch_shapes=[
            pltpu.VMEM((parts, part, heads_width), jnp.bfloat16),
            pltpu.VMEM((heads_width, tokens), jnp.bfloat16),
            pltpu.SemaphoreType.DMA((parts,)),
        ],
        compiler_params=pltpu.CompilerParams(vmem_limit_bytes=VMEM_BYTES),
        cost_estimate=pl.CostEstimate(
            flops=2 * tokens * width * heads_width,
            bytes_accessed=2 * width * heads_width,
            transcendentals=tokens * Q_HEADS * bias.shape[0],
        ),
    )(query_t, halo, local, sinks, bias, residual_t, gain, ids_t, route_t, out_proj_t)


def expert_kernel(experts, me_ref, x_ref, y_ref, gu0, gu1, dn0, dn1, *refs):
    *out_refs, rows, units, gu_v, dn_v, gu_sems, dn_sems = refs
    hidden = units.shape[1]
    width = gu_v.shape[4]
    tokens = x_ref.shape[1]
    parts, part = gu_v.shape[2:4]

    def gate_up_copy(half, side, k):
        source = (gu0, gu1)[half].at[pl.ds(pl.multiple_of(side * hidden + k * part, 16), part)]
        return pltpu.make_async_copy(source, gu_v.at[half, side, k], gu_sems.at[half, side, k])

    def down_copy(half, k):
        at = pl.ds(pl.multiple_of(k * part, 16), part)
        source = (dn0, dn1)[half].at[at]
        return pltpu.make_async_copy(source, dn_v.at[half, at], dn_sems.at[half, k])

    for k in range(parts):
        gate_up_copy(0, 0, k).start()
        gate_up_copy(0, 1, k).start()
    rows[:, :tokens] = x_ref[:, :]
    rows[:, tokens:] = y_ref[:, :]

    def step(half, k):
        gate_up_copy(half, 0, k).wait()
        gate_up_copy(half, 1, k).wait()
        if half == 0:
            gate_up_copy(1, 0, k).start()
            gate_up_copy(1, 1, k).start()
            down_copy(0, k).start()
        else:
            down_copy(1, k).start()
        gate, up = (
            jnp.dot(gu_v[half, side, k], rows[:width, :], preferred_element_type=jnp.float32)
            for side in range(2)
        )
        units[half, pl.ds(pl.multiple_of(k * part, 16), part), :] = (
            gate / (1.0 + jnp.exp(-gate)) * up
        ).astype(jnp.bfloat16)

    for half in range(2):
        pl.loop(0, parts)(functools.partial(step, half))
    extra = rows[width:, :].astype(jnp.float32)
    place = lax.broadcasted_iota(jnp.int32, extra.shape, 0)
    mine = (place == me_ref[0]) | (place == experts + me_ref[0])
    weight = jnp.sum(jnp.where(mine, extra, 0.0), axis=0, keepdims=True)
    for half in range(2):
        for k in range(parts):
            down_copy(half, k).wait()
    for first in range(0, width, OUT_PART):
        at = slice(first, min(first + OUT_PART, width))
        total = (product(dn_v[0, :, at], units[0]) + product(dn_v[1, :, at], units[1])) * weight
        out_refs[0][at, :] = total[:, :tokens].astype(out_refs[0].dtype)
        out_refs[1][at, :] = total[:, tokens:].astype(out_refs[1].dtype)


def product(down, units):
    return lax.dot_general(
        down, units, (((0,), (0,)), ((), ())), preferred_element_type=jnp.float32
    )


def expert_rows(me, x, y, weights, experts, kinds):
    gu0, gu1, dn0, dn1 = weights
    tokens = x.shape[1]
    hidden, width = gu0.shape[0] // 2, gu0.shape[1]
    part = even_rows(hidden, HIDDEN_PART)
    parts = hidden // part
    vmem = pl.BlockSpec(memory_space=pltpu.VMEM)
    hbm = pl.BlockSpec(memory_space=pl.ANY)
    return pl.pallas_call(
        functools.partial(expert_kernel, experts),
        out_shape=[jax.ShapeDtypeStruct((width, tokens), kind) for kind in kinds],
        in_specs=[pl.BlockSpec(memory_space=pltpu.SMEM), vmem, vmem, hbm, hbm, hbm, hbm],
        out_specs=[vmem] * len(kinds),
        scratch_shapes=[
            pltpu.VMEM((x.shape[0], 2 * tokens), jnp.bfloat16),
            pltpu.VMEM((2, hidden, 2 * tokens), jnp.bfloat16),
            pltpu.VMEM((2, 2, parts, part, width), jnp.bfloat16),
            pltpu.VMEM((2,) + dn0.shape, jnp.bfloat16),
            pltpu.SemaphoreType.DMA((2, 2, parts)),
            pltpu.SemaphoreType.DMA((2, parts)),
        ],
        compiler_params=pltpu.CompilerParams(vmem_limit_bytes=VMEM_BYTES),
        cost_estimate=pl.CostEstimate(
            flops=2 * 2 * tokens * 2 * 3 * width * hidden,
            bytes_accessed=2 * 2 * (gu0.size + dn0.size),
            transcendentals=4 * tokens * hidden,
        ),
    )(me, x, y, gu0, gu1, dn0, dn1)


def line_pairs(moves):
    return [(PLANE * p + r, PLANE * q + r) for p, q in moves for r in range(PLANE)]


def column_pairs(planes):
    return [(PLANE * p + r, (PLANE * p + r) ^ 2) for p in range(planes) for r in range(PLANE)]


def sources(planes):
    return [
        sorted(
            (q for q in range(planes) if q != p),
            key=lambda q: (abs(q - p), -(planes - p if q > p else p)),
        )
        for p in range(planes)
    ]


def rounds(moves):
    lists = []
    for p, q in moves:
        for held in lists:
            if all(q != to for _, to in held):
                held.append((p, q))
                break
        else:
            lists.append([(p, q)])
    return lists


def next_blocks(held, distance, planes):
    up = [(p, p + 1) for p in range(distance - 1, planes - 1)]
    down = [(p, p - 1) for p in range(1, planes - distance + 1)]
    if len(held) == 1 and distance > 1:
        return [lax.ppermute(held[0], "seq", line_pairs(up + down))]
    below, above = held if len(held) == 2 else held * 2
    return [
        lax.ppermute(below, "seq", line_pairs(up)),
        lax.ppermute(above, "seq", line_pairs(down)),
    ]


def slot_block(arrivals, plane, origins):
    chosen = {}
    for p, q in enumerate(origins):
        blocks = arrivals[abs(q - p)]
        block = blocks[0] if len(blocks) == 1 or q < p else blocks[1]
        chosen.setdefault(id(block), (block, []))[1].append(p)
    (result, _), *others = chosen.values()
    for block, holders in others:
        here = functools.reduce(jnp.logical_or, [plane == p for p in holders])
        result = jnp.where(here, block, result)
    return result


def on_device(
    query_rows,
    key_rows,
    value_rows,
    sink_positions,
    residual,
    out_proj,
    norm_gain,
    expert_ids,
    route_weights,
    gate_up,
    down_proj,
):
    rows_dev = query_rows.shape[0]
    width = residual.shape[1]
    shards = lax.axis_size("seq")
    planes = shards // PLANE
    experts = shards // 2
    my_index = lax.axis_index("seq")
    plane = my_index // PLANE
    local_rows, sink_rows, bias = prepared(
        my_index.reshape(1), sink_positions, key_rows, value_rows
    )
    halo_rows = lax.ppermute(local_rows, "seq", [(i, i + 1) for i in range(shards - 1)])
    later = (query_rows, gate_up, down_proj)
    sink_rows, halo_rows, later = summed(sink_rows, "seq", halo_rows, later)
    query_rows, gate_up, down_proj = later

    to_core = [(i, i ^ 1) for i in range(shards)]
    gu_own = jnp.swapaxes(gate_up[0], 0, 1)
    dn_own = down_proj[0]
    gu_other = lax.ppermute(gu_own, "seq", to_core)
    dn_other = lax.ppermute(dn_own, "seq", to_core)
    weights = (gu_own, gu_other, dn_own, dn_other)

    hidden_state, own = attended_rows(
        query_rows.T,
        halo_rows,
        local_rows,
        sink_rows,
        bias,
        residual.T,
        norm_gain[:, None],
        expert_ids.T,
        route_weights.T,
        out_proj.T,
        experts,
    )

    me = (my_index // 2).reshape(1)
    across = column_pairs(planes)
    order = sources(planes)
    expert = functools.partial(expert_rows, me)
    half = jnp.bfloat16

    held = next_blocks([own], 1, planes)
    arrivals = {1: held}
    cross = lax.ppermute(own, "seq", across)
    block, ready = own, (cross, *held)
    sums = []
    for j in range(1, planes):
        nearer = [after(x, *ready) for x in arrivals[j]]
        next_block = after(slot_block(arrivals, plane, [o[j - 1] for o in order]), *ready)
        next_cross = lax.ppermute(next_block, "seq", across)
        if j + 1 < planes:
            held = next_blocks(nearer, j + 1, planes)
        else:
            held = []
        flows = []
        if j == 1:
            mine, theirs = expert(block, cross, weights, experts, (jnp.float32, jnp.float32))
            column_sum = hidden_state.astype(jnp.float32) + mine
            cross_sum = theirs
            done = mine
        elif j == 2:
            near = expert(block, cross, weights, experts, (half, half))
            done = near[0]
        else:
            if j == 3:
                flows = [(0, near[0])]
            elif j == 4:
                flows = [(1, near[1])]
            sums.append((j - 1, expert(block, cross, weights, experts, (jnp.float32, half))))
            done = sums[-1][1][1]
        backs = []
        for side, part in flows:
            part = after(part, *ready)
            for moves in rounds([(p, o[0]) for p, o in enumerate(order)]):
                backs.append((side, lax.ppermute(part, "seq", line_pairs(moves))))
        for side, back in backs:
            if side == 0:
                column_sum = column_sum + back.astype(jnp.float32)
            else:
                cross_sum = cross_sum + back.astype(jnp.float32)
        block, cross = next_block, next_cross
        ready = (next_cross, done, *held, *[back for _, back in backs])
        if held:
            held = [after(x, *ready) for x in held]
            if len(held) == 2 and 2 * (j + 1) >= planes:
                held = [jnp.where(plane >= j + 1, held[0], held[1])]
            arrivals[j + 1] = held
    last = planes - 1
    parts = expert(block, cross, weights, experts, (jnp.float32, half))
    sums.append((last, parts))
    pending = None
    for n, (j, (mine, theirs)) in enumerate(sums):
        theirs = after(theirs, *ready)
        returned = lax.ppermute(theirs, "seq", across)
        backs = []
        if n == 0 and planes <= 4:
            part = after(near[1], *ready)
            for moves in rounds([(p, o[0]) for p, o in enumerate(order)]):
                back = lax.ppermute(part, "seq", line_pairs(moves))
                cross_sum = cross_sum + back.astype(jnp.float32)
                backs.append(back)
        if pending is not None:
            k, both = pending
            for moves in rounds([(p, o[k - 1]) for p, o in enumerate(order)]):
                back = lax.ppermute(both, "seq", line_pairs(moves))
                column_sum = column_sum + back.astype(jnp.float32)
        pending = (j, (mine + returned.astype(jnp.float32)).astype(half))
        ready = (returned, *backs)
    crossing = lax.ppermute(after(cross_sum.astype(half), *ready), "seq", across)
    k, both = pending
    for moves in rounds([(p, o[k - 1]) for p, o in enumerate(order)]):
        back = lax.ppermute(both, "seq", line_pairs(moves))
        column_sum = column_sum + back.astype(jnp.float32)
    return (column_sum + crossing.astype(jnp.float32)).astype(half).T


def solution(mesh):
    in_specs = (
        P(("groups", "seq"), None),
        P(("groups", "seq"), None),
        P(("groups", "seq"), None),
        P("groups"),
        P(("groups", "seq"), None),
        P(),
        P(),
        P(("groups", "seq"), None),
        P(("groups", "seq"), None),
        P("seq", None, None),
        P("seq", None, None),
    )
    out_specs = P(("groups", "seq"), None)
    return jax.shard_map(
        on_device, mesh=mesh, in_specs=in_specs, out_specs=out_specs, check_vma=False
    )
```

```python
import functools

import jax
import jax.numpy as jnp
from jax import lax
from jax.experimental import pallas as pl
from jax.experimental.pallas import tpu as pltpu
from jax.sharding import PartitionSpec as P

Q_HEADS = 32
KV_HEADS = 4
HEAD_DIM = 64
WINDOW = 128
TOPK = 4
PLANE = 4
NEVER = -1e30
VMEM_BYTES = 56 * 1024 * 1024
HIDDEN_PART = 240
OUT_PART = 1024


def prepare_kernel(index_ref, sinks_ref, keys, values, joined_ref, picked_ref, bias_ref):
    tokens, key_width = keys.shape
    count = sinks_ref.shape[0]
    first_pos = index_ref[0] * tokens
    slot = lax.broadcasted_iota(jnp.int32, (count, tokens), 0)
    lane = lax.broadcasted_iota(jnp.int32, (count, tokens), 1)
    place = jnp.zeros((count, tokens), jnp.int32)
    seen = jnp.zeros((count, tokens), jnp.int32)
    for i in range(count):
        repeated = jnp.int32(0)
        for k in range(i):
            repeated = jnp.where(sinks_ref[i] == sinks_ref[k], jnp.int32(1), repeated)
        place = jnp.where(slot == i, sinks_ref[i], place)
        seen = jnp.where(slot == i, repeated, seen)
    pick = jnp.where(place == first_pos + lane, 1.0, 0.0).astype(jnp.bfloat16)
    for at, rows in ((slice(0, key_width), keys), (slice(key_width, None), values)):
        joined_ref[:, at] = rows[:, :]
        picked_ref[:, at] = jnp.dot(
            pick, rows[:, :], preferred_element_type=jnp.float32
        ).astype(jnp.bfloat16)
    near = bias_ref.shape[0] - count
    key_pos = first_pos - WINDOW + lax.broadcasted_iota(jnp.int32, (near, tokens), 0)
    query_pos = first_pos + lax.broadcasted_iota(jnp.int32, (near, tokens), 1)
    allowed = (key_pos >= 0) & (key_pos <= query_pos) & (key_pos > query_pos - WINDOW)
    bias_ref[:near, :] = jnp.where(allowed, 0.0, NEVER)
    allowed = (seen == 0) & (place <= first_pos + lane - WINDOW)
    bias_ref[near:, :] = jnp.where(allowed, 0.0, NEVER)


def prepared(index, sink_positions, key_rows, value_rows):
    tokens, key_width = key_rows.shape
    count = sink_positions.shape[0]
    smem, vmem = (pl.BlockSpec(memory_space=space) for space in (pltpu.SMEM, pltpu.VMEM))
    return pl.pallas_call(
        prepare_kernel,
        out_shape=(
            jax.ShapeDtypeStruct((tokens, 2 * key_width), jnp.bfloat16),
            jax.ShapeDtypeStruct((count, 2 * key_width), jnp.bfloat16),
            jax.ShapeDtypeStruct((WINDOW + tokens + count, tokens), jnp.float32),
        ),
        in_specs=[smem, smem, vmem, vmem],
        out_specs=(vmem, vmem, vmem),
    )(index, sink_positions, key_rows, value_rows)


def after(block, *earlier):
    return lax.optimization_barrier((block, earlier))[0]


def summed(block, axis, halo, later):
    shards = lax.axis_size(axis)
    step = 1
    while step < shards:
        reach = min(4, shards // step)
        parts = [
            lax.ppermute(block, axis, [(i, i ^ (step * m)) for i in range(shards)])
            for m in range(1, reach)
        ]
        for part in parts:
            block = block + part
        if step == 1:
            block, halo, later = lax.optimization_barrier((block, halo, later))
        step *= reach
    return block, halo, later


def even_rows(rows, most):
    return max(r for r in range(16, most + 1, 16) if rows % r == 0)


def attention_kernel(
    experts,
    query_t,
    halo,
    local,
    sinks,
    bias,
    residual_t,
    gain,
    ids_t,
    route_t,
    out_proj_t,
    hidden_ref,
    rows_ref,
    proj_v,
    att_v,
    sems,
):
    parts, part, heads_width = proj_v.shape
    width = parts * part
    tokens = query_t.shape[1]

    def proj_copy(r):
        at = pl.ds(pl.multiple_of(r * part, 16), part)
        return pltpu.make_async_copy(out_proj_t.at[at], proj_v.at[r], sems.at[r])

    for r in range(parts):
        proj_copy(r).start()
    group = Q_HEADS // KV_HEADS
    near = halo.shape[0] + local.shape[0]
    wide_bias = jnp.concatenate([bias[:, :]] * group, 1)
    scale = HEAD_DIM ** (-0.5)
    for g in range(KV_HEADS):
        lanes = slice(g * HEAD_DIM, (g + 1) * HEAD_DIM)
        value_lanes = slice((KV_HEADS + g) * HEAD_DIM, (KV_HEADS + g + 1) * HEAD_DIM)
        first = g * group * HEAD_DIM
        query = jnp.concatenate(
            [
                query_t[first + h * HEAD_DIM : first + (h + 1) * HEAD_DIM, :]
                for h in range(group)
            ],
            1,
        )
        near_scores = (
            jnp.dot(
                jnp.concatenate([halo[:, lanes], local[:, lanes]], 0),
                query,
                preferred_element_type=jnp.float32,
            )
            * scale
            + wide_bias[:near]
        )
        sink_scores = (
            jnp.dot(sinks[:, lanes], query, preferred_element_type=jnp.float32) * scale
            + wide_bias[near:]
        )
        largest = jnp.maximum(
            jnp.max(near_scores, axis=0, keepdims=True),
            jnp.max(sink_scores, axis=0, keepdims=True),
        )
        near_terms = jnp.exp(near_scores - largest)
        sink_terms = jnp.exp(sink_scores - largest)
        total = jnp.sum(near_terms, axis=0, keepdims=True) + jnp.sum(
            sink_terms, axis=0, keepdims=True
        )
        down = (((0,), (0,)), ((), ()))
        gathered = lax.dot_general(
            jnp.concatenate([halo[:, value_lanes], local[:, value_lanes]], 0),
            near_terms.astype(jnp.bfloat16),
            down,
            preferred_element_type=jnp.float32,
        ) + lax.dot_general(
            sinks[:, value_lanes],
            sink_terms.astype(jnp.bfloat16),
            down,
            preferred_element_type=jnp.float32,
        )
        gathered = (gathered / total).astype(jnp.bfloat16)
        for h in range(group):
            att_v[first + h * HEAD_DIM : first + (h + 1) * HEAD_DIM, :] = gathered[
                :, h * tokens : (h + 1) * tokens
            ]

    def project(r, squares):
        proj_copy(r).wait()
        rows = pl.ds(pl.multiple_of(r * part, 16), part)
        state = (
            jnp.dot(proj_v[r], att_v[:, :], preferred_element_type=jnp.float32)
            + residual_t[rows, :].astype(jnp.float32)
        ).astype(jnp.bfloat16)
        hidden_ref[rows, :] = state
        state = state.astype(jnp.float32)
        return squares + jnp.sum(state * state, axis=0, keepdims=True)

    squares = lax.fori_loop(0, parts, project, jnp.zeros((1, tokens), jnp.float32))
    inverse = lax.rsqrt(squares / width + 1e-05)
    for r in range(parts):
        rows = slice(r * part, (r + 1) * part)
        rows_ref[rows, :] = (
            hidden_ref[rows, :].astype(jnp.float32) * inverse * gain[rows, :]
        ).astype(jnp.bfloat16)
    expert = lax.broadcasted_iota(jnp.int32, (experts, tokens), 0)
    weight = jnp.zeros((experts, tokens), jnp.float32)
    for k in range(TOPK):
        weight = weight + jnp.where(ids_t[k : k + 1, :] == expert, route_t[k : k + 1, :], 0.0)
    high = weight.astype(jnp.bfloat16).astype(jnp.float32)
    rows_ref[width:, :] = jnp.concatenate([high, weight - high], 0).astype(jnp.bfloat16)


def attended_rows(
    query_t, halo, local, sinks, bias, residual_t, gain, ids_t, route_t, out_proj_t, experts
):
    width, heads_width = out_proj_t.shape
    tokens = query_t.shape[1]
    part = even_rows(width, 480)
    parts = width // part
    vmem = pl.BlockSpec(memory_space=pltpu.VMEM)
    return pl.pallas_call(
        functools.partial(attention_kernel, experts),
        out_shape=(
            jax.ShapeDtypeStruct((width, tokens), jnp.bfloat16),
            jax.ShapeDtypeStruct((width + 2 * experts, tokens), jnp.bfloat16),
        ),
        in_specs=[vmem] * 9 + [pl.BlockSpec(memory_space=pl.ANY)],
        out_specs=(vmem, vmem),
        scratch_shapes=[
            pltpu.VMEM((parts, part, heads_width), jnp.bfloat16),
            pltpu.VMEM((heads_width, tokens), jnp.bfloat16),
            pltpu.SemaphoreType.DMA((parts,)),
        ],
        compiler_params=pltpu.CompilerParams(vmem_limit_bytes=VMEM_BYTES),
        cost_estimate=pl.CostEstimate(
            flops=2 * tokens * width * heads_width,
            bytes_accessed=2 * width * heads_width,
            transcendentals=tokens * Q_HEADS * bias.shape[0],
        ),
    )(query_t, halo, local, sinks, bias, residual_t, gain, ids_t, route_t, out_proj_t)


def expert_kernel(experts, me_ref, x_ref, y_ref, gu0, gu1, dn0, dn1, *refs):
    *out_refs, rows, units, gu_v, dn_v, gu_sems, dn_sems = refs
    hidden = units.shape[1]
    width = gu_v.shape[4]
    tokens = x_ref.shape[1]
    parts, part = gu_v.shape[2:4]

    def gate_up_copy(half, side, k):
        source = (gu0, gu1)[half].at[pl.ds(pl.multiple_of(side * hidden + k * part, 16), part)]
        return pltpu.make_async_copy(source, gu_v.at[half, side, k], gu_sems.at[half, side, k])

    def down_copy(half, k):
        at = pl.ds(pl.multiple_of(k * part, 16), part)
        source = (dn0, dn1)[half].at[at]
        return pltpu.make_async_copy(source, dn_v.at[half, at], dn_sems.at[half, k])

    for k in range(parts):
        gate_up_copy(0, 0, k).start()
        gate_up_copy(0, 1, k).start()
    rows[:, :tokens] = x_ref[:, :]
    rows[:, tokens:] = y_ref[:, :]

    def step(half, k):
        gate_up_copy(half, 0, k).wait()
        gate_up_copy(half, 1, k).wait()
        if half == 0:
            gate_up_copy(1, 0, k).start()
            gate_up_copy(1, 1, k).start()
            down_copy(0, k).start()
        else:
            down_copy(1, k).start()
        gate, up = (
            jnp.dot(gu_v[half, side, k], rows[:width, :], preferred_element_type=jnp.float32)
            for side in range(2)
        )
        units[half, pl.ds(pl.multiple_of(k * part, 16), part), :] = (
            gate / (1.0 + jnp.exp(-gate)) * up
        ).astype(jnp.bfloat16)

    for half in range(2):
        pl.loop(0, parts)(functools.partial(step, half))
    extra = rows[width:, :].astype(jnp.float32)
    place = lax.broadcasted_iota(jnp.int32, extra.shape, 0)
    mine = (place == me_ref[0]) | (place == experts + me_ref[0])
    weight = jnp.sum(jnp.where(mine, extra, 0.0), axis=0, keepdims=True)
    for half in range(2):
        for k in range(parts):
            down_copy(half, k).wait()
    for first in range(0, width, OUT_PART):
        at = slice(first, min(first + OUT_PART, width))
        total = (product(dn_v[0, :, at], units[0]) + product(dn_v[1, :, at], units[1])) * weight
        out_refs[0][at, :] = total[:, :tokens].astype(out_refs[0].dtype)
        out_refs[1][at, :] = total[:, tokens:].astype(out_refs[1].dtype)


def product(down, units):
    return lax.dot_general(
        down, units, (((0,), (0,)), ((), ())), preferred_element_type=jnp.float32
    )


def expert_rows(me, x, y, weights, experts, kinds):
    gu0, gu1, dn0, dn1 = weights
    tokens = x.shape[1]
    hidden, width = gu0.shape[0] // 2, gu0.shape[1]
    part = even_rows(hidden, HIDDEN_PART)
    parts = hidden // part
    vmem = pl.BlockSpec(memory_space=pltpu.VMEM)
    hbm = pl.BlockSpec(memory_space=pl.ANY)
    return pl.pallas_call(
        functools.partial(expert_kernel, experts),
        out_shape=[jax.ShapeDtypeStruct((width, tokens), kind) for kind in kinds],
        in_specs=[pl.BlockSpec(memory_space=pltpu.SMEM), vmem, vmem, hbm, hbm, hbm, hbm],
        out_specs=[vmem] * len(kinds),
        scratch_shapes=[
            pltpu.VMEM((x.shape[0], 2 * tokens), jnp.bfloat16),
            pltpu.VMEM((2, hidden, 2 * tokens), jnp.bfloat16),
            pltpu.VMEM((2, 2, parts, part, width), jnp.bfloat16),
            pltpu.VMEM((2,) + dn0.shape, jnp.bfloat16),
            pltpu.SemaphoreType.DMA((2, 2, parts)),
            pltpu.SemaphoreType.DMA((2, parts)),
        ],
        compiler_params=pltpu.CompilerParams(vmem_limit_bytes=VMEM_BYTES),
        cost_estimate=pl.CostEstimate(
            flops=2 * 2 * tokens * 2 * 3 * width * hidden,
            bytes_accessed=2 * 2 * (gu0.size + dn0.size),
            transcendentals=4 * tokens * hidden,
        ),
    )(me, x, y, gu0, gu1, dn0, dn1)


def line_pairs(moves):
    return [(PLANE * p + r, PLANE * q + r) for p, q in moves for r in range(PLANE)]


def column_pairs(planes):
    return [(PLANE * p + r, (PLANE * p + r) ^ 2) for p in range(planes) for r in range(PLANE)]


def sources(planes):
    return [
        sorted(
            (q for q in range(planes) if q != p),
            key=lambda q: (abs(q - p), -(planes - p if q > p else p)),
        )
        for p in range(planes)
    ]


def rounds(moves):
    lists = []
    for p, q in moves:
        for held in lists:
            if all(q != to for _, to in held):
                held.append((p, q))
                break
        else:
            lists.append([(p, q)])
    return lists


def next_blocks(held, distance, planes):
    up = [(p, p + 1) for p in range(distance - 1, planes - 1)]
    down = [(p, p - 1) for p in range(1, planes - distance + 1)]
    if len(held) == 1 and distance > 1:
        return [lax.ppermute(held[0], "seq", line_pairs(up + down))]
    below, above = held if len(held) == 2 else held * 2
    return [
        lax.ppermute(below, "seq", line_pairs(up)),
        lax.ppermute(above, "seq", line_pairs(down)),
    ]


def slot_block(arrivals, plane, origins):
    chosen = {}
    for p, q in enumerate(origins):
        blocks = arrivals[abs(q - p)]
        block = blocks[0] if len(blocks) == 1 or q < p else blocks[1]
        chosen.setdefault(id(block), (block, []))[1].append(p)
    (result, _), *others = chosen.values()
    for block, holders in others:
        here = functools.reduce(jnp.logical_or, [plane == p for p in holders])
        result = jnp.where(here, block, result)
    return result


def on_device(
    query_rows,
    key_rows,
    value_rows,
    sink_positions,
    residual,
    out_proj,
    norm_gain,
    expert_ids,
    route_weights,
    gate_up,
    down_proj,
):
    rows_dev = query_rows.shape[0]
    width = residual.shape[1]
    shards = lax.axis_size("seq")
    planes = shards // PLANE
    experts = shards // 2
    my_index = lax.axis_index("seq")
    plane = my_index // PLANE
    local_rows, sink_rows, bias = prepared(
        my_index.reshape(1), sink_positions, key_rows, value_rows
    )
    halo_rows = lax.ppermute(local_rows, "seq", [(i, i + 1) for i in range(shards - 1)])
    later = (query_rows, gate_up, down_proj)
    sink_rows, halo_rows, later = summed(sink_rows, "seq", halo_rows, later)
    query_rows, gate_up, down_proj = later

    to_core = [(i, i ^ 1) for i in range(shards)]
    gu_own = jnp.swapaxes(gate_up[0], 0, 1)
    dn_own = down_proj[0]
    gu_other = lax.ppermute(gu_own, "seq", to_core)
    dn_other = lax.ppermute(dn_own, "seq", to_core)
    weights = (gu_own, gu_other, dn_own, dn_other)

    hidden_state, own = attended_rows(
        query_rows.T,
        halo_rows,
        local_rows,
        sink_rows,
        bias,
        residual.T,
        norm_gain[:, None],
        expert_ids.T,
        route_weights.T,
        out_proj.T,
        experts,
    )

    me = (my_index // 2).reshape(1)
    across = column_pairs(planes)
    order = sources(planes)
    expert = functools.partial(expert_rows, me)
    half = jnp.bfloat16

    held = next_blocks([own], 1, planes)
    arrivals = {1: held}
    cross = lax.ppermute(own, "seq", across)
    block, ready = own, (cross, *held)
    sums, slow = [], []
    for j in range(1, planes):
        nearer = [after(x, *ready) for x in arrivals[j]]
        next_block = after(slot_block(arrivals, plane, [o[j - 1] for o in order]), *ready)
        next_cross = lax.ppermute(next_block, "seq", across)
        if j + 1 < planes:
            held = next_blocks(nearer, j + 1, planes)
        else:
            held = []
        flows = []
        if j == 1:
            mine, theirs = expert(block, cross, weights, experts, (jnp.float32, jnp.float32))
            column_sum = hidden_state.astype(jnp.float32) + mine
            cross_sum = theirs
            done = mine
        elif j == 2:
            near = expert(block, cross, weights, experts, (half, half))
            done = near[0]
        else:
            if j == 3:
                flows = [(0, near[0]), (1, near[1])]
            sums.append((j - 1, expert(block, cross, weights, experts, (jnp.float32, half))))
            done = sums[-1][1][1]
        backs = []
        for side, part in flows:
            part = after(part, *ready)
            for moves in rounds([(p, o[0]) for p, o in enumerate(order)]):
                backs.append((side, lax.ppermute(part, "seq", line_pairs(moves))))
        for side, back in backs:
            if side == 0:
                column_sum = column_sum + back.astype(jnp.float32)
            else:
                slow.append(back)
        block, cross = next_block, next_cross
        ready = (next_cross, done, *held, *[back for side, back in backs if side == 0])
        if held:
            held = [after(x, *ready) for x in held]
            if len(held) == 2 and 2 * (j + 1) >= planes:
                held = [jnp.where(plane >= j + 1, held[0], held[1])]
            arrivals[j + 1] = held
    last = planes - 1
    parts = expert(block, cross, weights, experts, (jnp.float32, half))
    sums.append((last, parts))
    pending = None
    for n, (j, (mine, theirs)) in enumerate(sums):
        theirs = after(theirs, *ready)
        returned = lax.ppermute(theirs, "seq", across)
        if n == 0:
            slow = [after(back, returned, parts[0]) for back in slow]
            for back in slow:
                cross_sum = cross_sum + back.astype(jnp.float32)
        if pending is not None:
            k, both = pending
            for moves in rounds([(p, o[k - 1]) for p, o in enumerate(order)]):
                back = lax.ppermute(both, "seq", line_pairs(moves))
                column_sum = column_sum + back.astype(jnp.float32)
        pending = (j, (mine + returned.astype(jnp.float32)).astype(half))
        ready = (returned, *slow)
    crossing = lax.ppermute(after(cross_sum.astype(half), *ready), "seq", across)
    k, both = pending
    for moves in rounds([(p, o[k - 1]) for p, o in enumerate(order)]):
        back = lax.ppermute(both, "seq", line_pairs(moves))
        column_sum = column_sum + back.astype(jnp.float32)
    return (column_sum + crossing.astype(jnp.float32)).astype(half).T


def solution(mesh):
    in_specs = (
        P(("groups", "seq"), None),
        P(("groups", "seq"), None),
        P(("groups", "seq"), None),
        P("groups"),
        P(("groups", "seq"), None),
        P(),
        P(),
        P(("groups", "seq"), None),
        P(("groups", "seq"), None),
        P("seq", None, None),
        P("seq", None, None),
    )
    out_specs = P(("groups", "seq"), None)
    return jax.shard_map(
        on_device, mesh=mesh, in_specs=in_specs, out_specs=out_specs, check_vma=False
    )
```

```python
import functools

import jax
import jax.numpy as jnp
from jax import lax
from jax.experimental import pallas as pl
from jax.experimental.pallas import tpu as pltpu
from jax.sharding import PartitionSpec as P

Q_HEADS = 32
KV_HEADS = 4
HEAD_DIM = 64
WINDOW = 128
TOPK = 4
PLANE = 4
NEVER = -1e30
VMEM_BYTES = 56 * 1024 * 1024
HIDDEN_PART = 240
OUT_PART = 1024


def prepare_kernel(index_ref, sinks_ref, keys, values, joined_ref, picked_ref, bias_ref):
    tokens, key_width = keys.shape
    count = sinks_ref.shape[0]
    first_pos = index_ref[0] * tokens
    slot = lax.broadcasted_iota(jnp.int32, (count, tokens), 0)
    lane = lax.broadcasted_iota(jnp.int32, (count, tokens), 1)
    place = jnp.zeros((count, tokens), jnp.int32)
    seen = jnp.zeros((count, tokens), jnp.int32)
    for i in range(count):
        repeated = jnp.int32(0)
        for k in range(i):
            repeated = jnp.where(sinks_ref[i] == sinks_ref[k], jnp.int32(1), repeated)
        place = jnp.where(slot == i, sinks_ref[i], place)
        seen = jnp.where(slot == i, repeated, seen)
    pick = jnp.where(place == first_pos + lane, 1.0, 0.0).astype(jnp.bfloat16)
    for at, rows in ((slice(0, key_width), keys), (slice(key_width, None), values)):
        joined_ref[:, at] = rows[:, :]
        picked_ref[:, at] = jnp.dot(
            pick, rows[:, :], preferred_element_type=jnp.float32
        ).astype(jnp.bfloat16)
    near = bias_ref.shape[0] - count
    key_pos = first_pos - WINDOW + lax.broadcasted_iota(jnp.int32, (near, tokens), 0)
    query_pos = first_pos + lax.broadcasted_iota(jnp.int32, (near, tokens), 1)
    allowed = (key_pos >= 0) & (key_pos <= query_pos) & (key_pos > query_pos - WINDOW)
    bias_ref[:near, :] = jnp.where(allowed, 0.0, NEVER)
    allowed = (seen == 0) & (place <= first_pos + lane - WINDOW)
    bias_ref[near:, :] = jnp.where(allowed, 0.0, NEVER)


def prepared(index, sink_positions, key_rows, value_rows):
    tokens, key_width = key_rows.shape
    count = sink_positions.shape[0]
    smem, vmem = (pl.BlockSpec(memory_space=space) for space in (pltpu.SMEM, pltpu.VMEM))
    return pl.pallas_call(
        prepare_kernel,
        out_shape=(
            jax.ShapeDtypeStruct((tokens, 2 * key_width), jnp.bfloat16),
            jax.ShapeDtypeStruct((count, 2 * key_width), jnp.bfloat16),
            jax.ShapeDtypeStruct((WINDOW + tokens + count, tokens), jnp.float32),
        ),
        in_specs=[smem, smem, vmem, vmem],
        out_specs=(vmem, vmem, vmem),
    )(index, sink_positions, key_rows, value_rows)


def after(block, *earlier):
    return lax.optimization_barrier((block, earlier))[0]


def summed(block, axis, halo, later):
    shards = lax.axis_size(axis)
    step = 1
    while step < shards:
        reach = min(4, shards // step)
        parts = [
            lax.ppermute(block, axis, [(i, i ^ (step * m)) for i in range(shards)])
            for m in range(1, reach)
        ]
        for part in parts:
            block = block + part
        if step == 1:
            block, halo, later = lax.optimization_barrier((block, halo, later))
        step *= reach
    return block, halo, later


def even_rows(rows, most):
    return max(r for r in range(16, most + 1, 16) if rows % r == 0)


def attention_kernel(
    experts,
    query_t,
    halo,
    local,
    sinks,
    bias,
    residual_t,
    gain,
    ids_t,
    route_t,
    out_proj_t,
    hidden_ref,
    rows_ref,
    proj_v,
    att_v,
    sems,
):
    parts, part, heads_width = proj_v.shape
    width = parts * part
    tokens = query_t.shape[1]

    def proj_copy(r):
        at = pl.ds(pl.multiple_of(r * part, 16), part)
        return pltpu.make_async_copy(out_proj_t.at[at], proj_v.at[r], sems.at[r])

    for r in range(parts):
        proj_copy(r).start()
    group = Q_HEADS // KV_HEADS
    near = halo.shape[0] + local.shape[0]
    wide_bias = jnp.concatenate([bias[:, :]] * group, 1)
    scale = HEAD_DIM ** (-0.5)
    for g in range(KV_HEADS):
        lanes = slice(g * HEAD_DIM, (g + 1) * HEAD_DIM)
        value_lanes = slice((KV_HEADS + g) * HEAD_DIM, (KV_HEADS + g + 1) * HEAD_DIM)
        first = g * group * HEAD_DIM
        query = jnp.concatenate(
            [
                query_t[first + h * HEAD_DIM : first + (h + 1) * HEAD_DIM, :]
                for h in range(group)
            ],
            1,
        )
        near_scores = (
            jnp.dot(
                jnp.concatenate([halo[:, lanes], local[:, lanes]], 0),
                query,
                preferred_element_type=jnp.float32,
            )
            * scale
            + wide_bias[:near]
        )
        sink_scores = (
            jnp.dot(sinks[:, lanes], query, preferred_element_type=jnp.float32) * scale
            + wide_bias[near:]
        )
        largest = jnp.maximum(
            jnp.max(near_scores, axis=0, keepdims=True),
            jnp.max(sink_scores, axis=0, keepdims=True),
        )
        near_terms = jnp.exp(near_scores - largest)
        sink_terms = jnp.exp(sink_scores - largest)
        total = jnp.sum(near_terms, axis=0, keepdims=True) + jnp.sum(
            sink_terms, axis=0, keepdims=True
        )
        down = (((0,), (0,)), ((), ()))
        gathered = lax.dot_general(
            jnp.concatenate([halo[:, value_lanes], local[:, value_lanes]], 0),
            near_terms.astype(jnp.bfloat16),
            down,
            preferred_element_type=jnp.float32,
        ) + lax.dot_general(
            sinks[:, value_lanes],
            sink_terms.astype(jnp.bfloat16),
            down,
            preferred_element_type=jnp.float32,
        )
        gathered = (gathered / total).astype(jnp.bfloat16)
        for h in range(group):
            att_v[first + h * HEAD_DIM : first + (h + 1) * HEAD_DIM, :] = gathered[
                :, h * tokens : (h + 1) * tokens
            ]

    def project(r, squares):
        proj_copy(r).wait()
        rows = pl.ds(pl.multiple_of(r * part, 16), part)
        state = (
            jnp.dot(proj_v[r], att_v[:, :], preferred_element_type=jnp.float32)
            + residual_t[rows, :].astype(jnp.float32)
        ).astype(jnp.bfloat16)
        hidden_ref[rows, :] = state
        state = state.astype(jnp.float32)
        return squares + jnp.sum(state * state, axis=0, keepdims=True)

    squares = lax.fori_loop(0, parts, project, jnp.zeros((1, tokens), jnp.float32))
    inverse = lax.rsqrt(squares / width + 1e-05)
    for r in range(parts):
        rows = slice(r * part, (r + 1) * part)
        rows_ref[rows, :] = (
            hidden_ref[rows, :].astype(jnp.float32) * inverse * gain[rows, :]
        ).astype(jnp.bfloat16)
    expert = lax.broadcasted_iota(jnp.int32, (experts, tokens), 0)
    weight = jnp.zeros((experts, tokens), jnp.float32)
    for k in range(TOPK):
        weight = weight + jnp.where(ids_t[k : k + 1, :] == expert, route_t[k : k + 1, :], 0.0)
    high = weight.astype(jnp.bfloat16).astype(jnp.float32)
    rows_ref[width:, :] = jnp.concatenate([high, weight - high], 0).astype(jnp.bfloat16)


def attended_rows(
    query_t, halo, local, sinks, bias, residual_t, gain, ids_t, route_t, out_proj_t, experts
):
    width, heads_width = out_proj_t.shape
    tokens = query_t.shape[1]
    part = even_rows(width, 480)
    parts = width // part
    vmem = pl.BlockSpec(memory_space=pltpu.VMEM)
    return pl.pallas_call(
        functools.partial(attention_kernel, experts),
        out_shape=(
            jax.ShapeDtypeStruct((width, tokens), jnp.bfloat16),
            jax.ShapeDtypeStruct((width + 2 * experts, tokens), jnp.bfloat16),
        ),
        in_specs=[vmem] * 9 + [pl.BlockSpec(memory_space=pl.ANY)],
        out_specs=(vmem, vmem),
        scratch_shapes=[
            pltpu.VMEM((parts, part, heads_width), jnp.bfloat16),
            pltpu.VMEM((heads_width, tokens), jnp.bfloat16),
            pltpu.SemaphoreType.DMA((parts,)),
        ],
        compiler_params=pltpu.CompilerParams(vmem_limit_bytes=VMEM_BYTES),
        cost_estimate=pl.CostEstimate(
            flops=2 * tokens * width * heads_width,
            bytes_accessed=2 * width * heads_width,
            transcendentals=tokens * Q_HEADS * bias.shape[0],
        ),
    )(query_t, halo, local, sinks, bias, residual_t, gain, ids_t, route_t, out_proj_t)


def expert_kernel(experts, me_ref, x_ref, y_ref, gu0, gu1, dn0, dn1, *refs):
    *out_refs, rows, units, gu_v, dn_v, gu_sems, dn_sems = refs
    hidden = units.shape[1]
    width = gu_v.shape[4]
    tokens = x_ref.shape[1]
    parts, part = gu_v.shape[2:4]

    def gate_up_copy(half, side, k):
        source = (gu0, gu1)[half].at[pl.ds(pl.multiple_of(side * hidden + k * part, 16), part)]
        return pltpu.make_async_copy(source, gu_v.at[half, side, k], gu_sems.at[half, side, k])

    def down_copy(half, k):
        at = pl.ds(pl.multiple_of(k * part, 16), part)
        source = (dn0, dn1)[half].at[at]
        return pltpu.make_async_copy(source, dn_v.at[half, at], dn_sems.at[half, k])

    for k in range(parts):
        gate_up_copy(0, 0, k).start()
        gate_up_copy(0, 1, k).start()
    rows[:, :tokens] = x_ref[:, :]
    rows[:, tokens:] = y_ref[:, :]

    def step(half, k):
        gate_up_copy(half, 0, k).wait()
        gate_up_copy(half, 1, k).wait()
        if half == 0:
            gate_up_copy(1, 0, k).start()
            gate_up_copy(1, 1, k).start()
            down_copy(0, k).start()
        else:
            down_copy(1, k).start()
        gate, up = (
            jnp.dot(gu_v[half, side, k], rows[:width, :], preferred_element_type=jnp.float32)
            for side in range(2)
        )
        units[half, pl.ds(pl.multiple_of(k * part, 16), part), :] = (
            gate / (1.0 + jnp.exp(-gate)) * up
        ).astype(jnp.bfloat16)

    for half in range(2):
        pl.loop(0, parts)(functools.partial(step, half))
    extra = rows[width:, :].astype(jnp.float32)
    place = lax.broadcasted_iota(jnp.int32, extra.shape, 0)
    mine = (place == me_ref[0]) | (place == experts + me_ref[0])
    weight = jnp.sum(jnp.where(mine, extra, 0.0), axis=0, keepdims=True)
    for half in range(2):
        for k in range(parts):
            down_copy(half, k).wait()
    for first in range(0, width, OUT_PART):
        at = slice(first, min(first + OUT_PART, width))
        total = (product(dn_v[0, :, at], units[0]) + product(dn_v[1, :, at], units[1])) * weight
        out_refs[0][at, :] = total[:, :tokens].astype(out_refs[0].dtype)
        out_refs[1][at, :] = total[:, tokens:].astype(out_refs[1].dtype)


def product(down, units):
    return lax.dot_general(
        down, units, (((0,), (0,)), ((), ())), preferred_element_type=jnp.float32
    )


def expert_rows(me, x, y, weights, experts, kinds):
    gu0, gu1, dn0, dn1 = weights
    tokens = x.shape[1]
    hidden, width = gu0.shape[0] // 2, gu0.shape[1]
    part = even_rows(hidden, HIDDEN_PART)
    parts = hidden // part
    vmem = pl.BlockSpec(memory_space=pltpu.VMEM)
    hbm = pl.BlockSpec(memory_space=pl.ANY)
    return pl.pallas_call(
        functools.partial(expert_kernel, experts),
        out_shape=[jax.ShapeDtypeStruct((width, tokens), kind) for kind in kinds],
        in_specs=[pl.BlockSpec(memory_space=pltpu.SMEM), vmem, vmem, hbm, hbm, hbm, hbm],
        out_specs=[vmem] * len(kinds),
        scratch_shapes=[
            pltpu.VMEM((x.shape[0], 2 * tokens), jnp.bfloat16),
            pltpu.VMEM((2, hidden, 2 * tokens), jnp.bfloat16),
            pltpu.VMEM((2, 2, parts, part, width), jnp.bfloat16),
            pltpu.VMEM((2,) + dn0.shape, jnp.bfloat16),
            pltpu.SemaphoreType.DMA((2, 2, parts)),
            pltpu.SemaphoreType.DMA((2, parts)),
        ],
        compiler_params=pltpu.CompilerParams(vmem_limit_bytes=VMEM_BYTES),
        cost_estimate=pl.CostEstimate(
            flops=2 * 2 * tokens * 2 * 3 * width * hidden,
            bytes_accessed=2 * 2 * (gu0.size + dn0.size),
            transcendentals=4 * tokens * hidden,
        ),
    )(me, x, y, gu0, gu1, dn0, dn1)


def line_pairs(moves):
    return [(PLANE * p + r, PLANE * q + r) for p, q in moves for r in range(PLANE)]


def column_pairs(planes):
    return [(PLANE * p + r, (PLANE * p + r) ^ 2) for p in range(planes) for r in range(PLANE)]


def sources(planes):
    return [
        sorted(
            (q for q in range(planes) if q != p),
            key=lambda q: (abs(q - p), -(planes - p if q > p else p)),
        )
        for p in range(planes)
    ]


def rounds(moves):
    lists = []
    for p, q in moves:
        for held in lists:
            if all(q != to for _, to in held):
                held.append((p, q))
                break
        else:
            lists.append([(p, q)])
    return lists


def next_blocks(held, distance, planes):
    up = [(p, p + 1) for p in range(distance - 1, planes - 1)]
    down = [(p, p - 1) for p in range(1, planes - distance + 1)]
    if len(held) == 1 and distance > 1:
        return [lax.ppermute(held[0], "seq", line_pairs(up + down))]
    below, above = held if len(held) == 2 else held * 2
    return [
        lax.ppermute(below, "seq", line_pairs(up)),
        lax.ppermute(above, "seq", line_pairs(down)),
    ]


def slot_block(arrivals, plane, origins):
    chosen = {}
    for p, q in enumerate(origins):
        blocks = arrivals[abs(q - p)]
        block = blocks[0] if len(blocks) == 1 or q < p else blocks[1]
        chosen.setdefault(id(block), (block, []))[1].append(p)
    (result, _), *others = chosen.values()
    for block, holders in others:
        here = functools.reduce(jnp.logical_or, [plane == p for p in holders])
        result = jnp.where(here, block, result)
    return result


def on_device(
    query_rows,
    key_rows,
    value_rows,
    sink_positions,
    residual,
    out_proj,
    norm_gain,
    expert_ids,
    route_weights,
    gate_up,
    down_proj,
):
    rows_dev = query_rows.shape[0]
    width = residual.shape[1]
    shards = lax.axis_size("seq")
    planes = shards // PLANE
    experts = shards // 2
    my_index = lax.axis_index("seq")
    plane = my_index // PLANE
    local_rows, sink_rows, bias = prepared(
        my_index.reshape(1), sink_positions, key_rows, value_rows
    )
    halo_rows = lax.ppermute(local_rows, "seq", [(i, i + 1) for i in range(shards - 1)])
    sink_rows, halo_rows, query_rows = summed(sink_rows, "seq", halo_rows, query_rows)
    query_t = query_rows.T
    gain = jnp.broadcast_to(norm_gain[:, None], (width, rows_dev))
    gate_up, down_proj, query_t, gain, sink_rows = lax.optimization_barrier(
        (gate_up, down_proj, query_t, gain, sink_rows)
    )

    to_core = [(i, i ^ 1) for i in range(shards)]
    gu_own = jnp.swapaxes(gate_up[0], 0, 1)
    dn_own = down_proj[0]
    gu_other = lax.ppermute(gu_own, "seq", to_core)
    dn_other = lax.ppermute(dn_own, "seq", to_core)
    weights = (gu_own, gu_other, dn_own, dn_other)

    hidden_state, own = attended_rows(
        query_t,
        halo_rows,
        local_rows,
        sink_rows,
        bias,
        residual.T,
        gain,
        expert_ids.T,
        route_weights.T,
        out_proj.T,
        experts,
    )

    me = (my_index // 2).reshape(1)
    across = column_pairs(planes)
    order = sources(planes)
    expert = functools.partial(expert_rows, me)
    half = jnp.bfloat16

    held = next_blocks([own], 1, planes)
    arrivals = {1: held}
    cross = lax.ppermute(own, "seq", across)
    block, ready = own, (cross, *held)
    sums, slow = [], []
    for j in range(1, planes):
        nearer = [after(x, *ready) for x in arrivals[j]]
        next_block = after(slot_block(arrivals, plane, [o[j - 1] for o in order]), *ready)
        next_cross = lax.ppermute(next_block, "seq", across)
        if j + 1 < planes:
            held = next_blocks(nearer, j + 1, planes)
        else:
            held = []
        flows = []
        if j == 1:
            mine, theirs = expert(block, cross, weights, experts, (jnp.float32, jnp.float32))
            column_sum = hidden_state.astype(jnp.float32) + mine
            cross_sum = theirs
            done = mine
        elif j == 2:
            near = expert(block, cross, weights, experts, (half, half))
            done = near[0]
        else:
            if j == 3:
                flows = [(0, near[0]), (1, near[1])]
            sums.append((j - 1, expert(block, cross, weights, experts, (jnp.float32, half))))
            done = sums[-1][1][1]
        backs = []
        for side, part in flows:
            part = after(part, *ready)
            for moves in rounds([(p, o[0]) for p, o in enumerate(order)]):
                backs.append((side, lax.ppermute(part, "seq", line_pairs(moves))))
        for side, back in backs:
            if side == 0:
                column_sum = column_sum + back.astype(jnp.float32)
            else:
                slow.append(back)
        block, cross = next_block, next_cross
        ready = (next_cross, done, *held, *[back for side, back in backs if side == 0])
        if held:
            held = [after(x, *ready) for x in held]
            if len(held) == 2 and 2 * (j + 1) >= planes:
                held = [jnp.where(plane >= j + 1, held[0], held[1])]
            arrivals[j + 1] = held
    last = planes - 1
    parts = expert(block, cross, weights, experts, (jnp.float32, half))
    sums.append((last, parts))
    pending = None
    for n, (j, (mine, theirs)) in enumerate(sums):
        theirs = after(theirs, *ready)
        returned = lax.ppermute(theirs, "seq", across)
        if n == 0:
            slow = [after(back, returned, parts[0]) for back in slow]
            for back in slow:
                cross_sum = cross_sum + back.astype(jnp.float32)
        if pending is not None:
            k, both = pending
            for moves in rounds([(p, o[k - 1]) for p, o in enumerate(order)]):
                back = lax.ppermute(both, "seq", line_pairs(moves))
                column_sum = column_sum + back.astype(jnp.float32)
        pending = (j, (mine + returned.astype(jnp.float32)).astype(half))
        ready = (returned, *slow)
    crossing = lax.ppermute(after(cross_sum.astype(half), *ready), "seq", across)
    k, both = pending
    for moves in rounds([(p, o[k - 1]) for p, o in enumerate(order)]):
        back = lax.ppermute(both, "seq", line_pairs(moves))
        column_sum = column_sum + back.astype(jnp.float32)
    return (column_sum + crossing.astype(jnp.float32)).astype(half).T


def solution(mesh):
    in_specs = (
        P(("groups", "seq"), None),
        P(("groups", "seq"), None),
        P(("groups", "seq"), None),
        P("groups"),
        P(("groups", "seq"), None),
        P(),
        P(),
        P(("groups", "seq"), None),
        P(("groups", "seq"), None),
        P("seq", None, None),
        P("seq", None, None),
    )
    out_specs = P(("groups", "seq"), None)
    return jax.shard_map(
        on_device, mesh=mesh, in_specs=in_specs, out_specs=out_specs, check_vma=False
    )
```

```python
import functools

import jax
import jax.numpy as jnp
from jax import lax
from jax.experimental import pallas as pl
from jax.experimental.pallas import tpu as pltpu
from jax.sharding import PartitionSpec as P

Q_HEADS = 32
KV_HEADS = 4
HEAD_DIM = 64
WINDOW = 128
TOPK = 4
PLANE = 4
NEVER = -1e30
VMEM_BYTES = 56 * 1024 * 1024
HIDDEN_PART = 240
OUT_PART = 1024


def prepare_kernel(index_ref, sinks_ref, keys, values, joined_ref, picked_ref, bias_ref):
    tokens, key_width = keys.shape
    count = sinks_ref.shape[0]
    first_pos = index_ref[0] * tokens
    slot = lax.broadcasted_iota(jnp.int32, (count, tokens), 0)
    lane = lax.broadcasted_iota(jnp.int32, (count, tokens), 1)
    place = jnp.zeros((count, tokens), jnp.int32)
    seen = jnp.zeros((count, tokens), jnp.int32)
    for i in range(count):
        repeated = jnp.int32(0)
        for k in range(i):
            repeated = jnp.where(sinks_ref[i] == sinks_ref[k], jnp.int32(1), repeated)
        place = jnp.where(slot == i, sinks_ref[i], place)
        seen = jnp.where(slot == i, repeated, seen)
    pick = jnp.where(place == first_pos + lane, 1.0, 0.0).astype(jnp.bfloat16)
    for at, rows in ((slice(0, key_width), keys), (slice(key_width, None), values)):
        joined_ref[:, at] = rows[:, :]
        picked_ref[:, at] = jnp.dot(
            pick, rows[:, :], preferred_element_type=jnp.float32
        ).astype(jnp.bfloat16)
    near = bias_ref.shape[0] - count
    key_pos = first_pos - WINDOW + lax.broadcasted_iota(jnp.int32, (near, tokens), 0)
    query_pos = first_pos + lax.broadcasted_iota(jnp.int32, (near, tokens), 1)
    allowed = (key_pos >= 0) & (key_pos <= query_pos) & (key_pos > query_pos - WINDOW)
    bias_ref[:near, :] = jnp.where(allowed, 0.0, NEVER)
    allowed = (seen == 0) & (place <= first_pos + lane - WINDOW)
    bias_ref[near:, :] = jnp.where(allowed, 0.0, NEVER)


def prepared(index, sink_positions, key_rows, value_rows):
    tokens, key_width = key_rows.shape
    count = sink_positions.shape[0]
    smem, vmem = (pl.BlockSpec(memory_space=space) for space in (pltpu.SMEM, pltpu.VMEM))
    return pl.pallas_call(
        prepare_kernel,
        out_shape=(
            jax.ShapeDtypeStruct((tokens, 2 * key_width), jnp.bfloat16),
            jax.ShapeDtypeStruct((count, 2 * key_width), jnp.bfloat16),
            jax.ShapeDtypeStruct((WINDOW + tokens + count, tokens), jnp.float32),
        ),
        in_specs=[smem, smem, vmem, vmem],
        out_specs=(vmem, vmem, vmem),
    )(index, sink_positions, key_rows, value_rows)


def after(block, *earlier):
    return lax.optimization_barrier((block, earlier))[0]


def summed(block, axis, halo, later):
    shards = lax.axis_size(axis)
    step = 1
    while step < shards:
        reach = min(4, shards // step)
        parts = [
            lax.ppermute(block, axis, [(i, i ^ (step * m)) for i in range(shards)])
            for m in range(1, reach)
        ]
        for part in parts:
            block = block + part
        if step == 1:
            block, halo, later = lax.optimization_barrier((block, halo, later))
        step *= reach
    return block, halo, later


def even_rows(rows, most):
    return max(r for r in range(16, most + 1, 16) if rows % r == 0)


def attention_kernel(
    experts,
    query_t,
    halo,
    local,
    sinks,
    bias,
    residual_t,
    gain,
    ids_t,
    route_t,
    out_proj_t,
    hidden_ref,
    rows_ref,
    proj_v,
    att_v,
    sems,
):
    parts, part, heads_width = proj_v.shape
    width = parts * part
    tokens = query_t.shape[1]

    def proj_copy(r):
        at = pl.ds(pl.multiple_of(r * part, 16), part)
        return pltpu.make_async_copy(out_proj_t.at[at], proj_v.at[r], sems.at[r])

    for r in range(parts):
        proj_copy(r).start()
    group = Q_HEADS // KV_HEADS
    near = halo.shape[0] + local.shape[0]
    wide_bias = jnp.concatenate([bias[:, :]] * group, 1)
    scale = HEAD_DIM ** (-0.5)
    for g in range(KV_HEADS):
        lanes = slice(g * HEAD_DIM, (g + 1) * HEAD_DIM)
        value_lanes = slice((KV_HEADS + g) * HEAD_DIM, (KV_HEADS + g + 1) * HEAD_DIM)
        first = g * group * HEAD_DIM
        query = jnp.concatenate(
            [
                query_t[first + h * HEAD_DIM : first + (h + 1) * HEAD_DIM, :]
                for h in range(group)
            ],
            1,
        )
        near_scores = (
            jnp.dot(
                jnp.concatenate([halo[:, lanes], local[:, lanes]], 0),
                query,
                preferred_element_type=jnp.float32,
            )
            * scale
            + wide_bias[:near]
        )
        sink_scores = (
            jnp.dot(sinks[:, lanes], query, preferred_element_type=jnp.float32) * scale
            + wide_bias[near:]
        )
        largest = jnp.maximum(
            jnp.max(near_scores, axis=0, keepdims=True),
            jnp.max(sink_scores, axis=0, keepdims=True),
        )
        near_terms = jnp.exp(near_scores - largest)
        sink_terms = jnp.exp(sink_scores - largest)
        total = jnp.sum(near_terms, axis=0, keepdims=True) + jnp.sum(
            sink_terms, axis=0, keepdims=True
        )
        down = (((0,), (0,)), ((), ()))
        gathered = lax.dot_general(
            jnp.concatenate([halo[:, value_lanes], local[:, value_lanes]], 0),
            near_terms.astype(jnp.bfloat16),
            down,
            preferred_element_type=jnp.float32,
        ) + lax.dot_general(
            sinks[:, value_lanes],
            sink_terms.astype(jnp.bfloat16),
            down,
            preferred_element_type=jnp.float32,
        )
        gathered = (gathered / total).astype(jnp.bfloat16)
        for h in range(group):
            att_v[first + h * HEAD_DIM : first + (h + 1) * HEAD_DIM, :] = gathered[
                :, h * tokens : (h + 1) * tokens
            ]

    def project(r, squares):
        proj_copy(r).wait()
        rows = pl.ds(pl.multiple_of(r * part, 16), part)
        state = (
            jnp.dot(proj_v[r], att_v[:, :], preferred_element_type=jnp.float32)
            + residual_t[rows, :].astype(jnp.float32)
        ).astype(jnp.bfloat16)
        hidden_ref[rows, :] = state
        state = state.astype(jnp.float32)
        return squares + jnp.sum(state * state, axis=0, keepdims=True)

    squares = lax.fori_loop(0, parts, project, jnp.zeros((1, tokens), jnp.float32))
    inverse = lax.rsqrt(squares / width + 1e-05)
    for r in range(parts):
        rows = slice(r * part, (r + 1) * part)
        rows_ref[rows, :] = (
            hidden_ref[rows, :].astype(jnp.float32) * inverse * gain[rows, :]
        ).astype(jnp.bfloat16)
    expert = lax.broadcasted_iota(jnp.int32, (experts, tokens), 0)
    weight = jnp.zeros((experts, tokens), jnp.float32)
    for k in range(TOPK):
        weight = weight + jnp.where(ids_t[k : k + 1, :] == expert, route_t[k : k + 1, :], 0.0)
    high = weight.astype(jnp.bfloat16).astype(jnp.float32)
    rows_ref[width:, :] = jnp.concatenate([high, weight - high], 0).astype(jnp.bfloat16)


def attended_rows(
    query_t, halo, local, sinks, bias, residual_t, gain, ids_t, route_t, out_proj_t, experts
):
    width, heads_width = out_proj_t.shape
    tokens = query_t.shape[1]
    part = even_rows(width, 480)
    parts = width // part
    vmem = pl.BlockSpec(memory_space=pltpu.VMEM)
    return pl.pallas_call(
        functools.partial(attention_kernel, experts),
        out_shape=(
            jax.ShapeDtypeStruct((width, tokens), jnp.bfloat16),
            jax.ShapeDtypeStruct((width + 2 * experts, tokens), jnp.bfloat16),
        ),
        in_specs=[vmem] * 9 + [pl.BlockSpec(memory_space=pl.ANY)],
        out_specs=(vmem, vmem),
        scratch_shapes=[
            pltpu.VMEM((parts, part, heads_width), jnp.bfloat16),
            pltpu.VMEM((heads_width, tokens), jnp.bfloat16),
            pltpu.SemaphoreType.DMA((parts,)),
        ],
        compiler_params=pltpu.CompilerParams(vmem_limit_bytes=VMEM_BYTES),
        cost_estimate=pl.CostEstimate(
            flops=2 * tokens * width * heads_width,
            bytes_accessed=2 * width * heads_width,
            transcendentals=tokens * Q_HEADS * bias.shape[0],
        ),
    )(query_t, halo, local, sinks, bias, residual_t, gain, ids_t, route_t, out_proj_t)


def expert_kernel(experts, me_ref, x_ref, y_ref, gu0, gu1, dn0, dn1, *refs):
    *out_refs, rows, units, gu_v, dn_v, gu_sems, dn_sems = refs
    hidden = units.shape[1]
    width = gu_v.shape[4]
    tokens = x_ref.shape[1]
    parts, part = gu_v.shape[2:4]

    def gate_up_copy(half, side, k):
        source = (gu0, gu1)[half].at[pl.ds(pl.multiple_of(side * hidden + k * part, 16), part)]
        return pltpu.make_async_copy(source, gu_v.at[half, side, k], gu_sems.at[half, side, k])

    def down_copy(half, k):
        at = pl.ds(pl.multiple_of(k * part, 16), part)
        source = (dn0, dn1)[half].at[at]
        return pltpu.make_async_copy(source, dn_v.at[half, at], dn_sems.at[half, k])

    for k in range(parts):
        gate_up_copy(0, 0, k).start()
        gate_up_copy(0, 1, k).start()
    rows[:, :tokens] = x_ref[:, :]
    rows[:, tokens:] = y_ref[:, :]

    def step(half, k):
        gate_up_copy(half, 0, k).wait()
        gate_up_copy(half, 1, k).wait()
        if half == 0:
            gate_up_copy(1, 0, k).start()
            gate_up_copy(1, 1, k).start()
            down_copy(0, k).start()
        else:
            down_copy(1, k).start()
        gate, up = (
            jnp.dot(gu_v[half, side, k], rows[:width, :], preferred_element_type=jnp.float32)
            for side in range(2)
        )
        units[half, pl.ds(pl.multiple_of(k * part, 16), part), :] = (
            gate / (1.0 + jnp.exp(-gate)) * up
        ).astype(jnp.bfloat16)

    for half in range(2):
        pl.loop(0, parts)(functools.partial(step, half))
    extra = rows[width:, :].astype(jnp.float32)
    place = lax.broadcasted_iota(jnp.int32, extra.shape, 0)
    mine = (place == me_ref[0]) | (place == experts + me_ref[0])
    weight = jnp.sum(jnp.where(mine, extra, 0.0), axis=0, keepdims=True)
    for half in range(2):
        for k in range(parts):
            down_copy(half, k).wait()
    for first in range(0, width, OUT_PART):
        at = slice(first, min(first + OUT_PART, width))
        total = (product(dn_v[0, :, at], units[0]) + product(dn_v[1, :, at], units[1])) * weight
        out_refs[0][at, :] = total[:, :tokens].astype(out_refs[0].dtype)
        out_refs[1][at, :] = total[:, tokens:].astype(out_refs[1].dtype)


def product(down, units):
    return lax.dot_general(
        down, units, (((0,), (0,)), ((), ())), preferred_element_type=jnp.float32
    )


def expert_rows(me, x, y, weights, experts, kinds):
    gu0, gu1, dn0, dn1 = weights
    tokens = x.shape[1]
    hidden, width = gu0.shape[0] // 2, gu0.shape[1]
    part = even_rows(hidden, HIDDEN_PART)
    parts = hidden // part
    vmem = pl.BlockSpec(memory_space=pltpu.VMEM)
    hbm = pl.BlockSpec(memory_space=pl.ANY)
    return pl.pallas_call(
        functools.partial(expert_kernel, experts),
        out_shape=[jax.ShapeDtypeStruct((width, tokens), kind) for kind in kinds],
        in_specs=[pl.BlockSpec(memory_space=pltpu.SMEM), vmem, vmem, hbm, hbm, hbm, hbm],
        out_specs=[vmem] * len(kinds),
        scratch_shapes=[
            pltpu.VMEM((x.shape[0], 2 * tokens), jnp.bfloat16),
            pltpu.VMEM((2, hidden, 2 * tokens), jnp.bfloat16),
            pltpu.VMEM((2, 2, parts, part, width), jnp.bfloat16),
            pltpu.VMEM((2,) + dn0.shape, jnp.bfloat16),
            pltpu.SemaphoreType.DMA((2, 2, parts)),
            pltpu.SemaphoreType.DMA((2, parts)),
        ],
        compiler_params=pltpu.CompilerParams(vmem_limit_bytes=VMEM_BYTES),
        cost_estimate=pl.CostEstimate(
            flops=2 * 2 * tokens * 2 * 3 * width * hidden,
            bytes_accessed=2 * 2 * (gu0.size + dn0.size),
            transcendentals=4 * tokens * hidden,
        ),
    )(me, x, y, gu0, gu1, dn0, dn1)


def line_pairs(moves):
    return [(PLANE * p + r, PLANE * q + r) for p, q in moves for r in range(PLANE)]


def column_pairs(planes):
    return [(PLANE * p + r, (PLANE * p + r) ^ 2) for p in range(planes) for r in range(PLANE)]


def sources(planes):
    return [
        sorted(
            (q for q in range(planes) if q != p),
            key=lambda q: (abs(q - p), -(planes - p if q > p else p)),
        )
        for p in range(planes)
    ]


def rounds(moves):
    lists = []
    for p, q in moves:
        for held in lists:
            if all(q != to for _, to in held):
                held.append((p, q))
                break
        else:
            lists.append([(p, q)])
    return lists


def next_blocks(held, distance, planes):
    up = [(p, p + 1) for p in range(distance - 1, planes - 1)]
    down = [(p, p - 1) for p in range(1, planes - distance + 1)]
    if len(held) == 1 and distance > 1:
        return [lax.ppermute(held[0], "seq", line_pairs(up + down))]
    below, above = held if len(held) == 2 else held * 2
    return [
        lax.ppermute(below, "seq", line_pairs(up)),
        lax.ppermute(above, "seq", line_pairs(down)),
    ]


def slot_block(arrivals, plane, origins):
    chosen = {}
    for p, q in enumerate(origins):
        blocks = arrivals[abs(q - p)]
        block = blocks[0] if len(blocks) == 1 or q < p else blocks[1]
        chosen.setdefault(id(block), (block, []))[1].append(p)
    (result, _), *others = chosen.values()
    for block, holders in others:
        here = functools.reduce(jnp.logical_or, [plane == p for p in holders])
        result = jnp.where(here, block, result)
    return result


def on_device(
    query_rows,
    key_rows,
    value_rows,
    sink_positions,
    residual,
    out_proj,
    norm_gain,
    expert_ids,
    route_weights,
    gate_up,
    down_proj,
):
    rows_dev = query_rows.shape[0]
    width = residual.shape[1]
    shards = lax.axis_size("seq")
    planes = shards // PLANE
    experts = shards // 2
    my_index = lax.axis_index("seq")
    plane = my_index // PLANE
    local_rows, sink_rows, bias = prepared(
        my_index.reshape(1), sink_positions, key_rows, value_rows
    )
    halo_rows = lax.ppermute(local_rows, "seq", [(i, i + 1) for i in range(shards - 1)])
    later = (query_rows, gate_up, down_proj)
    sink_rows, halo_rows, later = summed(sink_rows, "seq", halo_rows, later)
    query_rows, gate_up, down_proj = later

    to_core = [(i, i ^ 1) for i in range(shards)]
    gu_own = jnp.swapaxes(gate_up[0], 0, 1)
    dn_own = down_proj[0]
    gu_other = lax.ppermute(gu_own, "seq", to_core)
    dn_other = lax.ppermute(dn_own, "seq", to_core)
    weights = (gu_own, gu_other, dn_own, dn_other)

    hidden_state, own = attended_rows(
        query_rows.T,
        halo_rows,
        local_rows,
        sink_rows,
        bias,
        residual.T,
        norm_gain[:, None],
        expert_ids.T,
        route_weights.T,
        out_proj.T,
        experts,
    )

    me = (my_index // 2).reshape(1)
    across = column_pairs(planes)
    order = sources(planes)
    expert = functools.partial(expert_rows, me)
    half = jnp.bfloat16

    held = next_blocks([own], 1, planes)
    arrivals = {1: held}
    cross = lax.ppermute(own, "seq", across)
    block, ready = own, (cross, *held)
    sums, slow = [], []
    for j in range(1, planes):
        nearer = [after(x, *ready) for x in arrivals[j]]
        next_block = after(slot_block(arrivals, plane, [o[j - 1] for o in order]), *ready)
        next_cross = lax.ppermute(next_block, "seq", across)
        if j + 1 < planes:
            held = next_blocks(nearer, j + 1, planes)
        else:
            held = []
        flows = []
        if j == 1:
            mine, theirs = expert(block, cross, weights, experts, (jnp.float32, jnp.float32))
            column_sum = hidden_state.astype(jnp.float32) + mine
            cross_sum = theirs
            done = mine
        elif j == 2:
            near = expert(block, cross, weights, experts, (half, half))
            done = near[0]
        else:
            if j == 3:
                flows = [(0, near[0]), (1, near[1])]
            sums.append((j - 1, expert(block, cross, weights, experts, (jnp.float32, half))))
            done = sums[-1][1][1]
        backs = []
        for side, part in flows:
            part = after(part, *ready)
            for moves in rounds([(p, o[0]) for p, o in enumerate(order)]):
                backs.append((side, lax.ppermute(part, "seq", line_pairs(moves))))
        for side, back in backs:
            if side == 0:
                column_sum = column_sum + back.astype(jnp.float32)
            else:
                slow.append(back)
        block, cross = next_block, next_cross
        ready = (next_cross, done, *held, *[back for side, back in backs if side == 0])
        if held:
            held = [after(x, *ready) for x in held]
            if len(held) == 2 and 2 * (j + 1) >= planes:
                held = [jnp.where(plane >= j + 1, held[0], held[1])]
            arrivals[j + 1] = held
    last = planes - 1
    parts = expert(block, cross, weights, experts, (jnp.float32, half))
    sums.append((last, parts))
    pending = None
    for n, (j, (mine, theirs)) in enumerate(sums):
        theirs = after(theirs, *ready)
        returned = lax.ppermute(theirs, "seq", across)
        if n == 0:
            slow = [after(back, parts[0]) for back in slow]
            for back in slow:
                cross_sum = cross_sum + back.astype(jnp.float32)
        if pending is not None:
            k, both = pending
            for moves in rounds([(p, o[k - 1]) for p, o in enumerate(order)]):
                back = lax.ppermute(both, "seq", line_pairs(moves))
                column_sum = column_sum + back.astype(jnp.float32)
        pending = (j, (mine + returned.astype(jnp.float32)).astype(half))
        ready = (returned, *slow)
    crossing = lax.ppermute(after(cross_sum.astype(half), *ready), "seq", across)
    k, both = pending
    for moves in rounds([(p, o[k - 1]) for p, o in enumerate(order)]):
        back = lax.ppermute(both, "seq", line_pairs(moves))
        column_sum = column_sum + back.astype(jnp.float32)
    return (column_sum + crossing.astype(jnp.float32)).astype(half).T


def solution(mesh):
    in_specs = (
        P(("groups", "seq"), None),
        P(("groups", "seq"), None),
        P(("groups", "seq"), None),
        P("groups"),
        P(("groups", "seq"), None),
        P(),
        P(),
        P(("groups", "seq"), None),
        P(("groups", "seq"), None),
        P("seq", None, None),
        P("seq", None, None),
    )
    out_specs = P(("groups", "seq"), None)
    return jax.shard_map(
        on_device, mesh=mesh, in_specs=in_specs, out_specs=out_specs, check_vma=False
    )
```

```python
import functools

import jax
import jax.numpy as jnp
from jax import lax
from jax.experimental import pallas as pl
from jax.experimental.pallas import tpu as pltpu
from jax.sharding import PartitionSpec as P

Q_HEADS = 32
KV_HEADS = 4
HEAD_DIM = 64
WINDOW = 128
TOPK = 4
PLANE = 4
NEVER = -1e30
VMEM_BYTES = 56 * 1024 * 1024
HIDDEN_PART = 240
OUT_PART = 1024


def prepare_kernel(index_ref, sinks_ref, keys, values, joined_ref, picked_ref, bias_ref):
    tokens, key_width = keys.shape
    count = sinks_ref.shape[0]
    first_pos = index_ref[0] * tokens
    slot = lax.broadcasted_iota(jnp.int32, (count, tokens), 0)
    lane = lax.broadcasted_iota(jnp.int32, (count, tokens), 1)
    place = jnp.zeros((count, tokens), jnp.int32)
    seen = jnp.zeros((count, tokens), jnp.int32)
    for i in range(count):
        repeated = jnp.int32(0)
        for k in range(i):
            repeated = jnp.where(sinks_ref[i] == sinks_ref[k], jnp.int32(1), repeated)
        place = jnp.where(slot == i, sinks_ref[i], place)
        seen = jnp.where(slot == i, repeated, seen)
    pick = jnp.where(place == first_pos + lane, 1.0, 0.0).astype(jnp.bfloat16)
    for at, rows in ((slice(0, key_width), keys), (slice(key_width, None), values)):
        joined_ref[:, at] = rows[:, :]
        picked_ref[:, at] = jnp.dot(
            pick, rows[:, :], preferred_element_type=jnp.float32
        ).astype(jnp.bfloat16)
    near = bias_ref.shape[0] - count
    key_pos = first_pos - WINDOW + lax.broadcasted_iota(jnp.int32, (near, tokens), 0)
    query_pos = first_pos + lax.broadcasted_iota(jnp.int32, (near, tokens), 1)
    allowed = (key_pos >= 0) & (key_pos <= query_pos) & (key_pos > query_pos - WINDOW)
    bias_ref[:near, :] = jnp.where(allowed, 0.0, NEVER)
    allowed = (seen == 0) & (place <= first_pos + lane - WINDOW)
    bias_ref[near:, :] = jnp.where(allowed, 0.0, NEVER)


def prepared(index, sink_positions, key_rows, value_rows):
    tokens, key_width = key_rows.shape
    count = sink_positions.shape[0]
    smem, vmem = (pl.BlockSpec(memory_space=space) for space in (pltpu.SMEM, pltpu.VMEM))
    return pl.pallas_call(
        prepare_kernel,
        out_shape=(
            jax.ShapeDtypeStruct((tokens, 2 * key_width), jnp.bfloat16),
            jax.ShapeDtypeStruct((count, 2 * key_width), jnp.bfloat16),
            jax.ShapeDtypeStruct((WINDOW + tokens + count, tokens), jnp.float32),
        ),
        in_specs=[smem, smem, vmem, vmem],
        out_specs=(vmem, vmem, vmem),
    )(index, sink_positions, key_rows, value_rows)


def after(block, *earlier):
    return lax.optimization_barrier((block, earlier))[0]


def summed(block, axis, halo, later):
    shards = lax.axis_size(axis)
    step = 1
    while step < shards:
        reach = min(4, shards // step)
        parts = [
            lax.ppermute(block, axis, [(i, i ^ (step * m)) for i in range(shards)])
            for m in range(1, reach)
        ]
        for part in parts:
            block = block + part
        if step == 1:
            block, halo, later = lax.optimization_barrier((block, halo, later))
        step *= reach
    return block, halo, later


def even_rows(rows, most):
    return max(r for r in range(16, most + 1, 16) if rows % r == 0)


def attention_kernel(
    experts,
    query_t,
    halo,
    local,
    sinks,
    bias,
    residual_t,
    gain,
    ids_t,
    route_t,
    out_proj_t,
    hidden_ref,
    rows_ref,
    proj_v,
    att_v,
    sems,
):
    parts, part, heads_width = proj_v.shape
    width = parts * part
    tokens = query_t.shape[1]

    def proj_copy(r):
        at = pl.ds(pl.multiple_of(r * part, 16), part)
        return pltpu.make_async_copy(out_proj_t.at[at], proj_v.at[r], sems.at[r])

    for r in range(parts):
        proj_copy(r).start()
    group = Q_HEADS // KV_HEADS
    near = halo.shape[0] + local.shape[0]
    wide_bias = jnp.concatenate([bias[:, :]] * group, 1)
    scale = HEAD_DIM ** (-0.5)
    for g in range(KV_HEADS):
        lanes = slice(g * HEAD_DIM, (g + 1) * HEAD_DIM)
        value_lanes = slice((KV_HEADS + g) * HEAD_DIM, (KV_HEADS + g + 1) * HEAD_DIM)
        first = g * group * HEAD_DIM
        query = jnp.concatenate(
            [
                query_t[first + h * HEAD_DIM : first + (h + 1) * HEAD_DIM, :]
                for h in range(group)
            ],
            1,
        )
        near_scores = (
            jnp.dot(
                jnp.concatenate([halo[:, lanes], local[:, lanes]], 0),
                query,
                preferred_element_type=jnp.float32,
            )
            * scale
            + wide_bias[:near]
        )
        sink_scores = (
            jnp.dot(sinks[:, lanes], query, preferred_element_type=jnp.float32) * scale
            + wide_bias[near:]
        )
        largest = jnp.maximum(
            jnp.max(near_scores, axis=0, keepdims=True),
            jnp.max(sink_scores, axis=0, keepdims=True),
        )
        near_terms = jnp.exp(near_scores - largest)
        sink_terms = jnp.exp(sink_scores - largest)
        total = jnp.sum(near_terms, axis=0, keepdims=True) + jnp.sum(
            sink_terms, axis=0, keepdims=True
        )
        down = (((0,), (0,)), ((), ()))
        gathered = lax.dot_general(
            jnp.concatenate([halo[:, value_lanes], local[:, value_lanes]], 0),
            near_terms.astype(jnp.bfloat16),
            down,
            preferred_element_type=jnp.float32,
        ) + lax.dot_general(
            sinks[:, value_lanes],
            sink_terms.astype(jnp.bfloat16),
            down,
            preferred_element_type=jnp.float32,
        )
        gathered = (gathered / total).astype(jnp.bfloat16)
        for h in range(group):
            att_v[first + h * HEAD_DIM : first + (h + 1) * HEAD_DIM, :] = gathered[
                :, h * tokens : (h + 1) * tokens
            ]

    def project(r, squares):
        proj_copy(r).wait()
        rows = pl.ds(pl.multiple_of(r * part, 16), part)
        state = (
            jnp.dot(proj_v[r], att_v[:, :], preferred_element_type=jnp.float32)
            + residual_t[rows, :].astype(jnp.float32)
        ).astype(jnp.bfloat16)
        hidden_ref[rows, :] = state
        state = state.astype(jnp.float32)
        return squares + jnp.sum(state * state, axis=0, keepdims=True)

    squares = lax.fori_loop(0, parts, project, jnp.zeros((1, tokens), jnp.float32))
    inverse = lax.rsqrt(squares / width + 1e-05)
    for r in range(parts):
        rows = slice(r * part, (r + 1) * part)
        rows_ref[rows, :] = (
            hidden_ref[rows, :].astype(jnp.float32) * inverse * gain[rows, :]
        ).astype(jnp.bfloat16)
    expert = lax.broadcasted_iota(jnp.int32, (experts, tokens), 0)
    weight = jnp.zeros((experts, tokens), jnp.float32)
    for k in range(TOPK):
        weight = weight + jnp.where(ids_t[k : k + 1, :] == expert, route_t[k : k + 1, :], 0.0)
    high = weight.astype(jnp.bfloat16).astype(jnp.float32)
    rows_ref[width:, :] = jnp.concatenate([high, weight - high], 0).astype(jnp.bfloat16)


def attended_rows(
    query_t, halo, local, sinks, bias, residual_t, gain, ids_t, route_t, out_proj_t, experts
):
    width, heads_width = out_proj_t.shape
    tokens = query_t.shape[1]
    part = even_rows(width, 480)
    parts = width // part
    vmem = pl.BlockSpec(memory_space=pltpu.VMEM)
    return pl.pallas_call(
        functools.partial(attention_kernel, experts),
        out_shape=(
            jax.ShapeDtypeStruct((width, tokens), jnp.bfloat16),
            jax.ShapeDtypeStruct((width + 2 * experts, tokens), jnp.bfloat16),
        ),
        in_specs=[vmem] * 9 + [pl.BlockSpec(memory_space=pl.ANY)],
        out_specs=(vmem, vmem),
        scratch_shapes=[
            pltpu.VMEM((parts, part, heads_width), jnp.bfloat16),
            pltpu.VMEM((heads_width, tokens), jnp.bfloat16),
            pltpu.SemaphoreType.DMA((parts,)),
        ],
        compiler_params=pltpu.CompilerParams(vmem_limit_bytes=VMEM_BYTES),
        cost_estimate=pl.CostEstimate(
            flops=2 * tokens * width * heads_width,
            bytes_accessed=2 * width * heads_width,
            transcendentals=tokens * Q_HEADS * bias.shape[0],
        ),
    )(query_t, halo, local, sinks, bias, residual_t, gain, ids_t, route_t, out_proj_t)


def expert_kernel(experts, me_ref, x_ref, y_ref, gu0, gu1, dn0, dn1, *refs):
    *out_refs, rows, units, gu_v, dn_v, gu_sems, dn_sems = refs
    hidden = units.shape[1]
    width = gu_v.shape[4]
    tokens = x_ref.shape[1]
    parts, part = gu_v.shape[2:4]

    def gate_up_copy(half, side, k):
        source = (gu0, gu1)[half].at[pl.ds(pl.multiple_of(side * hidden + k * part, 16), part)]
        return pltpu.make_async_copy(source, gu_v.at[half, side, k], gu_sems.at[half, side, k])

    def down_copy(half, k):
        at = pl.ds(pl.multiple_of(k * part, 16), part)
        source = (dn0, dn1)[half].at[at]
        return pltpu.make_async_copy(source, dn_v.at[half, at], dn_sems.at[half, k])

    for k in range(parts):
        gate_up_copy(0, 0, k).start()
        gate_up_copy(0, 1, k).start()
    rows[:, :tokens] = x_ref[:, :]
    rows[:, tokens:] = y_ref[:, :]

    def step(half, k):
        gate_up_copy(half, 0, k).wait()
        gate_up_copy(half, 1, k).wait()
        if half == 0:
            gate_up_copy(1, 0, k).start()
            gate_up_copy(1, 1, k).start()
            down_copy(0, k).start()
        else:
            down_copy(1, k).start()
        gate, up = (
            jnp.dot(gu_v[half, side, k], rows[:width, :], preferred_element_type=jnp.float32)
            for side in range(2)
        )
        units[half, pl.ds(pl.multiple_of(k * part, 16), part), :] = (
            gate / (1.0 + jnp.exp(-gate)) * up
        ).astype(jnp.bfloat16)

    for half in range(2):
        pl.loop(0, parts)(functools.partial(step, half))
    extra = rows[width:, :].astype(jnp.float32)
    place = lax.broadcasted_iota(jnp.int32, extra.shape, 0)
    mine = (place == me_ref[0]) | (place == experts + me_ref[0])
    weight = jnp.sum(jnp.where(mine, extra, 0.0), axis=0, keepdims=True)
    for half in range(2):
        for k in range(parts):
            down_copy(half, k).wait()
    for first in range(0, width, OUT_PART):
        at = slice(first, min(first + OUT_PART, width))
        total = (product(dn_v[0, :, at], units[0]) + product(dn_v[1, :, at], units[1])) * weight
        out_refs[0][at, :] = total[:, :tokens].astype(out_refs[0].dtype)
        out_refs[1][at, :] = total[:, tokens:].astype(out_refs[1].dtype)


def product(down, units):
    return lax.dot_general(
        down, units, (((0,), (0,)), ((), ())), preferred_element_type=jnp.float32
    )


def expert_rows(me, x, y, weights, experts, kinds):
    gu0, gu1, dn0, dn1 = weights
    tokens = x.shape[1]
    hidden, width = gu0.shape[0] // 2, gu0.shape[1]
    part = even_rows(hidden, HIDDEN_PART)
    parts = hidden // part
    vmem = pl.BlockSpec(memory_space=pltpu.VMEM)
    hbm = pl.BlockSpec(memory_space=pl.ANY)
    return pl.pallas_call(
        functools.partial(expert_kernel, experts),
        out_shape=[jax.ShapeDtypeStruct((width, tokens), kind) for kind in kinds],
        in_specs=[pl.BlockSpec(memory_space=pltpu.SMEM), vmem, vmem, hbm, hbm, hbm, hbm],
        out_specs=[vmem] * len(kinds),
        scratch_shapes=[
            pltpu.VMEM((x.shape[0], 2 * tokens), jnp.bfloat16),
            pltpu.VMEM((2, hidden, 2 * tokens), jnp.bfloat16),
            pltpu.VMEM((2, 2, parts, part, width), jnp.bfloat16),
            pltpu.VMEM((2,) + dn0.shape, jnp.bfloat16),
            pltpu.SemaphoreType.DMA((2, 2, parts)),
            pltpu.SemaphoreType.DMA((2, parts)),
        ],
        compiler_params=pltpu.CompilerParams(vmem_limit_bytes=VMEM_BYTES),
        cost_estimate=pl.CostEstimate(
            flops=2 * 2 * tokens * 2 * 3 * width * hidden,
            bytes_accessed=2 * 2 * (gu0.size + dn0.size),
            transcendentals=4 * tokens * hidden,
        ),
    )(me, x, y, gu0, gu1, dn0, dn1)


def line_pairs(moves):
    return [(PLANE * p + r, PLANE * q + r) for p, q in moves for r in range(PLANE)]


def column_pairs(planes):
    return [(PLANE * p + r, (PLANE * p + r) ^ 2) for p in range(planes) for r in range(PLANE)]


def sources(planes):
    return [
        sorted(
            (q for q in range(planes) if q != p),
            key=lambda q: (abs(q - p), -(planes - p if q > p else p)),
        )
        for p in range(planes)
    ]


def rounds(moves):
    lists = []
    for p, q in moves:
        for held in lists:
            if all(q != to for _, to in held):
                held.append((p, q))
                break
        else:
            lists.append([(p, q)])
    return lists


def next_blocks(held, distance, planes):
    up = [(p, p + 1) for p in range(distance - 1, planes - 1)]
    down = [(p, p - 1) for p in range(1, planes - distance + 1)]
    if len(held) == 1 and distance > 1:
        return [lax.ppermute(held[0], "seq", line_pairs(up + down))]
    below, above = held if len(held) == 2 else held * 2
    return [
        lax.ppermute(below, "seq", line_pairs(up)),
        lax.ppermute(above, "seq", line_pairs(down)),
    ]


def slot_block(arrivals, plane, origins):
    chosen = {}
    for p, q in enumerate(origins):
        blocks = arrivals[abs(q - p)]
        block = blocks[0] if len(blocks) == 1 or q < p else blocks[1]
        chosen.setdefault(id(block), (block, []))[1].append(p)
    (result, _), *others = chosen.values()
    for block, holders in others:
        here = functools.reduce(jnp.logical_or, [plane == p for p in holders])
        result = jnp.where(here, block, result)
    return result


def on_device(
    query_rows,
    key_rows,
    value_rows,
    sink_positions,
    residual,
    out_proj,
    norm_gain,
    expert_ids,
    route_weights,
    gate_up,
    down_proj,
):
    rows_dev = query_rows.shape[0]
    width = residual.shape[1]
    shards = lax.axis_size("seq")
    planes = shards // PLANE
    experts = shards // 2
    my_index = lax.axis_index("seq")
    plane = my_index // PLANE
    local_rows, sink_rows, bias = prepared(
        my_index.reshape(1), sink_positions, key_rows, value_rows
    )
    halo_rows = lax.ppermute(local_rows, "seq", [(i, i + 1) for i in range(shards - 1)])
    later = (query_rows, gate_up, down_proj)
    sink_rows, halo_rows, later = summed(sink_rows, "seq", halo_rows, later)
    query_rows, gate_up, down_proj = later

    to_core = [(i, i ^ 1) for i in range(shards)]
    gu_own = jnp.swapaxes(gate_up[0], 0, 1)
    dn_own = down_proj[0]
    gu_other = lax.ppermute(gu_own, "seq", to_core)
    dn_other = lax.ppermute(dn_own, "seq", to_core)
    weights = (gu_own, gu_other, dn_own, dn_other)

    hidden_state, own = attended_rows(
        query_rows.T,
        halo_rows,
        local_rows,
        sink_rows,
        bias,
        residual.T,
        norm_gain[:, None],
        expert_ids.T,
        route_weights.T,
        out_proj.T,
        experts,
    )

    me = (my_index // 2).reshape(1)
    across = column_pairs(planes)
    order = sources(planes)
    expert = functools.partial(expert_rows, me)
    half = jnp.bfloat16

    held = next_blocks([own], 1, planes)
    arrivals = {1: held}
    cross = lax.ppermute(own, "seq", across)
    block, ready = own, (cross, *held)
    sums, slow = [], []
    for j in range(1, planes):
        nearer = [after(x, *ready) for x in arrivals[j]]
        next_block = after(slot_block(arrivals, plane, [o[j - 1] for o in order]), *ready)
        next_cross = lax.ppermute(next_block, "seq", across)
        if j + 1 < planes:
            held = next_blocks(nearer, j + 1, planes)
        else:
            held = []
        flows = []
        if j == 1:
            mine, theirs = expert(block, cross, weights, experts, (jnp.float32, jnp.float32))
            column_sum = hidden_state.astype(jnp.float32) + mine
            cross_sum = theirs
            done = mine
        elif j == 2:
            near = expert(block, cross, weights, experts, (half, half))
            done = near[0]
        else:
            if j == 3:
                flows = [(0, near[0]), (1, near[1])]
            sums.append((j - 1, expert(block, cross, weights, experts, (jnp.float32, half))))
            done = sums[-1][1][1]
        backs = []
        for side, part in flows:
            part = after(part, *ready)
            for moves in rounds([(p, o[0]) for p, o in enumerate(order)]):
                backs.append((side, lax.ppermute(part, "seq", line_pairs(moves))))
        for side, back in backs:
            if side == 0:
                column_sum = column_sum + back.astype(jnp.float32)
            else:
                slow.append(back)
        block, cross = next_block, next_cross
        ready = (next_cross, done, *held, *[back for side, back in backs if side == 0])
        if held:
            held = [after(x, *ready) for x in held]
            if len(held) == 2 and 2 * (j + 1) >= planes:
                held = [jnp.where(plane >= j + 1, held[0], held[1])]
            arrivals[j + 1] = held
    last = planes - 1
    parts = expert(block, cross, weights, experts, (jnp.float32, half))
    sums.append((last, parts))
    pending = None
    for n, (j, (mine, theirs)) in enumerate(sums):
        theirs = after(theirs, *ready)
        returned = lax.ppermute(theirs, "seq", across)
        if n == 0:
            slow = [after(slow[0], parts[0])] + [
                after(back, returned, parts[0]) for back in slow[1:]
            ]
            for back in slow:
                cross_sum = cross_sum + back.astype(jnp.float32)
        if pending is not None:
            k, both = pending
            for moves in rounds([(p, o[k - 1]) for p, o in enumerate(order)]):
                back = lax.ppermute(both, "seq", line_pairs(moves))
                column_sum = column_sum + back.astype(jnp.float32)
        pending = (j, (mine + returned.astype(jnp.float32)).astype(half))
        ready = (returned, *slow)
    crossing = lax.ppermute(after(cross_sum.astype(half), *ready), "seq", across)
    k, both = pending
    for moves in rounds([(p, o[k - 1]) for p, o in enumerate(order)]):
        back = lax.ppermute(both, "seq", line_pairs(moves))
        column_sum = column_sum + back.astype(jnp.float32)
    return (column_sum + crossing.astype(jnp.float32)).astype(half).T


def solution(mesh):
    in_specs = (
        P(("groups", "seq"), None),
        P(("groups", "seq"), None),
        P(("groups", "seq"), None),
        P("groups"),
        P(("groups", "seq"), None),
        P(),
        P(),
        P(("groups", "seq"), None),
        P(("groups", "seq"), None),
        P("seq", None, None),
        P("seq", None, None),
    )
    out_specs = P(("groups", "seq"), None)
    return jax.shard_map(
        on_device, mesh=mesh, in_specs=in_specs, out_specs=out_specs, check_vma=False
    )
```

```python
import functools

import jax
import jax.numpy as jnp
from jax import lax
from jax.experimental import pallas as pl
from jax.experimental.pallas import tpu as pltpu
from jax.sharding import PartitionSpec as P

Q_HEADS = 32
KV_HEADS = 4
HEAD_DIM = 64
WINDOW = 128
TOPK = 4
PLANE = 4
NEVER = -1e30
VMEM_BYTES = 56 * 1024 * 1024
HIDDEN_PART = 240
OUT_PART = 1024


def prepare_kernel(index_ref, sinks_ref, keys, values, joined_ref, picked_ref, bias_ref):
    tokens, key_width = keys.shape
    count = sinks_ref.shape[0]
    first_pos = index_ref[0] * tokens
    slot = lax.broadcasted_iota(jnp.int32, (count, tokens), 0)
    lane = lax.broadcasted_iota(jnp.int32, (count, tokens), 1)
    place = jnp.zeros((count, tokens), jnp.int32)
    seen = jnp.zeros((count, tokens), jnp.int32)
    for i in range(count):
        repeated = jnp.int32(0)
        for k in range(i):
            repeated = jnp.where(sinks_ref[i] == sinks_ref[k], jnp.int32(1), repeated)
        place = jnp.where(slot == i, sinks_ref[i], place)
        seen = jnp.where(slot == i, repeated, seen)
    pick = jnp.where(place == first_pos + lane, 1.0, 0.0).astype(jnp.bfloat16)
    for at, rows in ((slice(0, key_width), keys), (slice(key_width, None), values)):
        joined_ref[:, at] = rows[:, :]
        picked_ref[:, at] = jnp.dot(
            pick, rows[:, :], preferred_element_type=jnp.float32
        ).astype(jnp.bfloat16)
    near = bias_ref.shape[0] - count
    key_pos = first_pos - WINDOW + lax.broadcasted_iota(jnp.int32, (near, tokens), 0)
    query_pos = first_pos + lax.broadcasted_iota(jnp.int32, (near, tokens), 1)
    allowed = (key_pos >= 0) & (key_pos <= query_pos) & (key_pos > query_pos - WINDOW)
    bias_ref[:near, :] = jnp.where(allowed, 0.0, NEVER)
    allowed = (seen == 0) & (place <= first_pos + lane - WINDOW)
    bias_ref[near:, :] = jnp.where(allowed, 0.0, NEVER)


def prepared(index, sink_positions, key_rows, value_rows):
    tokens, key_width = key_rows.shape
    count = sink_positions.shape[0]
    smem, vmem = (pl.BlockSpec(memory_space=space) for space in (pltpu.SMEM, pltpu.VMEM))
    return pl.pallas_call(
        prepare_kernel,
        out_shape=(
            jax.ShapeDtypeStruct((tokens, 2 * key_width), jnp.bfloat16),
            jax.ShapeDtypeStruct((count, 2 * key_width), jnp.bfloat16),
            jax.ShapeDtypeStruct((WINDOW + tokens + count, tokens), jnp.float32),
        ),
        in_specs=[smem, smem, vmem, vmem],
        out_specs=(vmem, vmem, vmem),
    )(index, sink_positions, key_rows, value_rows)


def after(block, *earlier):
    return lax.optimization_barrier((block, earlier))[0]


def summed(block, axis, halo, later):
    shards = lax.axis_size(axis)
    step = 1
    while step < shards:
        reach = min(4, shards // step)
        parts = [
            lax.ppermute(block, axis, [(i, i ^ (step * m)) for i in range(shards)])
            for m in range(1, reach)
        ]
        for part in parts:
            block = block + part
        if step == 1:
            block, halo, later = lax.optimization_barrier((block, halo, later))
        step *= reach
    return block, halo, later


def even_rows(rows, most):
    return max(r for r in range(16, most + 1, 16) if rows % r == 0)


def attention_kernel(
    experts,
    query_t,
    halo,
    local,
    sinks,
    bias,
    residual_t,
    gain,
    ids_t,
    route_t,
    out_proj_t,
    hidden_ref,
    rows_ref,
    proj_v,
    att_v,
    sems,
):
    parts, part, heads_width = proj_v.shape
    width = parts * part
    tokens = query_t.shape[1]

    def proj_copy(r):
        at = pl.ds(pl.multiple_of(r * part, 16), part)
        return pltpu.make_async_copy(out_proj_t.at[at], proj_v.at[r], sems.at[r])

    for r in range(parts):
        proj_copy(r).start()
    group = Q_HEADS // KV_HEADS
    near = halo.shape[0] + local.shape[0]
    wide_bias = jnp.concatenate([bias[:, :]] * group, 1)
    scale = HEAD_DIM ** (-0.5)
    for g in range(KV_HEADS):
        lanes = slice(g * HEAD_DIM, (g + 1) * HEAD_DIM)
        value_lanes = slice((KV_HEADS + g) * HEAD_DIM, (KV_HEADS + g + 1) * HEAD_DIM)
        first = g * group * HEAD_DIM
        query = jnp.concatenate(
            [
                query_t[first + h * HEAD_DIM : first + (h + 1) * HEAD_DIM, :]
                for h in range(group)
            ],
            1,
        )
        near_scores = (
            jnp.dot(
                jnp.concatenate([halo[:, lanes], local[:, lanes]], 0),
                query,
                preferred_element_type=jnp.float32,
            )
            * scale
            + wide_bias[:near]
        )
        sink_scores = (
            jnp.dot(sinks[:, lanes], query, preferred_element_type=jnp.float32) * scale
            + wide_bias[near:]
        )
        largest = jnp.maximum(
            jnp.max(near_scores, axis=0, keepdims=True),
            jnp.max(sink_scores, axis=0, keepdims=True),
        )
        near_terms = jnp.exp(near_scores - largest)
        sink_terms = jnp.exp(sink_scores - largest)
        total = jnp.sum(near_terms, axis=0, keepdims=True) + jnp.sum(
            sink_terms, axis=0, keepdims=True
        )
        down = (((0,), (0,)), ((), ()))
        gathered = lax.dot_general(
            jnp.concatenate([halo[:, value_lanes], local[:, value_lanes]], 0),
            near_terms.astype(jnp.bfloat16),
            down,
            preferred_element_type=jnp.float32,
        ) + lax.dot_general(
            sinks[:, value_lanes],
            sink_terms.astype(jnp.bfloat16),
            down,
            preferred_element_type=jnp.float32,
        )
        gathered = (gathered / total).astype(jnp.bfloat16)
        for h in range(group):
            att_v[first + h * HEAD_DIM : first + (h + 1) * HEAD_DIM, :] = gathered[
                :, h * tokens : (h + 1) * tokens
            ]

    def project(r, squares):
        proj_copy(r).wait()
        rows = pl.ds(pl.multiple_of(r * part, 16), part)
        state = (
            jnp.dot(proj_v[r], att_v[:, :], preferred_element_type=jnp.float32)
            + residual_t[rows, :].astype(jnp.float32)
        ).astype(jnp.bfloat16)
        hidden_ref[rows, :] = state
        state = state.astype(jnp.float32)
        return squares + jnp.sum(state * state, axis=0, keepdims=True)

    squares = lax.fori_loop(0, parts, project, jnp.zeros((1, tokens), jnp.float32))
    inverse = lax.rsqrt(squares / width + 1e-05)
    for r in range(parts):
        rows = slice(r * part, (r + 1) * part)
        rows_ref[rows, :] = (
            hidden_ref[rows, :].astype(jnp.float32) * inverse * gain[rows, :]
        ).astype(jnp.bfloat16)
    expert = lax.broadcasted_iota(jnp.int32, (experts, tokens), 0)
    weight = jnp.zeros((experts, tokens), jnp.float32)
    for k in range(TOPK):
        weight = weight + jnp.where(ids_t[k : k + 1, :] == expert, route_t[k : k + 1, :], 0.0)
    high = weight.astype(jnp.bfloat16).astype(jnp.float32)
    rows_ref[width:, :] = jnp.concatenate([high, weight - high], 0).astype(jnp.bfloat16)


def attended_rows(
    query_t, halo, local, sinks, bias, residual_t, gain, ids_t, route_t, out_proj_t, experts
):
    width, heads_width = out_proj_t.shape
    tokens = query_t.shape[1]
    part = even_rows(width, 480)
    parts = width // part
    vmem = pl.BlockSpec(memory_space=pltpu.VMEM)
    return pl.pallas_call(
        functools.partial(attention_kernel, experts),
        out_shape=(
            jax.ShapeDtypeStruct((width, tokens), jnp.bfloat16),
            jax.ShapeDtypeStruct((width + 2 * experts, tokens), jnp.bfloat16),
        ),
        in_specs=[vmem] * 9 + [pl.BlockSpec(memory_space=pl.ANY)],
        out_specs=(vmem, vmem),
        scratch_shapes=[
            pltpu.VMEM((parts, part, heads_width), jnp.bfloat16),
            pltpu.VMEM((heads_width, tokens), jnp.bfloat16),
            pltpu.SemaphoreType.DMA((parts,)),
        ],
        compiler_params=pltpu.CompilerParams(vmem_limit_bytes=VMEM_BYTES),
        cost_estimate=pl.CostEstimate(
            flops=2 * tokens * width * heads_width,
            bytes_accessed=2 * width * heads_width,
            transcendentals=tokens * Q_HEADS * bias.shape[0],
        ),
    )(query_t, halo, local, sinks, bias, residual_t, gain, ids_t, route_t, out_proj_t)


def expert_kernel(experts, me_ref, x_ref, y_ref, gu0, gu1, dn0, dn1, *refs):
    *out_refs, rows, units, gu_v, dn_v, gu_sems, dn_sems = refs
    hidden = units.shape[1]
    width = gu_v.shape[4]
    tokens = x_ref.shape[1]
    parts, part = gu_v.shape[2:4]

    def gate_up_copy(half, side, k):
        source = (gu0, gu1)[half].at[pl.ds(pl.multiple_of(side * hidden + k * part, 16), part)]
        return pltpu.make_async_copy(source, gu_v.at[half, side, k], gu_sems.at[half, side, k])

    def down_copy(half, k):
        at = pl.ds(pl.multiple_of(k * part, 16), part)
        source = (dn0, dn1)[half].at[at]
        return pltpu.make_async_copy(source, dn_v.at[half, at], dn_sems.at[half, k])

    for k in range(parts):
        gate_up_copy(0, 0, k).start()
        gate_up_copy(0, 1, k).start()
    rows[:, :tokens] = x_ref[:, :]
    rows[:, tokens:] = y_ref[:, :]

    def step(half, k):
        gate_up_copy(half, 0, k).wait()
        gate_up_copy(half, 1, k).wait()
        if half == 0:
            gate_up_copy(1, 0, k).start()
            gate_up_copy(1, 1, k).start()
            down_copy(0, k).start()
        else:
            down_copy(1, k).start()
        gate, up = (
            jnp.dot(gu_v[half, side, k], rows[:width, :], preferred_element_type=jnp.float32)
            for side in range(2)
        )
        units[half, pl.ds(pl.multiple_of(k * part, 16), part), :] = (
            gate / (1.0 + jnp.exp(-gate)) * up
        ).astype(jnp.bfloat16)

    for half in range(2):
        pl.loop(0, parts)(functools.partial(step, half))
    extra = rows[width:, :].astype(jnp.float32)
    place = lax.broadcasted_iota(jnp.int32, extra.shape, 0)
    mine = (place == me_ref[0]) | (place == experts + me_ref[0])
    weight = jnp.sum(jnp.where(mine, extra, 0.0), axis=0, keepdims=True)
    for half in range(2):
        for k in range(parts):
            down_copy(half, k).wait()
    for first in range(0, width, OUT_PART):
        at = slice(first, min(first + OUT_PART, width))
        total = (product(dn_v[0, :, at], units[0]) + product(dn_v[1, :, at], units[1])) * weight
        out_refs[0][at, :] = total[:, :tokens].astype(out_refs[0].dtype)
        out_refs[1][at, :] = total[:, tokens:].astype(out_refs[1].dtype)


def product(down, units):
    return lax.dot_general(
        down, units, (((0,), (0,)), ((), ())), preferred_element_type=jnp.float32
    )


def expert_rows(me, x, y, weights, experts, kinds):
    gu0, gu1, dn0, dn1 = weights
    tokens = x.shape[1]
    hidden, width = gu0.shape[0] // 2, gu0.shape[1]
    part = even_rows(hidden, HIDDEN_PART)
    parts = hidden // part
    vmem = pl.BlockSpec(memory_space=pltpu.VMEM)
    hbm = pl.BlockSpec(memory_space=pl.ANY)
    return pl.pallas_call(
        functools.partial(expert_kernel, experts),
        out_shape=[jax.ShapeDtypeStruct((width, tokens), kind) for kind in kinds],
        in_specs=[pl.BlockSpec(memory_space=pltpu.SMEM), vmem, vmem, hbm, hbm, hbm, hbm],
        out_specs=[vmem] * len(kinds),
        scratch_shapes=[
            pltpu.VMEM((x.shape[0], 2 * tokens), jnp.bfloat16),
            pltpu.VMEM((2, hidden, 2 * tokens), jnp.bfloat16),
            pltpu.VMEM((2, 2, parts, part, width), jnp.bfloat16),
            pltpu.VMEM((2,) + dn0.shape, jnp.bfloat16),
            pltpu.SemaphoreType.DMA((2, 2, parts)),
            pltpu.SemaphoreType.DMA((2, parts)),
        ],
        compiler_params=pltpu.CompilerParams(vmem_limit_bytes=VMEM_BYTES),
        cost_estimate=pl.CostEstimate(
            flops=2 * 2 * tokens * 2 * 3 * width * hidden,
            bytes_accessed=2 * 2 * (gu0.size + dn0.size),
            transcendentals=4 * tokens * hidden,
        ),
    )(me, x, y, gu0, gu1, dn0, dn1)


def line_pairs(moves):
    return [(PLANE * p + r, PLANE * q + r) for p, q in moves for r in range(PLANE)]


def column_pairs(planes):
    return [(PLANE * p + r, (PLANE * p + r) ^ 2) for p in range(planes) for r in range(PLANE)]


def sources(planes):
    return [
        sorted(
            (q for q in range(planes) if q != p),
            key=lambda q: (abs(q - p), -(planes - p if q > p else p)),
        )
        for p in range(planes)
    ]


def rounds(moves):
    lists = []
    for p, q in moves:
        for held in lists:
            if all(q != to for _, to in held):
                held.append((p, q))
                break
        else:
            lists.append([(p, q)])
    return lists


def next_blocks(held, distance, planes):
    up = [(p, p + 1) for p in range(distance - 1, planes - 1)]
    down = [(p, p - 1) for p in range(1, planes - distance + 1)]
    if len(held) == 1 and distance > 1:
        return [lax.ppermute(held[0], "seq", line_pairs(up + down))]
    below, above = held if len(held) == 2 else held * 2
    return [
        lax.ppermute(below, "seq", line_pairs(up)),
        lax.ppermute(above, "seq", line_pairs(down)),
    ]


def slot_block(arrivals, plane, origins):
    chosen = {}
    for p, q in enumerate(origins):
        blocks = arrivals[abs(q - p)]
        block = blocks[0] if len(blocks) == 1 or q < p else blocks[1]
        chosen.setdefault(id(block), (block, []))[1].append(p)
    (result, _), *others = chosen.values()
    for block, holders in others:
        here = functools.reduce(jnp.logical_or, [plane == p for p in holders])
        result = jnp.where(here, block, result)
    return result


def on_device(
    query_rows,
    key_rows,
    value_rows,
    sink_positions,
    residual,
    out_proj,
    norm_gain,
    expert_ids,
    route_weights,
    gate_up,
    down_proj,
):
    rows_dev = query_rows.shape[0]
    width = residual.shape[1]
    shards = lax.axis_size("seq")
    planes = shards // PLANE
    experts = shards // 2
    my_index = lax.axis_index("seq")
    plane = my_index // PLANE
    local_rows, sink_rows, bias = prepared(
        my_index.reshape(1), sink_positions, key_rows, value_rows
    )
    halo_rows = lax.ppermute(local_rows, "seq", [(i, i + 1) for i in range(shards - 1)])
    later = (query_rows, gate_up, down_proj)
    sink_rows, halo_rows, later = summed(sink_rows, "seq", halo_rows, later)
    query_rows, gate_up, down_proj = later

    to_core = [(i, i ^ 1) for i in range(shards)]
    gu_own = jnp.swapaxes(gate_up[0], 0, 1)
    dn_own = down_proj[0]
    gu_other = lax.ppermute(gu_own, "seq", to_core)
    dn_other = lax.ppermute(dn_own, "seq", to_core)
    weights = (gu_own, gu_other, dn_own, dn_other)

    hidden_state, own = attended_rows(
        query_rows.T,
        halo_rows,
        local_rows,
        sink_rows,
        bias,
        residual.T,
        norm_gain[:, None],
        expert_ids.T,
        route_weights.T,
        out_proj.T,
        experts,
    )

    me = (my_index // 2).reshape(1)
    across = column_pairs(planes)
    order = sources(planes)
    expert = functools.partial(expert_rows, me)
    half = jnp.bfloat16

    held = next_blocks([own], 1, planes)
    arrivals = {1: held}
    cross = lax.ppermute(own, "seq", across)
    block, ready = own, (cross, *held)
    sums, slow = [], []
    for j in range(1, planes):
        nearer = [after(x, *ready) for x in arrivals[j]]
        next_block = after(slot_block(arrivals, plane, [o[j - 1] for o in order]), *ready)
        next_cross = lax.ppermute(next_block, "seq", across)
        if j + 1 < planes:
            held = next_blocks(nearer, j + 1, planes)
        else:
            held = []
        flows = []
        if j == 1:
            mine, theirs = expert(block, cross, weights, experts, (jnp.float32, jnp.float32))
            column_sum = hidden_state.astype(jnp.float32) + mine
            cross_sum = theirs
            done = mine
        elif j == 2:
            near = expert(block, cross, weights, experts, (half, half))
            done = near[0]
        else:
            if j == 3:
                flows = [(0, near[0]), (1, near[1])]
            sums.append((j - 1, expert(block, cross, weights, experts, (jnp.float32, half))))
            done = sums[-1][1][1]
        backs = []
        for side, part in flows:
            part = after(part, *ready)
            for moves in rounds([(p, o[0]) for p, o in enumerate(order)]):
                backs.append((side, lax.ppermute(part, "seq", line_pairs(moves))))
        for side, back in backs:
            if side == 0:
                column_sum = column_sum + back.astype(jnp.float32)
            else:
                slow.append(back)
        block, cross = next_block, next_cross
        ready = (next_cross, done, *held, *[back for side, back in backs if side == 0])
        if held:
            held = [after(x, *ready) for x in held]
            if len(held) == 2 and 2 * (j + 1) >= planes:
                held = [jnp.where(plane >= j + 1, held[0], held[1])]
            arrivals[j + 1] = held
    last = planes - 1
    parts = expert(block, cross, weights, experts, (jnp.float32, half))
    sums.append((last, parts))
    pending = None
    for n, (j, (mine, theirs)) in enumerate(sums):
        theirs = after(theirs, *ready)
        returned = lax.ppermute(theirs, "seq", across)
        if n == 0:
            slow = [after(slow[0], parts[0])] + [
                after(back, returned, parts[0]) for back in slow[1:]
            ]
            for back in slow:
                cross_sum = cross_sum + back.astype(jnp.float32)
        if pending is not None:
            k, both = pending
            for moves in rounds([(p, o[k - 1]) for p, o in enumerate(order)]):
                back = lax.ppermute(both, "seq", line_pairs(moves))
                column_sum = column_sum + back.astype(jnp.float32)
        pending = (j, (mine + returned.astype(jnp.float32)).astype(half))
        ready = (returned, *slow)
    crossing = lax.ppermute(after(cross_sum.astype(half), *ready), "seq", across)
    k, both = pending
    for moves in reversed(rounds([(p, o[k - 1]) for p, o in enumerate(order)])):
        back = lax.ppermute(both, "seq", line_pairs(moves))
        column_sum = column_sum + back.astype(jnp.float32)
    return (column_sum + crossing.astype(jnp.float32)).astype(half).T


def solution(mesh):
    in_specs = (
        P(("groups", "seq"), None),
        P(("groups", "seq"), None),
        P(("groups", "seq"), None),
        P("groups"),
        P(("groups", "seq"), None),
        P(),
        P(),
        P(("groups", "seq"), None),
        P(("groups", "seq"), None),
        P("seq", None, None),
        P("seq", None, None),
    )
    out_specs = P(("groups", "seq"), None)
    return jax.shard_map(
        on_device, mesh=mesh, in_specs=in_specs, out_specs=out_specs, check_vma=False
    )
```
